128 devices in a mesh: gx: 8 (over y, core), gy: 16 (over z, x).
Axes of the slice: x: 4, y: 4, z: 4, core: 2. Of those that a mesh axis runs over, the one named last changes fastest.
Arguments:
- features: bfloat16 [32, 256, 1536], P('gx', 'gy'), may hold values from -6 to 6
- block_mask: int32 [8, 64, 4], P('gx', 'gy'), may hold values 0 or 1
- weight_first: bfloat16 [27, 96, 128], replicated, may hold values from -0.125 to 0.125
- weight_second: bfloat16 [27, 128, 128], replicated, may hold values from -0.109375 to 0.109375
- weight_down: bfloat16 [8, 128, 128], replicated, may hold values from -0.1875 to 0.1875
- owners: int32 [8, 16, 16, 1], P('gx', 'gy'), may hold values from 0 to 15; in each aligned block of 16 rows (0 to 15, 16 to 31, ..., all dimensions but the last counted through in order) at most 2 rows name the same one
- moved_grad: bfloat16 [8, 16, 32, 1024], P('gx', 'gy'), may hold values from -0.5 to 0.5
Outputs:
- moved: bfloat16 [8, 16, 32, 1024], P('gx', 'gy')
- grad_first: float32 [27, 96, 128], replicated
- grad_second: float32 [27, 128, 128], replicated
- grad_down: float32 [8, 128, 128], replicated
The draws below stay inside these ranges and needn't reach their ends.
Inputs may be any that keep to these rules, and one draw needn't show every extreme that they name: `owners`: within one device's 16 rows no value appears more than 2 times; in some device's rows one value appears exactly 2 times.
All inputs are finite; a program needn't handle non-finite values. No bound on the sum of `block_mask` on one device may be relied on, other than what follows from the above.
Results may differ from the reference program's by a relative error of at most 0.012.
Values may be sent and summed in bfloat16 or wider, within the bound.
No kernel may reach another device: no remote copies, remote signals or barrier semaphores. Data moves between devices by JAX's collectives and lax.ppermute only.
A program may use at most 64 MiB of HBM per device.

```python
import math
import jax
import jax.numpy as jnp
import numpy as np
from jax import lax

CX = 4
CY = 16
CIN = 96
CH = 128
NX = 32
NY = 256
NZ = 16
BLK = 16
CAP = 2
N_GX = 8
N_GY = 16


def touch_ends(result, key, low, largest):
    longest = result.shape.index(max(result.shape))
    spots = []
    for shift in (0, 1):
        where = [jax.random.randint(jax.random.fold_in(key, axis), (), 0, length) for axis, length in enumerate(result.shape)]
        where[longest] = (where[longest] + shift) % result.shape[longest]
        spots.append(tuple(where))
    return result.at[spots[0]].set(low).at[spots[1]].set(largest)


def shard_levels(stream_key, dims, pieces, smallest, high):
    def one(position, shards_of):
        draws = jax.random.uniform(jax.random.fold_in(jax.random.fold_in(stream_key, 6), position), (shards_of,), jnp.float32, smallest / len(pieces), high / len(pieces))
        return jnp.repeat(jnp.exp(draws), dims[position] // shards_of).reshape((-1,) + (1,) * (len(dims) - position - 1))

    factor_of = one(*pieces[0])
    for cut in pieces[1:]:
        factor_of = factor_of * one(*cut)
    return factor_of


def deal_out(stream_key, own, number, rows, number_of, top, bound, slope):
    ranking = jax.random.permutation(stream_key, number_of)
    crowded, usual = load_shares(number_of, rows * top, bound, slope, True), load_shares(number_of, rows * top, bound, slope, False)
    places = jnp.arange(number_of)

    def named(lengths, rotation):
        used = int((lengths > 0).sum())
        fixed = max(1, used // 4)
        passed = fixed + (places - fixed + rotation * (used - fixed)) % max(1, number_of - fixed)
        return jnp.zeros((number_of,), jnp.int32).at[ranking[jnp.where(places < fixed, places, passed)]].set(jnp.asarray(lengths, jnp.int32))

    lengths = jnp.where(number % 4 == 0, named(crowded, number // 4), named(usual, number - number // 4 - 1))
    mixed = jax.random.permutation(jax.random.fold_in(own, 3), number_of)
    source_of, taker = mixed[0:number_of // 2 * 2:2], mixed[1:number_of // 2 * 2:2]
    slack = jnp.minimum(lengths[source_of] - 1, bound - lengths[taker]) // 2
    slack = jnp.where((source_of == ranking[0]) | (taker == ranking[0]) | (lengths[taker] == 0), 0, jnp.maximum(slack, 0))
    passed = jax.random.randint(jax.random.fold_in(own, 4), (number_of // 2,), 0, 1 << 20) % (slack + 1)
    lengths = lengths.at[source_of].add(-passed).at[taker].add(passed)
    members = jnp.searchsorted(jnp.cumsum(lengths), jnp.arange(rows * top), side="right").astype(jnp.int32)
    grid = members.reshape(top, rows).T
    grid = grid[jax.random.permutation(jax.random.fold_in(own, 1), rows)]
    rotation = jax.random.randint(jax.random.fold_in(own, 2), (rows, 1), 0, top)
    return jnp.take_along_axis(grid, (jnp.arange(top)[None, :] + rotation) % top, axis=1)


def load_shares(number_of, total, bound, skew, full):
    weights = [(1 << 20) // math.isqrt(grade ** skew) + 1 for grade in range(1, number_of + 1)]
    largest = bound if full else min(bound, max(-(-total // number_of), total * weights[0] // sum(weights)))
    least = 1 if total - largest >= number_of - 1 else 0
    counts, rest = [largest] + [least] * (number_of - 1), total - largest - least * (number_of - 1)
    while rest > 0:
        free = [i for i in range(1, number_of) if counts[i] < largest] or [i for i in range(1, number_of) if counts[i] < bound]
        pool, left = sum([weights[i] for i in free]), rest
        for i in free:
            addition = min(bound - counts[i], max(1, left * weights[i] // pool), rest)
            counts[i] = counts[i] + addition
            rest = rest - addition
    return np.array(counts)


def noise(stream_key, shape, spread, limit, pieces=(), held_as=jnp.bfloat16):
    values = spread * jax.random.normal(stream_key, shape, jnp.float32)
    if pieces:
        values = values * shard_levels(stream_key, shape, pieces, -0.22, 0.18)
    return jnp.clip(values, -limit, limit).astype(held_as)


def setup_inputs(seed: int = 0) -> dict:
    seeds = jax.random.split(jax.random.key(seed), 8)
    features = noise(seeds[0], (NX, NY, NZ * CIN), 1.0, 6.0, ((0, 8), (1, 16)))
    block_mask = touch_ends((jax.random.randint(seeds[1], (NX // 4, NY // 4, NZ // 4), 0, 5) < 3).astype(jnp.int32), jax.random.fold_in(seeds[1], 1), 0, 1)
    weight_first = noise(seeds[2], (27, CIN, CH), (27 * CIN) ** -0.5, 0.125)
    weight_second = noise(seeds[3], (27, CH, CH), (27 * CH) ** -0.5, 0.109375)
    weight_down = noise(seeds[4], (8, CH, CH), (8 * CH) ** -0.5, 0.1875)
    owners_keys = jax.random.split(jax.random.fold_in(seeds[5], 1), N_GX * N_GY * BLK // BLK)
    owners_turns = jax.random.permutation(jax.random.fold_in(seeds[5], 3), N_GX * N_GY * BLK // BLK)
    owners = jax.vmap(lambda own, number: deal_out(jax.random.fold_in(seeds[5], 2), own, number, BLK, N_GY, 1, CAP, 2))(owners_keys, owners_turns).reshape((N_GX, N_GY, BLK, 1))
    moved_grad = noise(seeds[6], (N_GX, N_GY, N_GY * CAP, 8 * CH), (64.0 / (N_GX * N_GY * BLK)), 0.5, ((0, 8), (1, 16)))
    return {"features": features, "block_mask": block_mask, "weight_first": weight_first, "weight_second": weight_second, "weight_down": weight_down, "owners": owners, "moved_grad": moved_grad}


def silu_grad(v):
    s = jax.nn.sigmoid(v)
    return s * (1.0 + v * (1.0 - s))

def conv(v, w):
    sx, sy, sz = (v.shape[0], v.shape[1], v.shape[2])
    padded = jnp.pad(v, ((1, 1), (1, 1), (1, 1), (0, 0)))
    total = jnp.zeros((sx, sy, sz, w.shape[2]), jnp.float32)
    for t in range(27):
        i, j, k = (t // 9, t // 3 % 3, t % 3)
        total = total + jnp.einsum('xyzc,cd->xyzd', padded[i:i + sx, j:j + sy, k:k + sz], w[t].astype(jnp.float32))
    return total

def conv_back(g, w):
    sx, sy, sz = (g.shape[0], g.shape[1], g.shape[2])
    padded = jnp.pad(g, ((1, 1), (1, 1), (1, 1), (0, 0)))
    total = jnp.zeros((sx, sy, sz, w.shape[1]), jnp.float32)
    for t in range(27):
        i, j, k = (t // 9, t // 3 % 3, t % 3)
        total = total + jnp.einsum('xyzd,cd->xyzc', padded[2 - i:2 - i + sx, 2 - j:2 - j + sy, 2 - k:2 - k + sz], w[t].astype(jnp.float32))
    return total

def weight_grad(v, g):
    sx, sy, sz = (v.shape[0], v.shape[1], v.shape[2])
    padded = jnp.pad(v, ((1, 1), (1, 1), (1, 1), (0, 0)))
    terms = []
    for t in range(27):
        i, j, k = (t // 9, t // 3 % 3, t % 3)
        terms.append(jnp.einsum('xyzc,xyzd->cd', padded[i:i + sx, j:j + sy, k:k + sz], g))
    return jnp.stack(terms)

def reference(features, block_mask, weight_first, weight_second, weight_down, owners, moved_grad):
    blocks = block_mask.astype(jnp.float32)
    active = jnp.broadcast_to(blocks[:, None, :, None, :, None], (NX // 4, 4, NY // 4, 4, NZ // 4, 4)).reshape(NX, NY, NZ)[..., None]
    inputs = (features.astype(jnp.float32).reshape(NX, NY, NZ, CIN) * active).astype(jnp.bfloat16)
    inputs_f = inputs.astype(jnp.float32)
    pre_first = active * conv(inputs_f, weight_first)
    first = jax.nn.silu(pre_first).astype(jnp.bfloat16)
    first_f = first.astype(jnp.float32)
    pre_second = active * conv(first_f, weight_second) + first_f
    second = jax.nn.silu(pre_second).astype(jnp.bfloat16)
    second_r = second.astype(jnp.float32).reshape(NX // 2, 2, NY // 2, 2, NZ // 2, 2, CH)
    down_w = weight_down.astype(jnp.float32).reshape(2, 2, 2, CH, CH)
    coarse = jnp.einsum('xaybzcd,abcde->xyze', second_r, down_w).astype(jnp.bfloat16)
    bricks = coarse.astype(jnp.float32).reshape(N_GX, CX // 4, 2, N_GY, CY // 4, 2, NZ // 4, 2, CH)
    bricks = bricks.transpose(0, 3, 1, 4, 6, 2, 5, 7, 8).reshape(N_GX, N_GY, BLK, 8 * CH)
    dest = owners[..., 0]
    onehot = (dest[..., None] == jnp.arange(N_GY, dtype=jnp.int32)[None, None, None, :]).astype(jnp.int32)
    rank = lax.optimization_barrier(jnp.sum((jnp.cumsum(onehot, axis=2) - onehot) * onehot, axis=3))
    slot = dest * CAP + rank
    select = (slot[..., None] == jnp.arange(N_GY * CAP, dtype=jnp.int32)).astype(jnp.float32)
    select = select.reshape(N_GX, N_GY, BLK, N_GY, CAP)
    moved = jnp.einsum('gsrjk,gsrv->gjskv', select, bricks).reshape(N_GX, N_GY, N_GY * CAP, 8 * CH).astype(jnp.bfloat16)
    back = moved_grad.astype(jnp.float32).reshape(N_GX, N_GY, N_GY, CAP, 8 * CH)
    grad_bricks = jnp.einsum('gsrjk,gjskv->gsrv', select, back)
    grad_coarse = grad_bricks.reshape(N_GX, N_GY, CX // 4, CY // 4, NZ // 4, 2, 2, 2, CH)
    grad_coarse = grad_coarse.transpose(0, 2, 5, 1, 3, 6, 4, 7, 8).reshape(NX // 2, NY // 2, NZ // 2, CH)
    grad_down = jnp.einsum('xaybzcd,xyze->abcde', second_r, grad_coarse).reshape(8, CH, CH)
    grad_act = jnp.einsum('xyze,abcde->xaybzcd', grad_coarse, down_w).reshape(NX, NY, NZ, CH)
    grad_pre_second = (active * grad_act * silu_grad(pre_second)).astype(jnp.bfloat16).astype(jnp.float32)
    grad_second = weight_grad(first_f, grad_pre_second)
    grad_first_act = grad_pre_second + conv_back(grad_pre_second, weight_second)
    grad_pre_first = (active * grad_first_act * silu_grad(pre_first)).astype(jnp.bfloat16).astype(jnp.float32)
    grad_first = weight_grad(inputs_f, grad_pre_first)
    return (moved, grad_first, grad_second, grad_down)
```

```python
import jax
import jax.numpy as jnp
from jax import lax
from jax.sharding import Mesh, PartitionSpec as P

GX, GY, CHIPS = ("y", "c"), ("z", "x"), ("y", "z", "x")


def padded_2(block, sides, width):
    for axis, dim in sides:
        count = lax.axis_size(axis)
        forward = [(i, i + 1) for i in range(count - 1)]
        backward = [(target, source) for source, target in forward]
        low = lax.ppermute(
            lax.slice_in_dim(block, block.shape[dim] - width, None, axis=dim), axis, forward
        )
        high = lax.ppermute(lax.slice_in_dim(block, 0, width, axis=dim), axis, backward)
        block = jnp.concatenate([low, block, high], axis=dim)
    return block


def silu_grad(v):
    s = jax.nn.sigmoid(v)
    return s * (1.0 + v * (1.0 - s))


def extend(v):
    padded = padded_2(v, ((GX, 0), (GY, 1)), 1)
    return jnp.pad(padded, ((0, 0), (0, 0), (1, 1), (0, 0)))


def taps_forward(padded, w, sx, sy, sz):
    total = jnp.zeros((sx * sy * sz, w.shape[2]), jnp.float32)
    for t in range(27):
        i, j, k = (t // 9, t // 3 % 3, t % 3)
        window = padded[i : i + sx, j : j + sy, k : k + sz].reshape(sx * sy * sz, w.shape[1])
        total = total + jnp.dot(window, w[t], preferred_element_type=jnp.float32)
    return total.reshape(sx, sy, sz, w.shape[2])


def taps_backward(padded, w, sx, sy, sz):
    total = jnp.zeros((sx * sy * sz, w.shape[1]), jnp.float32)
    for t in range(27):
        i, j, k = (t // 9, t // 3 % 3, t % 3)
        window = padded[2 - i : 2 - i + sx, 2 - j : 2 - j + sy, 2 - k : 2 - k + sz].reshape(
            sx * sy * sz, w.shape[2]
        )
        total = total + lax.dot_general(
            window, w[t], (((1,), (1,)), ((), ())), preferred_element_type=jnp.float32
        )
    return total.reshape(sx, sy, sz, w.shape[1])


def taps_weight(padded, grads, sx, sy, sz):
    flat = grads.reshape(sx * sy * sz, grads.shape[3])
    terms = []
    for t in range(27):
        i, j, k = (t // 9, t // 3 % 3, t % 3)
        window = padded[i : i + sx, j : j + sy, k : k + sz].reshape(sx * sy * sz, padded.shape[3])
        terms.append(
            lax.dot_general(
                window, flat, (((0,), (0,)), ((), ())), preferred_element_type=jnp.float32
            )
        )
    return jnp.stack(terms)


def swap_cores(v):
    return lax.ppermute(v, "c", [(0, 1), (1, 0)])


def sum_over_devices(terms):
    chips = lax.axis_size(CHIPS)
    core = lax.axis_index("c")
    flat = jnp.concatenate([t.reshape(-1, 128).astype(jnp.bfloat16) for t in terms])
    rows = flat.shape[0]
    part = -(-rows // (2 * chips * 8)) * 8
    flat = jnp.pad(flat, ((0, 2 * chips * part - rows), (0, 0))).reshape(2, chips * part, 128)
    mine = lax.dynamic_index_in_dim(flat, core, 0, keepdims=False)
    theirs = swap_cores(lax.dynamic_index_in_dim(flat, 1 - core, 0, keepdims=False))
    half = (mine.astype(jnp.float32) + theirs.astype(jnp.float32)).astype(jnp.bfloat16)
    pieces = lax.all_to_all(half.reshape(chips, part, 128), CHIPS, 0, 0, tiled=True)
    own = jnp.sum(pieces.astype(jnp.float32), axis=0).astype(jnp.bfloat16)
    half = lax.all_to_all(
        jnp.broadcast_to(own[None], (chips, part, 128)), CHIPS, 0, 0, tiled=True
    ).reshape(chips * part, 128)
    other = swap_cores(half)
    total = jnp.where(core == 0, jnp.concatenate([half, other]), jnp.concatenate([other, half]))
    total = total.astype(jnp.float32)
    out, at = [], 0
    for t in terms:
        n = t.size // 128
        out.append(total[at : at + n].reshape(t.shape))
        at += n
    return out


def per_device(features, block_mask, weight_first, weight_second, weight_down, owners, moved_grad):
    chan_in = weight_first.shape[1]
    chan = weight_first.shape[2]
    sx, sy = (features.shape[0], features.shape[1])
    sz = features.shape[2] // chan_in
    peers = lax.axis_size(GY)
    slots = moved_grad.shape[2]
    bricks_dev = sx // 4 * (sy // 4) * (sz // 4)
    blocks = block_mask.astype(jnp.float32)
    active = jnp.broadcast_to(
        blocks[:, None, :, None, :, None], (sx // 4, 4, sy // 4, 4, sz // 4, 4)
    ).reshape(sx, sy, sz)[..., None]
    inputs = (features.reshape(sx, sy, sz, chan_in) * active).astype(jnp.bfloat16)
    padded_in = extend(inputs)
    pre_first = active * taps_forward(padded_in, weight_first, sx, sy, sz)
    first = jax.nn.silu(pre_first).astype(jnp.bfloat16)
    padded_first = extend(first)
    pre_second = active * taps_forward(padded_first, weight_second, sx, sy, sz) + first.astype(
        jnp.float32
    )
    second = jax.nn.silu(pre_second).astype(jnp.bfloat16)
    second_r = second.reshape(sx // 2, 2, sy // 2, 2, sz // 2, 2, chan)
    down_w = weight_down.reshape(2, 2, 2, chan, chan)
    coarse = jnp.einsum(
        "xaybzcd,abcde->xyze", second_r, down_w, preferred_element_type=jnp.float32
    ).astype(jnp.bfloat16)
    bricks = (
        coarse.reshape(sx // 4, 2, sy // 4, 2, sz // 4, 2, chan)
        .transpose(0, 2, 4, 1, 3, 5, 6)
        .reshape(bricks_dev, 8 * chan)
    )
    dest = owners.reshape(bricks_dev)
    onehot = (dest[:, None] == jnp.arange(peers, dtype=jnp.int32)[None, :]).astype(jnp.int32)
    rank = jnp.sum((jnp.cumsum(onehot, axis=0) - onehot) * onehot, axis=1)
    slot_of = dest * (slots // peers) + rank
    select = slot_of[:, None] == jnp.arange(slots, dtype=jnp.int32)[None, :]
    select_b = select.astype(jnp.bfloat16)
    outgoing = lax.dot_general(
        select_b, bricks, (((0,), (0,)), ((), ())), preferred_element_type=jnp.float32
    ).astype(jnp.bfloat16)
    arrived = lax.all_to_all(outgoing, GY, split_axis=0, concat_axis=0, tiled=True)
    moved = arrived.reshape(1, 1, slots, 8 * chan)
    returned = lax.all_to_all(
        moved_grad.reshape(slots, 8 * chan), GY, split_axis=0, concat_axis=0, tiled=True
    )
    grad_bricks = jnp.dot(select.astype(jnp.bfloat16), returned, preferred_element_type=jnp.float32)
    grad_coarse = grad_bricks.astype(jnp.bfloat16).reshape(sx // 4, sy // 4, sz // 4, 2, 2, 2, chan)
    grad_coarse = grad_coarse.transpose(0, 3, 1, 4, 2, 5, 6).reshape(
        sx // 2, sy // 2, sz // 2, chan
    )
    grad_down = jnp.einsum(
        "xaybzcd,xyze->abcde", second_r, grad_coarse, preferred_element_type=jnp.float32
    ).reshape(8, chan, chan)
    grad_act = jnp.einsum(
        "xyze,abcde->xaybzcd", grad_coarse, down_w, preferred_element_type=jnp.float32
    ).reshape(sx, sy, sz, chan)
    grad_pre_second = (active * grad_act * silu_grad(pre_second)).astype(jnp.bfloat16)
    grad_second = taps_weight(padded_first, grad_pre_second, sx, sy, sz)
    padded_grad = extend(grad_pre_second)
    grad_first_act = grad_pre_second.astype(jnp.float32) + taps_backward(
        padded_grad, weight_second, sx, sy, sz
    )
    grad_pre_first = (active * grad_first_act * silu_grad(pre_first)).astype(jnp.bfloat16)
    grad_first = taps_weight(padded_in, grad_pre_first, sx, sy, sz)
    grad_first, grad_second, grad_down = sum_over_devices((grad_first, grad_second, grad_down))
    return (moved, grad_first, grad_second, grad_down)


def solution(mesh):
    shape = dict(mesh.shape)
    fine = Mesh(mesh.devices.reshape(shape["gx"] // 2, 2, 4, shape["gy"] // 4), ("y", "c", "z", "x"))
    in_specs = (P(GX, GY, None), P(GX, GY, None), P(), P(), P(), P(GX, GY, None, None), P(GX, GY, None, None))
    out_specs = (P(GX, GY, None, None), P(), P(), P())
    return jax.shard_map(
        per_device, mesh=fine, in_specs=in_specs, out_specs=out_specs, check_vma=False
    )
```

```python
import jax
import jax.numpy as jnp
import numpy as np
from jax import lax
from jax.experimental import pallas as pl
from jax.experimental.pallas import tpu as pltpu
from jax.sharding import Mesh, PartitionSpec as P

GX, GY, CHIPS = ("y", "c"), ("z", "x"), ("y", "z", "x")
F32, BF = jnp.float32, jnp.bfloat16
X, Y, Z, C, CIN = 4, 16, 16, 128, 96
HALF = 3584
NN = (((1,), (0,)), ((), ()))
NT = (((1,), (1,)), ((), ()))
TN = (((0,), (0,)), ((), ()))


def mm(a, b, dims=NN):
    return lax.dot_general(a, b, dims, preferred_element_type=F32)


def z_of(rows):
    return lax.broadcasted_iota(jnp.int32, (rows, C), 0) % Z


def from_above(v):
    return jnp.where(z_of(v.shape[0]) < Z - 1, pltpu.roll(v, v.shape[0] - 1, 0), 0.0)


def from_below(v):
    return jnp.where(z_of(v.shape[0]) > 0, pltpu.roll(v, 1, 0), 0.0)


def lanes(p, k):
    return p[:, k * C : (k + 1) * C]


def section(
    core_ref, in_ref, mask_ref, w1_ref, w2_ref, wd_ref, gc_ref, up_ref, sel_ref,
    grads_ref, out_ref,
    wa, wb, first, sg1, second, ge, g2, gs, vt,
):
    core = core_ref[0]

    def line(x, y0, cells):
        return jnp.concatenate(
            [mask_ref[(x + 4) // 4, (y + 4) // 4] for y in range(y0, y0 + cells)], axis=0
        )

    def taps(ref, width, x, cells, w, dims=NN, flip=False):
        wins = []
        for i in range(3):
            for j in range(3):
                ii, jj = (2 - i, 2 - j) if flip else (i, j)
                at = ((x + ii) * width + jj) * Z
                wins.append(ref[at : at + cells * Z, :])
        return mm(jnp.concatenate(wins, axis=1), w[...], dims)

    def weight_grad(ref, width, x0, y0, rows, put):
        for j in range(3):
            for x in range(6):
                at = ((x0 + x) * width + y0 + j) * Z
                vt[j * C : (j + 1) * C, x * Y * Z : (x + 1) * Y * Z] = ref[at : at + Y * Z, :].T
        for i in range(3):
            p = mm(vt[:, i * Y * Z : (i + X) * Y * Z], gs[...]).astype(BF)
            for j in range(3):
                for k in range(3):
                    put(9 * i + 3 * j + k, p[j * C : j * C + rows, k * C : (k + 1) * C])

    def put_z_taps(x, g):
        at = x * Y * Z
        gs[at : at + Y * Z, 0:C] = from_above(g).astype(BF)
        gs[at : at + Y * Z, C : 2 * C] = g.astype(BF)
        gs[at : at + Y * Z, 2 * C : 3 * C] = from_below(g).astype(BF)

    for m in range(9):
        for k in range(3):
            wa[m * C : m * C + CIN, k * C : (k + 1) * C] = w1_ref[3 * m + k]
        wa[m * C + CIN : (m + 1) * C, :] = jnp.zeros((C - CIN, 3 * C), BF)

    for x in range(8):
        p = taps(in_ref, 22, x, 20, wa)
        act = line(x - 2, -2, 20)
        pre = act * (lanes(p, 1) + from_below(lanes(p, 0)) + from_above(lanes(p, 2)))
        s = jax.nn.sigmoid(pre)
        first[x * 20 * Z : (x + 1) * 20 * Z, :] = (pre * s).astype(BF)
        if 2 <= x < 6:
            d = act * (s * (1.0 + pre * (1.0 - s)))
            sg1[(x - 2) * Y * Z : (x - 1) * Y * Z, :] = d[2 * Z : 18 * Z]

    for m in range(9):
        for k in range(3):
            wa[m * C : (m + 1) * C, k * C : (k + 1) * C] = w2_ref[3 * m + k]
            wb[k * C : (k + 1) * C, m * C : (m + 1) * C] = w2_ref[3 * m + k]

    even = z_of(6 * Z) % 2 == 0
    for u in range(4):
        both = jnp.concatenate(
            [jnp.concatenate([gc_ref[u, 2 * b + c] for b in range(2)], axis=1) for c in range(2)],
            axis=0,
        )
        r = mm(up_ref[...], both)
        for v in range(10):
            by, b = (v + 1) // 2, (v + 1) % 2
            t = r[by * Z : (by + 1) * Z, b * C : (b + 1) * C]
            at = (u * 10 + v) * Z
            ge[at : at + Z, 0:C] = jnp.where(even[:Z], t, 0.0).astype(BF)
            ge[at : at + Z, C : 2 * C] = jnp.where(even[:Z], 0.0, t).astype(BF)

    for x in range(6):
        p = taps(first, 20, x, 18, wa)
        at = ((x + 1) * 20 + 1) * Z
        act = line(x - 1, -1, 18)
        pre = act * (lanes(p, 1) + from_below(lanes(p, 0)) + from_above(lanes(p, 2)))
        pre = pre + first[at : at + 18 * Z, :].astype(F32)
        s = jax.nn.sigmoid(pre)
        if 1 <= x < 5:
            second[(x - 1) * Y * Z : x * Y * Z, :] = (pre * s)[Z : 17 * Z].astype(BF)
        u, a = (x + 1) // 2, (x + 1) % 2
        back = []
        for b in range(2):
            at = (u * 10 + 1 - b) * Z
            w = jnp.concatenate([wd_ref[4 * a + 2 * b], wd_ref[4 * a + 2 * b + 1]], axis=1)
            back.append(mm(ge[at : at + 9 * Z, :], w, NT))
        g = jnp.concatenate(
            [back[1 - y % 2][y // 2 * Z : (y // 2 + 1) * Z] for y in range(18)], axis=0
        )
        g = (act * g * (s * (1.0 + pre * (1.0 - s)))).astype(BF)
        g2[x * 18 * Z : (x + 1) * 18 * Z, :] = g
        if 1 <= x < 5:
            put_z_taps(x - 1, g[Z : 17 * Z].astype(F32))

    def corner(a, b):
        return jnp.concatenate(
            [
                second[((2 * u + a) * Y + 2 * v + b) * Z : ((2 * u + a) * Y + 2 * v + b + 1) * Z, :]
                for u in range(2)
                for v in range(8)
            ],
            axis=0,
        )

    corners = [corner(a, b) for a in range(2) for b in range(2)]
    wd = jnp.concatenate(
        [jnp.concatenate([wd_ref[2 * q], wd_ref[2 * q + 1]], axis=1) for q in range(4)], axis=0
    )
    p = mm(jnp.concatenate(corners, axis=1), wd)
    coarse = (lanes(p, 0) + from_above(lanes(p, 1))).astype(BF)
    bricks = jnp.concatenate(
        [
            jnp.concatenate(
                [
                    coarse[(a * 8 + 2 * by + b) * Z : (a * 8 + 2 * by + b + 1) * Z]
                    for by in range(4)
                ],
                axis=0,
            )
            for a in range(2)
            for b in range(2)
        ],
        axis=1,
    )
    r = mm(sel_ref[...], bricks).astype(BF)
    for q in range(4):
        for c in range(2):
            out_ref[:, (2 * q + c) * C : (2 * q + c + 1) * C] = r[
                c * 32 : (c + 1) * 32, q * C : (q + 1) * C
            ]

    gec = jnp.concatenate([ge[(u * 10 + 1) * Z : (u * 10 + 9) * Z, :] for u in (1, 2)], axis=0)

    def put_a(at, v):
        grads_ref[core, at : at + v.shape[0], :] = v

    def put_b(at, v):
        grads_ref[1 - core, at : at + v.shape[0], :] = v

    for q in range(4):
        r = mm(corners[q], gec, TN).astype(BF)
        for c in range(2):
            t = 2 * q + c
            if t == 0:
                put_a(27 * C, lanes(r, c))
            else:
                put_b(27 * CIN + (t - 1) * C, lanes(r, c))
    put_b(27 * CIN + 7 * C, jnp.zeros((HALF - 27 * CIN - 7 * C, C), BF))
    weight_grad(first, 20, 1, 1, C, lambda t, v: put_a(t * C, v))

    for x in range(X):
        p = taps(g2, 18, x, Y, wb, NT, flip=True)
        at = ((x + 1) * 18 + 1) * Z
        g = lanes(p, 1) + from_above(lanes(p, 0)) + from_below(lanes(p, 2))
        g = g + g2[at : at + Y * Z, :].astype(F32)
        g = (g * sg1[x * Y * Z : (x + 1) * Y * Z, :]).astype(BF)
        put_z_taps(x, g.astype(F32))
    weight_grad(in_ref, 22, 2, 2, CIN, lambda t, v: put_b(t * CIN, v))


def run_section(core, cells, mask, w1, w2, wd, gc, up, sel):
    vm = pl.BlockSpec(memory_space=pltpu.VMEM)
    return pl.pallas_call(
        section,
        out_shape=(
            jax.ShapeDtypeStruct((2, HALF, C), BF),
            jax.ShapeDtypeStruct((32, 8 * C), BF),
        ),
        in_specs=[pl.BlockSpec(memory_space=pltpu.SMEM)] + [vm] * 8,
        out_specs=(vm, vm),
        scratch_shapes=[
            pltpu.VMEM((9 * C, 3 * C), BF),
            pltpu.VMEM((3 * C, 9 * C), BF),
            pltpu.VMEM((8 * 20 * Z, C), BF),
            pltpu.VMEM((X * Y * Z, C), F32),
            pltpu.VMEM((X * Y * Z, C), BF),
            pltpu.VMEM((40 * Z, 2 * C), BF),
            pltpu.VMEM((6 * 18 * Z, C), BF),
            pltpu.VMEM((X * Y * Z, 3 * C), BF),
            pltpu.VMEM((3 * C, 6 * Y * Z), BF),
        ],
        compiler_params=pltpu.CompilerParams(vmem_limit_bytes=48 * 1024 * 1024),
        cost_estimate=pl.CostEstimate(
            flops=8_000_000_000, bytes_accessed=6_000_000, transcendentals=600_000
        ),
    )(core, cells, mask, w1, w2, wd, gc, up, sel)


def shift(v, axes, step):
    n = lax.axis_size(axes)
    return lax.ppermute(v, axes, [(i, i + step) for i in range(n) if 0 <= i + step < n])


def swap_cores(v):
    return lax.ppermute(v, "c", [(0, 1), (1, 0)])


def tile_of(*rows):
    return jnp.pad(
        jnp.stack([jnp.pad(r.reshape(-1).astype(BF), (0, C - r.size)) for r in rows]),
        ((0, 16 - len(rows)), (0, 0)),
    )


def up_matrix():
    m = np.zeros((6 * Z, 64), np.float32)
    for by in range(6):
        for z in range(Z):
            m[by * Z + z, z // 2 % 2 * 32 + by * 4 + z // 4] = 1
    return jnp.asarray(m, BF)


def per_device(features, block_mask, weight_first, weight_second, weight_down, owners, moved_grad):
    core = lax.axis_index("c")
    blocks = block_mask.reshape(4, 4)
    active = jnp.repeat(jnp.repeat(blocks, 4, axis=0), 4, axis=1).astype(F32)
    own = features.reshape(X, Y, Z, CIN) * active[None, :, :, None]
    own = jnp.pad(own.astype(BF), ((0, 0), (0, 0), (0, 0), (0, C - CIN)))

    dest = owners.reshape(16)
    earlier = jnp.asarray(np.tril(np.ones((16, 16), np.int32), -1))
    rank = jnp.sum((dest[:, None] == dest[None, :]).astype(jnp.int32) * earlier, axis=1)
    slot = dest * 2 + rank

    side = 3 * 4 * Z
    low = shift(
        jnp.concatenate([own[:, 13:].reshape(side, C), tile_of(slot, blocks[3])]), GY, 1
    )
    high = shift(
        jnp.concatenate([own[:, :3].reshape(side, C), tile_of(slot, blocks[0])]), GY, -1
    )
    rows = jnp.pad(moved_grad.reshape(16, 2, 8 * C), ((1, 1), (0, 0), (0, 0)))
    rows = jnp.concatenate([rows[0:16], rows[1:17], rows[2:18]], axis=1)
    rows = lax.all_to_all(rows, GY, 0, 0, tiled=True).reshape(96, 8 * C)

    mid = jnp.concatenate(
        [low[:side].reshape(X, 3, Z, C), own, high[:side].reshape(X, 3, Z, C)], axis=1
    )
    slots = jnp.concatenate(
        [low[side, 12:16].astype(jnp.int32), slot, high[side, :4].astype(jnp.int32)]
    )
    place = slots // 2 * 6 + slots % 2 + jnp.asarray([0] * 4 + [2] * 16 + [4] * 4, jnp.int32)
    pick = jnp.pad(place, (0, 8), constant_values=-1)[:, None] == jnp.arange(96)[None, :]
    bricks = mm(pick.astype(BF), rows).astype(BF)
    blocks = jnp.concatenate(
        [low[side + 1, :4], blocks.reshape(16).astype(BF), high[side + 1, :4]]
    )

    def strip(cells, a):
        cots = [bricks[:, (4 * a + q) * C : (4 * a + q + 1) * C] for q in range(4)]
        return jnp.concatenate([cells.reshape(-1, C)] + cots + [tile_of(blocks)])

    low = shift(strip(mid[1:], 1), GX, 1)
    high = shift(strip(mid[:3], 0), GX, -1)
    side = 3 * 22 * Z
    cells = jnp.concatenate([low[:side], mid.reshape(-1, C), high[:side]])
    own_gc = bricks.reshape(32, 8, C).transpose(1, 0, 2)
    gc = jnp.concatenate(
        [low[side : side + 128].reshape(4, 32, C), own_gc, high[side : side + 128].reshape(4, 32, C)]
    ).reshape(4, 4, 32, C)
    blocks = jnp.stack([low[side + 128, :24], blocks, high[side + 128, :24]])
    mask = jnp.repeat(blocks.reshape(3, 6, 4).astype(F32), 4, axis=2)
    mask = jnp.broadcast_to(mask[..., None], (3, 6, Z, C))

    where = jnp.arange(64)
    slot_z = jnp.repeat(slot, 4)
    sel = (slot_z[None, :] == where[:, None] % 32) & (where[None, :] % 4 == where[:, None] // 32 * 2)
    grads, outgoing = run_section(
        core.reshape(1).astype(jnp.int32), cells, mask, weight_first, weight_second, weight_down,
        gc, up_matrix(), sel.astype(BF),
    )

    moved = lax.all_to_all(outgoing.reshape(16, 2, 8 * C), GY, 0, 0, tiled=True)
    moved = moved.reshape(1, 1, 32, 8 * C)

    chips = lax.axis_size(CHIPS)
    part = HALF // chips
    theirs = swap_cores(grads[1])
    half = (grads[0].astype(F32) + theirs.astype(F32)).astype(BF)
    pieces = lax.all_to_all(half.reshape(chips, part, C), CHIPS, 0, 0, tiled=True)
    total = jnp.sum(pieces.astype(F32), axis=0).astype(BF)
    half = lax.all_to_all(
        jnp.broadcast_to(total[None], (chips, part, C)), CHIPS, 0, 0, tiled=True
    ).reshape(HALF, C)
    other = swap_cores(half)
    a = jnp.where(core == 0, half, other).astype(F32)
    b = jnp.where(core == 0, other, half).astype(F32)
    grad_second = a[: 27 * C].reshape(27, C, C)
    grad_first = b[: 27 * CIN].reshape(27, CIN, C)
    grad_down = jnp.concatenate([a[27 * C :], b[27 * CIN : 27 * CIN + 7 * C]]).reshape(8, C, C)
    return moved, grad_first, grad_second, grad_down


def solution(mesh):
    shape = dict(mesh.shape)
    fine = Mesh(
        mesh.devices.reshape(shape["gx"] // 2, 2, 4, shape["gy"] // 4), ("y", "c", "z", "x")
    )
    whole, tiles = P(GX, GY, None), P(GX, GY, None, None)
    return jax.shard_map(
        per_device,
        mesh=fine,
        in_specs=(whole, whole, P(), P(), P(), tiles, tiles),
        out_specs=(tiles, P(), P(), P()),
        check_vma=False,
    )
```

```python
import math
import jax
import jax.numpy as jnp
import numpy as np
from jax import lax
from jax.experimental import pallas as pl
from jax.experimental.pallas import tpu as pltpu
from jax.sharding import Mesh, PartitionSpec as P

GX, GY, ALL = ("y", "c"), ("z", "x"), ("y", "c", "z", "x")
F32, BF = jnp.float32, jnp.bfloat16
X, Y, Z, C, CIN = 4, 16, 16, 128, 96
HALF, PART = 3584, 224
COTS, MASK, STRIP = 1056, 1248, 1344
NN = (((1,), (0,)), ((), ()))
NT = (((1,), (1,)), ((), ()))
TN = (((0,), (0,)), ((), ()))


def mm(a, b, dims=NN):
    return lax.dot_general(a, b, dims, preferred_element_type=F32)


def iota(shape, axis):
    return lax.broadcasted_iota(jnp.int32, shape, axis)


def one(where):
    return jnp.where(where, 1.0, 0.0).astype(BF)


def z_of(rows):
    return iota((rows, C), 0) % Z


def from_above(v):
    return jnp.where(z_of(v.shape[0]) < Z - 1, pltpu.roll(v, v.shape[0] - 1, 0), 0.0)


def from_below(v):
    return jnp.where(z_of(v.shape[0]) > 0, pltpu.roll(v, 1, 0), 0.0)


def lanes(p, k):
    return p[:, k * C : (k + 1) * C]


def section(
    low_ref, mid_ref, high_ref, mask_ref, gc_ref, place_ref, w1_ref, w2_ref, wd_ref, up_ref,
    grads_ref, out_ref,
    wa, wb, first, sg1, second, ge, g2, gs, vt,
):
    core = lax.axis_index("c")

    def cells(x, y, n):
        ref, x = ((low_ref, x), (mid_ref, x - 3), (high_ref, x - 7))[(x > 2) + (x > 6)]
        return ref[(x * 22 + y) * Z : (x * 22 + y + n) * Z, :]

    def firsts(x, y, n):
        return first[(x * 20 + y) * Z : (x * 20 + y + n) * Z, :]

    def cots(x, y, n):
        return g2[(x * 18 + y) * Z : (x * 18 + y + n) * Z, :]

    def mask_tile(bx, by):
        ref, at = ((low_ref, MASK), (mask_ref, 0), (high_ref, MASK))[bx]
        return ref[at + by * Z : at + (by + 1) * Z, :].astype(F32)

    def cotangent(u, q):
        if u in (1, 2):
            return gc_ref[u - 1, q]
        return (low_ref if u == 0 else high_ref)[COTS + q * 48 : COTS + (q + 1) * 48, :]

    def line(x, y0, cells):
        return jnp.concatenate(
            [mask_tile((x + 4) // 4, (y + 4) // 4) for y in range(y0, y0 + cells)], axis=0
        )

    def taps(get, x, n, w, dims=NN, flip=False):
        wins = []
        for i in range(3):
            for j in range(3):
                ii, jj = (2 - i, 2 - j) if flip else (i, j)
                wins.append(get(x + ii, jj, n))
        return mm(jnp.concatenate(wins, axis=1), w[...], dims)

    def weight_grad(get, x0, y0, rows, put):
        for j in range(3):
            for x in range(6):
                vt[j * C : (j + 1) * C, x * Y * Z : (x + 1) * Y * Z] = get(x0 + x, y0 + j, Y).T
        for i in range(3):
            p = mm(vt[:, i * Y * Z : (i + X) * Y * Z], gs[...]).astype(BF)
            for j in range(3):
                for k in range(3):
                    put(9 * i + 3 * j + k, p[j * C : j * C + rows, k * C : (k + 1) * C])

    def put_z_taps(x, g):
        at = x * Y * Z
        gs[at : at + Y * Z, 0:C] = from_above(g).astype(BF)
        gs[at : at + Y * Z, C : 2 * C] = g.astype(BF)
        gs[at : at + Y * Z, 2 * C : 3 * C] = from_below(g).astype(BF)

    for m in range(9):
        for k in range(3):
            wa[m * C : m * C + CIN, k * C : (k + 1) * C] = w1_ref[3 * m + k]
        wa[m * C + CIN : (m + 1) * C, :] = jnp.zeros((C - CIN, 3 * C), BF)

    for x in range(8):
        p = taps(cells, x, 20, wa)
        act = line(x - 2, -2, 20)
        pre = act * (lanes(p, 1) + from_below(lanes(p, 0)) + from_above(lanes(p, 2)))
        s = jax.nn.sigmoid(pre)
        first[x * 20 * Z : (x + 1) * 20 * Z, :] = (pre * s).astype(BF)
        if 2 <= x < 6:
            d = act * (s * (1.0 + pre * (1.0 - s)))
            sg1[(x - 2) * Y * Z : (x - 1) * Y * Z, :] = d[2 * Z : 18 * Z]

    for m in range(9):
        for k in range(3):
            wa[m * C : (m + 1) * C, k * C : (k + 1) * C] = w2_ref[3 * m + k]
            wb[k * C : (k + 1) * C, m * C : (m + 1) * C] = w2_ref[3 * m + k]

    even = z_of(6 * Z) % 2 == 0
    for u in range(4):
        both = jnp.concatenate(
            [jnp.concatenate([cotangent(u, 2 * b + c) for b in range(2)], axis=1) for c in range(2)],
            axis=0,
        )
        r = mm(up_ref[...], both)
        for v in range(10):
            by, b = (v + 1) // 2, (v + 1) % 2
            t = r[by * Z : (by + 1) * Z, b * C : (b + 1) * C]
            at = (u * 10 + v) * Z
            ge[at : at + Z, 0:C] = jnp.where(even[:Z], t, 0.0).astype(BF)
            ge[at : at + Z, C : 2 * C] = jnp.where(even[:Z], 0.0, t).astype(BF)

    for x in range(6):
        p = taps(firsts, x, 18, wa)
        act = line(x - 1, -1, 18)
        pre = act * (lanes(p, 1) + from_below(lanes(p, 0)) + from_above(lanes(p, 2)))
        pre = pre + firsts(x + 1, 1, 18).astype(F32)
        s = jax.nn.sigmoid(pre)
        if 1 <= x < 5:
            second[(x - 1) * Y * Z : x * Y * Z, :] = (pre * s)[Z : 17 * Z].astype(BF)
        u, a = (x + 1) // 2, (x + 1) % 2
        back = []
        for b in range(2):
            at = (u * 10 + 1 - b) * Z
            w = jnp.concatenate([wd_ref[4 * a + 2 * b], wd_ref[4 * a + 2 * b + 1]], axis=1)
            back.append(mm(ge[at : at + 9 * Z, :], w, NT))
        g = jnp.concatenate(
            [back[1 - y % 2][y // 2 * Z : (y // 2 + 1) * Z] for y in range(18)], axis=0
        )
        g = (act * g * (s * (1.0 + pre * (1.0 - s)))).astype(BF)
        g2[x * 18 * Z : (x + 1) * 18 * Z, :] = g
        if 1 <= x < 5:
            put_z_taps(x - 1, g[Z : 17 * Z].astype(F32))

    def corner(a, b):
        return jnp.concatenate(
            [
                second[((2 * u + a) * Y + 2 * v + b) * Z : ((2 * u + a) * Y + 2 * v + b + 1) * Z, :]
                for u in range(2)
                for v in range(8)
            ],
            axis=0,
        )

    corners = [corner(a, b) for a in range(2) for b in range(2)]
    wd = jnp.concatenate(
        [jnp.concatenate([wd_ref[2 * q], wd_ref[2 * q + 1]], axis=1) for q in range(4)], axis=0
    )
    p = mm(jnp.concatenate(corners, axis=1), wd)
    coarse = (lanes(p, 0) + from_above(lanes(p, 1))).astype(BF)
    row, col = iota((128, 256), 0), iota((128, 256), 1)
    a, by, b, z = col // 128, col // 32 % 4, col // 16 % 2, col % Z
    order = (row // 16 == 4 * a + 2 * b + z // 2 % 2) & (row % 16 == by * 4 + z // 4) & (z % 2 == 0)
    bricks = mm(one(order), coarse).astype(BF)
    place = jnp.concatenate([place_ref[...].astype(F32)] * 8, axis=0)
    place = jnp.concatenate([place] * 2, axis=1)
    target = (8 * (col // 16) + col % 2).astype(F32)
    out_ref[...] = mm(one((place == target) & (row // 16 == col // 2 % 8)), bricks, TN).astype(BF)

    gec = jnp.concatenate([ge[(u * 10 + 1) * Z : (u * 10 + 9) * Z, :] for u in (1, 2)], axis=0)

    def put_a(at, v):
        grads_ref[core, at : at + v.shape[0], :] = v

    def put_b(at, v):
        grads_ref[1 - core, at : at + v.shape[0], :] = v

    for q in range(4):
        r = mm(corners[q], gec, TN).astype(BF)
        for c in range(2):
            t = 2 * q + c
            if t == 0:
                put_a(27 * C, lanes(r, c))
            else:
                put_b(27 * CIN + (t - 1) * C, lanes(r, c))
    put_b(27 * CIN + 7 * C, jnp.zeros((HALF - 27 * CIN - 7 * C, C), BF))
    weight_grad(firsts, 1, 1, C, lambda t, v: put_a(t * C, v))

    for x in range(X):
        p = taps(cots, x, Y, wb, NT, flip=True)
        g = lanes(p, 1) + from_above(lanes(p, 0)) + from_below(lanes(p, 2))
        g = g + cots(x + 1, 1, Y).astype(F32)
        g = (g * sg1[x * Y * Z : (x + 1) * Y * Z, :]).astype(BF)
        put_z_taps(x, g.astype(F32))
    weight_grad(cells, 2, 2, CIN, lambda t, v: put_b(t * CIN, v))


VM = pl.BlockSpec(memory_space=pltpu.VMEM)
SM = pl.BlockSpec(memory_space=pltpu.SMEM)


def call(kernel, outs, args, in_specs=None, scratch=(), flops=10_000_000):
    return pl.pallas_call(
        kernel,
        out_shape=tuple(jax.ShapeDtypeStruct(shape, dtype) for shape, dtype in outs),
        in_specs=in_specs or [VM] * len(args),
        out_specs=tuple([VM] * len(outs)),
        scratch_shapes=[pltpu.VMEM(shape, dtype) for shape, dtype in scratch],
        compiler_params=pltpu.CompilerParams(vmem_limit_bytes=40 * 1024 * 1024),
        cost_estimate=pl.CostEstimate(
            flops=flops, bytes_accessed=1_000_000, transcendentals=0
        ),
    )(*args)


def prepare(feat_ref, blocks_ref, owners_ref, own_ref, low_ref, high_ref, misc_ref, wide):
    lane = iota((Y, C), 1)
    for x in range(X):
        f = feat_ref[x].astype(F32)
        f = jnp.concatenate([f, jnp.zeros((Y, C), F32)], axis=1)
        for z in range(Z):
            t = jnp.where(lane < CIN, f[:, z * CIN : z * CIN + C], 0.0)
            wide[pl.ds(x * Y * Z + z, Y, stride=Z), :] = t
    part = iota((Z, C), 0) // 4
    for by in range(4):
        m = jnp.zeros((Z, C), jnp.int32)
        for bz in range(4):
            m = jnp.where(part == bz, blocks_ref[0, by, bz], m)
        m = m.astype(F32)
        misc_ref[by * Z : (by + 1) * Z, :] = m.astype(BF)
        for x in range(X):
            for y in range(4 * by, 4 * by + 4):
                at = (x * Y + y) * Z
                own_ref[at : at + Z, :] = (wide[at : at + Z, :] * m).astype(BF)
    dest = jnp.broadcast_to(owners_ref[0, 0].astype(F32), (16, C))
    row, lane = iota((16, C), 0), iota((16, C), 1)
    across = jnp.sum(jnp.where(row == lane, dest, 0.0), axis=0, keepdims=True)
    rank = jnp.sum(jnp.where((lane < row) & (dest == across), 1.0, 0.0), axis=1, keepdims=True)
    place = (dest * 8.0 + rank).astype(BF)
    misc_ref[4 * Z : 5 * Z, :] = place
    for x in range(X):
        low_ref[x * 3 * Z : (x + 1) * 3 * Z, :] = own_ref[(x * Y + 13) * Z : (x + 1) * Y * Z, :]
        high_ref[x * 3 * Z : (x + 1) * 3 * Z, :] = own_ref[x * Y * Z : (x * Y + 3) * Z, :]
    for ref, by in ((low_ref, 3), (high_ref, 0)):
        ref[192:208, :] = place
        ref[208:224, :] = misc_ref[by * Z : (by + 1) * Z, :]


def windows(grad_ref, misc_ref, rows_ref):
    row, col = iota((128, 32), 0), iota((128, 32), 1)
    take = one((col == 2 * (row // 8) - 2 + row % 8) & (row % 8 < 6))
    rows_ref[...] = mm(take, grad_ref[0, 0]).astype(BF)


def widen(own_ref, misc_ref, low_ref, high_ref, rows_ref, mid_ref, mask_ref, gc_ref, up_ref, down_ref):
    for x in range(X):
        at = x * 22 * Z
        mid_ref[at : at + 3 * Z, :] = low_ref[x * 3 * Z : (x + 1) * 3 * Z, :]
        mid_ref[at + 3 * Z : at + 19 * Z, :] = own_ref[x * Y * Z : (x + 1) * Y * Z, :]
        mid_ref[at + 19 * Z : at + 22 * Z, :] = high_ref[x * 3 * Z : (x + 1) * 3 * Z, :]
    mask_ref[0:Z, :] = low_ref[208:224, :]
    mask_ref[Z : 5 * Z, :] = misc_ref[0 : 4 * Z, :]
    mask_ref[5 * Z : 6 * Z, :] = high_ref[208:224, :]
    place = jnp.concatenate(
        [
            low_ref[192:208, :].astype(F32),
            misc_ref[4 * Z : 5 * Z, :].astype(F32) + 2.0,
            high_ref[192:208, :].astype(F32) + 4.0,
        ],
        axis=0,
    )
    bricks = mm(one(place == iota((48, C), 1).astype(F32)), rows_ref[...]).astype(BF)
    for q in range(4):
        gc_ref[0, q] = lanes(bricks, q)
        gc_ref[1, q] = lanes(bricks, 4 + q)
        up_ref[COTS + q * 48 : COTS + (q + 1) * 48, :] = lanes(bricks, 4 + q)
        down_ref[COTS + q * 48 : COTS + (q + 1) * 48, :] = lanes(bricks, q)
    up_ref[0:COTS, :] = mid_ref[22 * Z :, :]
    down_ref[0:COTS, :] = mid_ref[0:COTS, :]
    up_ref[MASK : MASK + 96, :] = mask_ref[...]
    down_ref[MASK : MASK + 96, :] = mask_ref[...]


def unfold(half_ref, other_ref, first_ref, second_ref, down_ref):
    here = (lax.axis_index("z"), lax.axis_index("x"))

    def emit(ref, core, spans):
        for n in range(16):
            s = [lax.rem(h - t + 4, 4) for h, t in zip(here, (n // 4, n % 4))]
            outer, inner = s if core == 0 else (s[1], s[0])
            at = pl.multiple_of((outer * 4 + inner) * PART, 16)
            for lo, hi, out, to in spans:
                i, j = max(lo, n * PART), min(hi, (n + 1) * PART)
                if i < j:
                    v = ref[pl.ds(at + i - n * PART, j - i), :].astype(F32)
                    out[to + i - lo : to + j - lo, :] = v

    def both(a_ref, b_ref):
        emit(a_ref, 0, ((0, 27 * C, second_ref, 0), (27 * C, 28 * C, down_ref, 0)))
        emit(b_ref, 1, ((0, 27 * CIN, first_ref, 0), (27 * CIN, 27 * CIN + 7 * C, down_ref, C)))

    @pl.when(lax.axis_index("c") == 0)
    def _():
        both(half_ref, other_ref)

    @pl.when(lax.axis_index("c") == 1)
    def _():
        both(other_ref, half_ref)


def shift(v, axes, step):
    n = lax.axis_size(axes)
    return lax.ppermute(v, axes, [(i, i + step) for i in range(n) if 0 <= i + step < n])


def swap_cores(v):
    return lax.ppermute(v, "c", [(0, 1), (1, 0)])


def up_matrix():
    m = np.zeros((6 * Z, 96), np.float32)
    for by in range(6):
        for z in range(Z):
            m[by * Z + z, z // 2 % 2 * 48 + (12, 16, 20, 24, 28, 32)[by] + z // 4] = 1
    return jnp.asarray(m, BF)


def turn(v, axes, step):
    size = [lax.axis_size(n) for n in ALL]
    pairs = []
    for d in range(math.prod(size)):
        at = list(np.unravel_index(d, size))
        n = ALL.index(axes[at[1]])
        at[n] = (at[n] + step) % size[n]
        pairs.append((d, int(np.ravel_multi_index(at, size))))
    return lax.ppermute(v, ALL, pairs)


def per_device(features, block_mask, weight_first, weight_second, weight_down, owners, moved_grad):
    own, low, high, misc = call(
        prepare,
        [((X * Y * Z, C), BF), ((224, C), BF), ((224, C), BF), ((80, C), BF)],
        (features, block_mask, owners),
        [VM, SM, VM],
        [((X * Y * Z, C), F32)],
    )
    low, high = shift(low, GY, 1), shift(high, GY, -1)
    (rows,) = call(windows, [((128, 8 * C), BF)], (moved_grad, misc))
    rows = lax.all_to_all(rows, GY, 0, 0, tiled=True)

    mid, mask, gc, up, down = call(
        widen,
        [((4 * 22 * Z, C), BF), ((96, C), BF), ((2, 4, 48, C), BF), ((STRIP, C), BF), ((STRIP, C), BF)],
        (own, misc, low, high, rows),
    )
    low, high = shift(up, GX, 1), shift(down, GX, -1)

    grads, outgoing = call(
        section,
        [((2, HALF, C), BF), ((256, C), BF)],
        (low, mid, high, mask, gc, misc[64:], weight_first, weight_second, weight_down, up_matrix()),
        scratch=[
            ((9 * C, 3 * C), BF),
            ((3 * C, 9 * C), BF),
            ((8 * 20 * Z, C), BF),
            ((X * Y * Z, C), F32),
            ((X * Y * Z, C), BF),
            ((40 * Z, 2 * C), BF),
            ((6 * 18 * Z, C), BF),
            ((X * Y * Z, 3 * C), BF),
            ((3 * C, 6 * Y * Z), BF),
        ],
        flops=8_000_000_000,
    )

    theirs = swap_cores(grads[1])
    half = (grads[0].astype(F32) + theirs.astype(F32)).astype(BF)
    pieces = lax.all_to_all(
        jnp.concatenate([half.reshape(16, PART, C), outgoing.reshape(16, 16, C)], axis=1),
        GY, 0, 0, tiled=True,
    )
    moved = pieces[:, PART:].reshape(16, 8, 2, C).transpose(0, 2, 1, 3).reshape(1, 1, 32, 8 * C)
    part = jnp.sum(pieces[:, :PART].astype(F32), axis=0).astype(BF)
    turned = [turn(part, ("y", "y"), n).astype(F32) for n in (1, 2, 3)]
    part = ((part.astype(F32) + turned[1]) + (turned[0] + turned[2])).astype(BF)
    for axes in (("x", "z"), ("z", "x")):
        part = jnp.concatenate([part] + [turn(part, axes, n) for n in (1, 2, 3)])
    grad_first, grad_second, grad_down = call(
        unfold,
        [((27 * CIN, C), F32), ((27 * C, C), F32), ((8 * C, C), F32)],
        (part, swap_cores(part)),
    )
    return (
        moved,
        grad_first.reshape(27, CIN, C),
        grad_second.reshape(27, C, C),
        grad_down.reshape(8, C, C),
    )


def solution(mesh):
    shape = dict(mesh.shape)
    fine = Mesh(
        mesh.devices.reshape(shape["gx"] // 2, 2, 4, shape["gy"] // 4), ("y", "c", "z", "x")
    )
    whole, tiles = P(GX, GY, None), P(GX, GY, None, None)
    return jax.shard_map(
        per_device,
        mesh=fine,
        in_specs=(whole, whole, P(), P(), P(), tiles, tiles),
        out_specs=(tiles, P(), P(), P()),
        check_vma=False,
    )
```

```python
import math
import jax
import jax.numpy as jnp
import numpy as np
from jax import lax
from jax.experimental import pallas as pl
from jax.experimental.pallas import tpu as pltpu
from jax.sharding import Mesh, PartitionSpec as P

GX, GY, ALL = ("y", "c"), ("z", "x"), ("y", "c", "z", "x")
F32, BF = jnp.float32, jnp.bfloat16
X, Y, Z, C, CIN = 4, 16, 16, 128, 96
HALF, PART = 3584, 224
COTS, MASK, STRIP = 1056, 1248, 1344
NN = (((1,), (0,)), ((), ()))
NT = (((1,), (1,)), ((), ()))
TN = (((0,), (0,)), ((), ()))


def mm(a, b, dims=NN):
    return lax.dot_general(a, b, dims, preferred_element_type=F32)


def iota(shape, axis):
    return lax.broadcasted_iota(jnp.int32, shape, axis)


def one(where):
    return jnp.where(where, 1.0, 0.0).astype(BF)


def z_of(rows):
    return iota((rows, C), 0) % Z


def from_above(v):
    return jnp.where(z_of(v.shape[0]) < Z - 1, pltpu.roll(v, v.shape[0] - 1, 0), 0.0)


def from_below(v):
    return jnp.where(z_of(v.shape[0]) > 0, pltpu.roll(v, 1, 0), 0.0)


def lanes(p, k):
    return p[:, k * C : (k + 1) * C]


def section(
    low_ref, mid_ref, high_ref, mask_ref, gc_ref, misc_ref, w1_ref, w2_ref, back_ref, wd_ref, up_ref,
    grads_ref, out_ref,
    first, sg1, second, ge, g2, gs, vt,
):
    core = lax.axis_index("c")

    def cells(x, y, n):
        ref, x = ((low_ref, x), (mid_ref, x - 3), (high_ref, x - 7))[(x > 2) + (x > 6)]
        return ref[(x * 22 + y) * Z : (x * 22 + y + n) * Z, :]

    def firsts(x, y, n):
        return first[(x * 20 + y) * Z : (x * 20 + y + n) * Z, :]

    def cots(x, y, n):
        return g2[(x * 18 + y) * Z : (x * 18 + y + n) * Z, :]

    def mask_tile(bx, by):
        ref, at = ((low_ref, MASK), (mask_ref, 0), (high_ref, MASK))[bx]
        return ref[at + by * Z : at + (by + 1) * Z, :].astype(F32)

    def cotangent(u, q):
        if u in (1, 2):
            return gc_ref[u - 1, q]
        return (low_ref if u == 0 else high_ref)[COTS + q * 48 : COTS + (q + 1) * 48, :]

    def line(x, y0, cells):
        return jnp.concatenate(
            [mask_tile((x + 4) // 4, (y + 4) // 4) for y in range(y0, y0 + cells)], axis=0
        )

    def taps(get, x, n, w, dims=NN, flip=False):
        wins = []
        for i in range(3):
            for j in range(3):
                ii, jj = (2 - i, 2 - j) if flip else (i, j)
                wins.append(get(x + ii, jj, n))
        return mm(jnp.concatenate(wins, axis=1), w[...], dims)

    def weight_grad(get, x0, y0, rows, put):
        for j in range(3):
            for x in range(6):
                vt[j * C : (j + 1) * C, x * Y * Z : (x + 1) * Y * Z] = get(x0 + x, y0 + j, Y).T
        for i in range(3):
            p = mm(vt[:, i * Y * Z : (i + X) * Y * Z], gs[...]).astype(BF)
            for j in range(3):
                for k in range(3):
                    put(9 * i + 3 * j + k, p[j * C : j * C + rows, k * C : (k + 1) * C])

    def put_z_taps(x, g):
        at = x * Y * Z
        gs[at : at + Y * Z, 0:C] = from_above(g).astype(BF)
        gs[at : at + Y * Z, C : 2 * C] = g.astype(BF)
        gs[at : at + Y * Z, 2 * C : 3 * C] = from_below(g).astype(BF)

    for x in range(8):
        p = taps(cells, x, 20, w1_ref)
        act = line(x - 2, -2, 20)
        pre = act * (lanes(p, 1) + from_below(lanes(p, 0)) + from_above(lanes(p, 2)))
        s = jax.nn.sigmoid(pre)
        first[x * 20 * Z : (x + 1) * 20 * Z, :] = (pre * s).astype(BF)
        if 2 <= x < 6:
            d = act * (s * (1.0 + pre * (1.0 - s)))
            sg1[(x - 2) * Y * Z : (x - 1) * Y * Z, :] = d[2 * Z : 18 * Z]

    even = z_of(6 * Z) % 2 == 0
    for u in range(4):
        both = jnp.concatenate(
            [jnp.concatenate([cotangent(u, 2 * b + c) for b in range(2)], axis=1) for c in range(2)],
            axis=0,
        )
        r = mm(up_ref[...], both)
        for v in range(10):
            by, b = (v + 1) // 2, (v + 1) % 2
            t = r[by * Z : (by + 1) * Z, b * C : (b + 1) * C]
            at = (u * 10 + v) * Z
            ge[at : at + Z, 0:C] = jnp.where(even[:Z], t, 0.0).astype(BF)
            ge[at : at + Z, C : 2 * C] = jnp.where(even[:Z], 0.0, t).astype(BF)

    for x in range(6):
        p = taps(firsts, x, 18, w2_ref)
        act = line(x - 1, -1, 18)
        pre = act * (lanes(p, 1) + from_below(lanes(p, 0)) + from_above(lanes(p, 2)))
        pre = pre + firsts(x + 1, 1, 18).astype(F32)
        s = jax.nn.sigmoid(pre)
        if 1 <= x < 5:
            second[(x - 1) * Y * Z : x * Y * Z, :] = (pre * s)[Z : 17 * Z].astype(BF)
        u, a = (x + 1) // 2, (x + 1) % 2
        back = []
        for b in range(2):
            at = (u * 10 + 1 - b) * Z
            w = jnp.concatenate([wd_ref[4 * a + 2 * b], wd_ref[4 * a + 2 * b + 1]], axis=1)
            back.append(mm(ge[at : at + 9 * Z, :], w, NT))
        g = jnp.concatenate(
            [back[1 - y % 2][y // 2 * Z : (y // 2 + 1) * Z] for y in range(18)], axis=0
        )
        g = (act * g * (s * (1.0 + pre * (1.0 - s)))).astype(BF)
        g2[x * 18 * Z : (x + 1) * 18 * Z, :] = g
        if 1 <= x < 5:
            put_z_taps(x - 1, g[Z : 17 * Z].astype(F32))

    def corner(a, b):
        return jnp.concatenate(
            [
                second[((2 * u + a) * Y + 2 * v + b) * Z : ((2 * u + a) * Y + 2 * v + b + 1) * Z, :]
                for u in range(2)
                for v in range(8)
            ],
            axis=0,
        )

    corners = [corner(a, b) for a in range(2) for b in range(2)]
    wd = jnp.concatenate(
        [jnp.concatenate([wd_ref[2 * q], wd_ref[2 * q + 1]], axis=1) for q in range(4)], axis=0
    )
    p = mm(jnp.concatenate(corners, axis=1), wd)
    coarse = (lanes(p, 0) + from_above(lanes(p, 1))).astype(BF)
    row, col = iota((128, 256), 0), iota((128, 256), 1)
    a, by, b, z = col // 128, col // 32 % 4, col // 16 % 2, col % Z
    order = (row // 16 == 4 * a + 2 * b + z // 2 % 2) & (row % 16 == by * 4 + z // 4) & (z % 2 == 0)
    bricks = mm(one(order), coarse).astype(BF)
    place = jnp.concatenate([misc_ref[4 * Z : 5 * Z, :].astype(F32)] * 8, axis=0)
    place = jnp.concatenate([place] * 2, axis=1)
    target = (8 * (col // 16) + col % 2).astype(F32)
    out_ref[...] = mm(one((place == target) & (row // 16 == col // 2 % 8)), bricks, TN).astype(BF)

    gec = jnp.concatenate([ge[(u * 10 + 1) * Z : (u * 10 + 9) * Z, :] for u in (1, 2)], axis=0)

    def put_a(at, v):
        grads_ref[core, at : at + v.shape[0], :] = v

    def put_b(at, v):
        grads_ref[1 - core, at : at + v.shape[0], :] = v

    for q in range(4):
        r = mm(corners[q], gec, TN).astype(BF)
        for c in range(2):
            t = 2 * q + c
            if t == 0:
                put_a(27 * C, lanes(r, c))
            else:
                put_b(27 * CIN + (t - 1) * C, lanes(r, c))
    put_b(27 * CIN + 7 * C, jnp.zeros((HALF - 27 * CIN - 7 * C, C), BF))
    weight_grad(firsts, 1, 1, C, lambda t, v: put_a(t * C, v))

    for x in range(X):
        p = taps(cots, x, Y, back_ref, NT, flip=True)
        g = lanes(p, 1) + from_above(lanes(p, 0)) + from_below(lanes(p, 2))
        g = g + cots(x + 1, 1, Y).astype(F32)
        g = (g * sg1[x * Y * Z : (x + 1) * Y * Z, :]).astype(BF)
        put_z_taps(x, g.astype(F32))
    weight_grad(cells, 2, 2, CIN, lambda t, v: put_b(t * CIN, v))


VM = pl.BlockSpec(memory_space=pltpu.VMEM)


def call(kernel, outs, args, in_specs=None, scratch=(), flops=10_000_000, vmem=40 << 20):
    return pl.pallas_call(
        kernel,
        out_shape=tuple(jax.ShapeDtypeStruct(shape, dtype) for shape, dtype in outs),
        in_specs=in_specs or [VM] * len(args),
        out_specs=tuple([VM] * len(outs)),
        scratch_shapes=[pltpu.VMEM(*s) if isinstance(s, tuple) else s for s in scratch],
        compiler_params=pltpu.CompilerParams(vmem_limit_bytes=vmem),
        cost_estimate=pl.CostEstimate(
            flops=flops, bytes_accessed=1_000_000, transcendentals=0
        ),
    )(*args)


def arrange(w1_ref, w2_ref, after_ref, first_ref, second_ref, back_ref):
    for m in range(9):
        for k in range(3):
            first_ref[m * C : m * C + CIN, k * C : (k + 1) * C] = w1_ref[3 * m + k]
            second_ref[m * C : (m + 1) * C, k * C : (k + 1) * C] = w2_ref[3 * m + k]
            back_ref[k * C : (k + 1) * C, m * C : (m + 1) * C] = w2_ref[3 * m + k]
        first_ref[m * C + CIN : (m + 1) * C, :] = jnp.zeros((C - CIN, 3 * C), BF)


def prepare(
    grad_hbm, feat_hbm, blocks_hbm, owners_hbm, rows_ref, own_ref, low_ref, high_ref, misc_ref,
    wide, grad_ref, feat_ref, blocks_ref, owners_ref, sems,
):
    copies = [
        pltpu.make_async_copy(a, b, sems.at[n])
        for n, (a, b) in enumerate(
            ((grad_hbm, grad_ref), (feat_hbm, feat_ref), (blocks_hbm, blocks_ref), (owners_hbm, owners_ref))
        )
    ]
    for c in copies:
        c.start()
    copies[0].wait()
    row, col = iota((128, 32), 0), iota((128, 32), 1)
    take = one((col == 2 * (row // 8) - 2 + row % 8) & (row % 8 < 6))
    rows_ref[...] = mm(take, grad_ref[0, 0]).astype(BF)
    for c in copies[1:]:
        c.wait()
    lane = iota((Y, C), 1)
    for x in range(X):
        f = feat_ref[x].astype(F32)
        f = jnp.concatenate([f, jnp.zeros((Y, C), F32)], axis=1)
        for z in range(Z):
            t = jnp.where(lane < CIN, f[:, z * CIN : z * CIN + C], 0.0)
            wide[pl.ds(x * Y * Z + z, Y, stride=Z), :] = t
    blocks = blocks_ref[0].astype(F32)
    mine = iota((Z, 4), 0) // 4 == iota((Z, 4), 1)
    for by in range(4):
        m = jnp.sum(jnp.where(mine, blocks[by : by + 1, :], 0.0), axis=1, keepdims=True)
        m = jnp.broadcast_to(m, (Z, C))
        misc_ref[by * Z : (by + 1) * Z, :] = m.astype(BF)
        for x in range(X):
            for y in range(4 * by, 4 * by + 4):
                at = (x * Y + y) * Z
                own_ref[at : at + Z, :] = (wide[at : at + Z, :] * m).astype(BF)
    row, col = iota((16, 16), 0), iota((16, 16), 1)
    across = jnp.broadcast_to(owners_ref[...].astype(F32), (16, 16))
    dest = jnp.sum(jnp.where(row == col, across, 0.0), axis=1, keepdims=True)
    rank = jnp.sum(jnp.where((col < row) & (dest == across), 1.0, 0.0), axis=1, keepdims=True)
    place = jnp.broadcast_to(dest * 8.0 + rank, (16, C)).astype(BF)
    misc_ref[4 * Z : 5 * Z, :] = place
    for x in range(X):
        low_ref[x * 3 * Z : (x + 1) * 3 * Z, :] = own_ref[(x * Y + 13) * Z : (x + 1) * Y * Z, :]
        high_ref[x * 3 * Z : (x + 1) * 3 * Z, :] = own_ref[x * Y * Z : (x * Y + 3) * Z, :]
    for ref, by in ((low_ref, 3), (high_ref, 0)):
        ref[192:208, :] = place
        ref[208:224, :] = misc_ref[by * Z : (by + 1) * Z, :]


def widen(own_ref, misc_ref, low_ref, high_ref, rows_ref, mid_ref, mask_ref, gc_ref, up_ref, down_ref):
    for x in range(X):
        at = x * 22 * Z
        mid_ref[at : at + 3 * Z, :] = low_ref[x * 3 * Z : (x + 1) * 3 * Z, :]
        mid_ref[at + 3 * Z : at + 19 * Z, :] = own_ref[x * Y * Z : (x + 1) * Y * Z, :]
        mid_ref[at + 19 * Z : at + 22 * Z, :] = high_ref[x * 3 * Z : (x + 1) * 3 * Z, :]
    mask_ref[0:Z, :] = low_ref[208:224, :]
    mask_ref[Z : 5 * Z, :] = misc_ref[0 : 4 * Z, :]
    mask_ref[5 * Z : 6 * Z, :] = high_ref[208:224, :]
    place = jnp.concatenate(
        [
            low_ref[192:208, :].astype(F32),
            misc_ref[4 * Z : 5 * Z, :].astype(F32) + 2.0,
            high_ref[192:208, :].astype(F32) + 4.0,
        ],
        axis=0,
    )
    bricks = mm(one(place == iota((48, C), 1).astype(F32)), rows_ref[...]).astype(BF)
    for q in range(4):
        gc_ref[0, q] = lanes(bricks, q)
        gc_ref[1, q] = lanes(bricks, 4 + q)
        up_ref[COTS + q * 48 : COTS + (q + 1) * 48, :] = lanes(bricks, 4 + q)
        down_ref[COTS + q * 48 : COTS + (q + 1) * 48, :] = lanes(bricks, q)
    up_ref[0:COTS, :] = mid_ref[22 * Z :, :]
    down_ref[0:COTS, :] = mid_ref[0:COTS, :]
    up_ref[MASK : MASK + 96, :] = mask_ref[...]
    down_ref[MASK : MASK + 96, :] = mask_ref[...]


def unfold(half_ref, other_ref, first_ref, second_ref, down_ref):
    def both(a_ref, b_ref):
        second_ref[...] = a_ref[: 27 * C, :].astype(F32)
        down_ref[:C, :] = a_ref[27 * C :, :].astype(F32)
        first_ref[...] = b_ref[: 27 * CIN, :].astype(F32)
        down_ref[C:, :] = b_ref[27 * CIN : 27 * CIN + 7 * C, :].astype(F32)

    @pl.when(lax.axis_index("c") == 0)
    def _():
        both(half_ref, other_ref)

    @pl.when(lax.axis_index("c") == 1)
    def _():
        both(other_ref, half_ref)


def shift(v, axes, step):
    n = lax.axis_size(axes)
    return lax.ppermute(v, axes, [(i, i + step) for i in range(n) if 0 <= i + step < n])


def swap_cores(v):
    return lax.ppermute(v, "c", [(0, 1), (1, 0)])


def up_matrix():
    m = np.zeros((6 * Z, 96), np.float32)
    for by in range(6):
        for z in range(Z):
            m[by * Z + z, z // 2 % 2 * 48 + (12, 16, 20, 24, 28, 32)[by] + z // 4] = 1
    return jnp.asarray(m, BF)


def turn(v, axes, step):
    size = [lax.axis_size(n) for n in ALL]
    pairs = []
    for d in range(math.prod(size)):
        at = list(np.unravel_index(d, size))
        n = ALL.index(axes[at[1]])
        at[n] = (at[n] + step) % size[n]
        pairs.append((d, int(np.ravel_multi_index(at, size))))
    return lax.ppermute(v, ALL, pairs)


def per_device(features, block_mask, weight_first, weight_second, weight_down, owners, moved_grad):
    rows, own, low, high, misc = call(
        prepare,
        [((128, 8 * C), BF), ((X * Y * Z, C), BF), ((224, C), BF), ((224, C), BF), ((80, C), BF)],
        (moved_grad, features, block_mask, owners.reshape(1, 16)),
        [pl.BlockSpec(memory_space=pltpu.HBM)] * 4,
        [
            ((X * Y * Z, C), F32),
            (moved_grad.shape, BF),
            (features.shape, BF),
            (block_mask.shape, jnp.int32),
            ((1, 16), jnp.int32),
            pltpu.SemaphoreType.DMA((4,)),
        ],
        vmem=60 << 20,
    )
    low, high = shift(low, GY, 1), shift(high, GY, -1)
    rows = lax.all_to_all(rows, GY, 0, 0, tiled=True)

    mid, mask, gc, up, down = call(
        widen,
        [((4 * 22 * Z, C), BF), ((96, C), BF), ((2, 4, 48, C), BF), ((STRIP, C), BF), ((STRIP, C), BF)],
        (own, misc, low, high, rows),
    )
    low, high = shift(up, GX, 1), shift(down, GX, -1)
    w1, w2, back = call(
        arrange,
        [((9 * C, 3 * C), BF), ((9 * C, 3 * C), BF), ((3 * C, 9 * C), BF)],
        (weight_first, weight_second, mask),
        flops=2_000_000_000,
    )

    grads, outgoing = call(
        section,
        [((2, HALF, C), BF), ((256, C), BF)],
        (low, mid, high, mask, gc, misc, w1, w2, back, weight_down, up_matrix()),
        scratch=[
            ((8 * 20 * Z, C), BF),
            ((X * Y * Z, C), F32),
            ((X * Y * Z, C), BF),
            ((40 * Z, 2 * C), BF),
            ((6 * 18 * Z, C), BF),
            ((X * Y * Z, 3 * C), BF),
            ((3 * C, 6 * Y * Z), BF),
        ],
        flops=8_000_000_000,
    )

    theirs = swap_cores(grads[1])
    half = (grads[0].astype(F32) + theirs.astype(F32)).astype(BF)
    pieces = lax.all_to_all(
        jnp.concatenate([half.reshape(16, PART, C), outgoing.reshape(16, 16, C)], axis=1),
        GY, 0, 0, tiled=True,
    )
    moved = pieces[:, PART:].reshape(16, 8, 2, C).transpose(0, 2, 1, 3).reshape(1, 1, 32, 8 * C)
    part = jnp.sum(pieces[:, :PART].astype(F32), axis=0).astype(BF)
    turned = [turn(part, ("y", "y"), n).astype(F32) for n in (1, 2, 3)]
    part = ((part.astype(F32) + turned[1]) + (turned[0] + turned[2])).astype(BF)
    part = lax.all_to_all(jnp.broadcast_to(part[None], (16, PART, C)), GY, 0, 0, tiled=True)
    part = part.reshape(HALF, C)
    grad_first, grad_second, grad_down = call(
        unfold,
        [((27 * CIN, C), F32), ((27 * C, C), F32), ((8 * C, C), F32)],
        (part, swap_cores(part)),
    )
    return (
        moved,
        grad_first.reshape(27, CIN, C),
        grad_second.reshape(27, C, C),
        grad_down.reshape(8, C, C),
    )


def solution(mesh):
    shape = dict(mesh.shape)
    fine = Mesh(
        mesh.devices.reshape(shape["gx"] // 2, 2, 4, shape["gy"] // 4), ("y", "c", "z", "x")
    )
    whole, tiles = P(GX, GY, None), P(GX, GY, None, None)
    return jax.shard_map(
        per_device,
        mesh=fine,
        in_specs=(whole, whole, P(), P(), P(), tiles, tiles),
        out_specs=(tiles, P(), P(), P()),
        check_vma=False,
    )
```

```python
import jax
import jax.numpy as jnp
import numpy as np
from jax import lax
from jax.experimental import pallas as pl
from jax.experimental.pallas import tpu as pltpu
from jax.sharding import Mesh, PartitionSpec as P

GX, GY = ("y", "c"), ("z", "x")
F32, BF = jnp.float32, jnp.bfloat16
X, Y, Z, C, CIN = 4, 16, 16, 128, 96
HALF, PART = 3584, 224
COTS, MASK, STRIP = 1056, 1248, 1344
NN = (((1,), (0,)), ((), ()))
NT = (((1,), (1,)), ((), ()))
TN = (((0,), (0,)), ((), ()))


def mm(a, b, dims=NN):
    return lax.dot_general(a, b, dims, preferred_element_type=F32)


def iota(shape, axis):
    return lax.broadcasted_iota(jnp.int32, shape, axis)


def one(where):
    return jnp.where(where, 1.0, 0.0).astype(BF)


def z_of(rows):
    return iota((rows, C), 0) % Z


def from_above(v):
    return jnp.where(z_of(v.shape[0]) < Z - 1, pltpu.roll(v, v.shape[0] - 1, 0), 0.0)


def from_below(v):
    return jnp.where(z_of(v.shape[0]) > 0, pltpu.roll(v, 1, 0), 0.0)


def lanes(p, k):
    return p[:, k * C : (k + 1) * C]


def section(
    near_ref, mid_ref, far_ref, mask_ref, gc_ref, misc_ref, w1_ref, w2_ref, back_ref, wd_ref, up_ref,
    grads_ref, out_ref,
    sides, first, sg1, second, ge, g2, gs, vt,
):
    core = lax.axis_index("c")
    sides[1 - core] = near_ref[...]
    sides[core] = far_ref[...]
    low_ref, high_ref = sides.at[0], sides.at[1]

    def cells(x, y, n):
        ref, x = ((low_ref, x), (mid_ref, x - 3), (high_ref, x - 7))[(x > 2) + (x > 6)]
        return ref[(x * 22 + y) * Z : (x * 22 + y + n) * Z, :]

    def firsts(x, y, n):
        return first[(x * 20 + y) * Z : (x * 20 + y + n) * Z, :]

    def cots(x, y, n):
        return g2[(x * 18 + y) * Z : (x * 18 + y + n) * Z, :]

    def mask_tile(bx, by):
        ref, at = ((low_ref, MASK), (mask_ref, 0), (high_ref, MASK))[bx]
        return ref[at + by * Z : at + (by + 1) * Z, :].astype(F32)

    def cotangent(u, q):
        if u in (1, 2):
            return gc_ref[u - 1, q]
        return (low_ref if u == 0 else high_ref)[COTS + q * 48 : COTS + (q + 1) * 48, :]

    def line(x, y0, cells):
        return jnp.concatenate(
            [mask_tile((x + 4) // 4, (y + 4) // 4) for y in range(y0, y0 + cells)], axis=0
        )

    def taps(get, x, n, w, dims=NN, flip=False):
        wins = []
        for i in range(3):
            for j in range(3):
                ii, jj = (2 - i, 2 - j) if flip else (i, j)
                wins.append(get(x + ii, jj, n))
        return mm(jnp.concatenate(wins, axis=1), w[...], dims)

    def weight_grad(get, x0, y0, rows, put):
        for j in range(3):
            for x in range(6):
                vt[j * C : (j + 1) * C, x * Y * Z : (x + 1) * Y * Z] = get(x0 + x, y0 + j, Y).T
        for i in range(3):
            p = mm(vt[:, i * Y * Z : (i + X) * Y * Z], gs[...]).astype(BF)
            for j in range(3):
                for k in range(3):
                    put(9 * i + 3 * j + k, p[j * C : j * C + rows, k * C : (k + 1) * C])

    def put_z_taps(x, g):
        at = x * Y * Z
        gs[at : at + Y * Z, 0:C] = from_above(g).astype(BF)
        gs[at : at + Y * Z, C : 2 * C] = g.astype(BF)
        gs[at : at + Y * Z, 2 * C : 3 * C] = from_below(g).astype(BF)

    for x in range(8):
        p = taps(cells, x, 20, w1_ref)
        act = line(x - 2, -2, 20)
        pre = act * (lanes(p, 1) + from_below(lanes(p, 0)) + from_above(lanes(p, 2)))
        s = jax.nn.sigmoid(pre)
        first[x * 20 * Z : (x + 1) * 20 * Z, :] = (pre * s).astype(BF)
        if 2 <= x < 6:
            d = act * (s * (1.0 + pre * (1.0 - s)))
            sg1[(x - 2) * Y * Z : (x - 1) * Y * Z, :] = d[2 * Z : 18 * Z]

    even = z_of(6 * Z) % 2 == 0
    for u in range(4):
        both = jnp.concatenate(
            [jnp.concatenate([cotangent(u, 2 * b + c) for b in range(2)], axis=1) for c in range(2)],
            axis=0,
        )
        r = mm(up_ref[...], both)
        for v in range(10):
            by, b = (v + 1) // 2, (v + 1) % 2
            t = r[by * Z : (by + 1) * Z, b * C : (b + 1) * C]
            at = (u * 10 + v) * Z
            ge[at : at + Z, 0:C] = jnp.where(even[:Z], t, 0.0).astype(BF)
            ge[at : at + Z, C : 2 * C] = jnp.where(even[:Z], 0.0, t).astype(BF)

    for x in range(6):
        p = taps(firsts, x, 18, w2_ref)
        act = line(x - 1, -1, 18)
        pre = act * (lanes(p, 1) + from_below(lanes(p, 0)) + from_above(lanes(p, 2)))
        pre = pre + firsts(x + 1, 1, 18).astype(F32)
        s = jax.nn.sigmoid(pre)
        if 1 <= x < 5:
            second[(x - 1) * Y * Z : x * Y * Z, :] = (pre * s)[Z : 17 * Z].astype(BF)
        u, a = (x + 1) // 2, (x + 1) % 2
        back = []
        for b in range(2):
            at = (u * 10 + 1 - b) * Z
            w = jnp.concatenate([wd_ref[4 * a + 2 * b], wd_ref[4 * a + 2 * b + 1]], axis=1)
            back.append(mm(ge[at : at + 9 * Z, :], w, NT))
        g = jnp.concatenate(
            [back[1 - y % 2][y // 2 * Z : (y // 2 + 1) * Z] for y in range(18)], axis=0
        )
        g = (act * g * (s * (1.0 + pre * (1.0 - s)))).astype(BF)
        g2[x * 18 * Z : (x + 1) * 18 * Z, :] = g
        if 1 <= x < 5:
            put_z_taps(x - 1, g[Z : 17 * Z].astype(F32))

    def corner(a, b):
        return jnp.concatenate(
            [
                second[((2 * u + a) * Y + 2 * v + b) * Z : ((2 * u + a) * Y + 2 * v + b + 1) * Z, :]
                for u in range(2)
                for v in range(8)
            ],
            axis=0,
        )

    corners = [corner(a, b) for a in range(2) for b in range(2)]
    wd = jnp.concatenate(
        [jnp.concatenate([wd_ref[2 * q], wd_ref[2 * q + 1]], axis=1) for q in range(4)], axis=0
    )
    p = mm(jnp.concatenate(corners, axis=1), wd)
    coarse = (lanes(p, 0) + from_above(lanes(p, 1))).astype(BF)
    row, col = iota((128, 256), 0), iota((128, 256), 1)
    a, by, b, z = col // 128, col // 32 % 4, col // 16 % 2, col % Z
    order = (row // 16 == 4 * a + 2 * b + z // 2 % 2) & (row % 16 == by * 4 + z // 4) & (z % 2 == 0)
    bricks = mm(one(order), coarse).astype(BF)
    place = jnp.concatenate([misc_ref[4 * Z : 5 * Z, :].astype(F32)] * 8, axis=0)
    place = jnp.concatenate([place] * 2, axis=1)
    target = (8 * (col // 16) + col % 2).astype(F32)
    out_ref[...] = mm(one((place == target) & (row // 16 == col // 2 % 8)), bricks, TN).astype(BF)

    gec = jnp.concatenate([ge[(u * 10 + 1) * Z : (u * 10 + 9) * Z, :] for u in (1, 2)], axis=0)

    def put_a(at, v):
        grads_ref[core, at : at + v.shape[0], :] = v

    def put_b(at, v):
        grads_ref[1 - core, at : at + v.shape[0], :] = v

    for q in range(4):
        r = mm(corners[q], gec, TN).astype(BF)
        for c in range(2):
            t = 2 * q + c
            if t == 0:
                put_a(27 * C, lanes(r, c))
            else:
                put_b(27 * CIN + (t - 1) * C, lanes(r, c))
    put_b(27 * CIN + 7 * C, jnp.zeros((HALF - 27 * CIN - 7 * C, C), BF))
    weight_grad(firsts, 1, 1, C, lambda t, v: put_a(t * C, v))

    for x in range(X):
        p = taps(cots, x, Y, back_ref, NT, flip=True)
        g = lanes(p, 1) + from_above(lanes(p, 0)) + from_below(lanes(p, 2))
        g = g + cots(x + 1, 1, Y).astype(F32)
        g = (g * sg1[x * Y * Z : (x + 1) * Y * Z, :]).astype(BF)
        put_z_taps(x, g.astype(F32))
    weight_grad(cells, 2, 2, CIN, lambda t, v: put_b(t * CIN, v))


VM = pl.BlockSpec(memory_space=pltpu.VMEM)


def call(kernel, outs, args, in_specs=None, scratch=(), flops=10_000_000, vmem=40 << 20):
    return pl.pallas_call(
        kernel,
        out_shape=tuple(jax.ShapeDtypeStruct(shape, dtype) for shape, dtype in outs),
        in_specs=in_specs or [VM] * len(args),
        out_specs=tuple([VM] * len(outs)),
        scratch_shapes=[pltpu.VMEM(*s) if isinstance(s, tuple) else s for s in scratch],
        compiler_params=pltpu.CompilerParams(vmem_limit_bytes=vmem),
        cost_estimate=pl.CostEstimate(
            flops=flops, bytes_accessed=1_000_000, transcendentals=0
        ),
    )(*args)


def arrange(w1_ref, w2_ref, after_ref, first_ref, second_ref, back_ref):
    for m in range(9):
        for k in range(3):
            first_ref[m * C : m * C + CIN, k * C : (k + 1) * C] = w1_ref[3 * m + k]
            second_ref[m * C : (m + 1) * C, k * C : (k + 1) * C] = w2_ref[3 * m + k]
            back_ref[k * C : (k + 1) * C, m * C : (m + 1) * C] = w2_ref[3 * m + k]
        first_ref[m * C + CIN : (m + 1) * C, :] = jnp.zeros((C - CIN, 3 * C), BF)


def prepare(
    grad_hbm, feat_hbm, blocks_hbm, owners_hbm, rows_ref, own_ref, near_ref, far_ref, misc_ref,
    wide, grad_ref, feat_ref, blocks_ref, owners_ref, sems,
):
    copies = [
        pltpu.make_async_copy(a, b, sems.at[n])
        for n, (a, b) in enumerate(
            ((grad_hbm, grad_ref), (feat_hbm, feat_ref), (blocks_hbm, blocks_ref), (owners_hbm, owners_ref))
        )
    ]
    for c in copies:
        c.start()
    copies[0].wait()
    row, col = iota((128, 32), 0), iota((128, 32), 1)
    take = one((col == 2 * (row // 8) - 2 + row % 8) & (row % 8 < 6))
    rows_ref[...] = mm(take, grad_ref[0, 0]).astype(BF)
    for c in copies[1:]:
        c.wait()
    lane = iota((Y, C), 1)
    for x in range(X):
        f = feat_ref[x].astype(F32)
        f = jnp.concatenate([f, jnp.zeros((Y, C), F32)], axis=1)
        for z in range(Z):
            t = jnp.where(lane < CIN, f[:, z * CIN : z * CIN + C], 0.0)
            wide[pl.ds(x * Y * Z + z, Y, stride=Z), :] = t
    blocks = blocks_ref[0].astype(F32)
    mine = iota((Z, 4), 0) // 4 == iota((Z, 4), 1)
    for by in range(4):
        m = jnp.sum(jnp.where(mine, blocks[by : by + 1, :], 0.0), axis=1, keepdims=True)
        m = jnp.broadcast_to(m, (Z, C))
        misc_ref[by * Z : (by + 1) * Z, :] = m.astype(BF)
        for x in range(X):
            for y in range(4 * by, 4 * by + 4):
                at = (x * Y + y) * Z
                own_ref[at : at + Z, :] = (wide[at : at + Z, :] * m).astype(BF)
    row, col = iota((16, 16), 0), iota((16, 16), 1)
    across = jnp.broadcast_to(owners_ref[...].astype(F32), (16, 16))
    dest = jnp.sum(jnp.where(row == col, across, 0.0), axis=1, keepdims=True)
    rank = jnp.sum(jnp.where((col < row) & (dest == across), 1.0, 0.0), axis=1, keepdims=True)
    place = jnp.broadcast_to(dest * 8.0 + rank, (16, C)).astype(BF)
    misc_ref[4 * Z : 5 * Z, :] = place

    def fill(up, down):
        for x in range(X):
            up[x * 3 * Z : (x + 1) * 3 * Z, :] = own_ref[(x * Y + 13) * Z : (x + 1) * Y * Z, :]
            down[x * 3 * Z : (x + 1) * 3 * Z, :] = own_ref[x * Y * Z : (x * Y + 3) * Z, :]
        for ref, by in ((up, 3), (down, 0)):
            ref[192:208, :] = place
            ref[208:224, :] = misc_ref[by * Z : (by + 1) * Z, :]

    @pl.when(lax.rem(lax.axis_index("x"), 2) == 0)
    def _():
        fill(near_ref, far_ref)

    @pl.when(lax.rem(lax.axis_index("x"), 2) == 1)
    def _():
        fill(far_ref, near_ref)


def widen(
    own_ref, misc_ref, beside_ref, beyond_ref, rows_ref,
    mid_ref, mask_ref, gc_ref, near_ref, far_ref,
    sides,
):
    odd = lax.rem(lax.axis_index("x"), 2)
    sides[1 - odd] = beside_ref[...]
    sides[odd] = beyond_ref[...]
    low_ref, high_ref = sides.at[0], sides.at[1]
    for x in range(X):
        at = x * 22 * Z
        mid_ref[at : at + 3 * Z, :] = low_ref[x * 3 * Z : (x + 1) * 3 * Z, :]
        mid_ref[at + 3 * Z : at + 19 * Z, :] = own_ref[x * Y * Z : (x + 1) * Y * Z, :]
        mid_ref[at + 19 * Z : at + 22 * Z, :] = high_ref[x * 3 * Z : (x + 1) * 3 * Z, :]
    mask_ref[0:Z, :] = low_ref[208:224, :]
    mask_ref[Z : 5 * Z, :] = misc_ref[0 : 4 * Z, :]
    mask_ref[5 * Z : 6 * Z, :] = high_ref[208:224, :]
    place = jnp.concatenate(
        [
            low_ref[192:208, :].astype(F32),
            misc_ref[4 * Z : 5 * Z, :].astype(F32) + 2.0,
            high_ref[192:208, :].astype(F32) + 4.0,
        ],
        axis=0,
    )
    bricks = mm(one(place == iota((48, C), 1).astype(F32)), rows_ref[...]).astype(BF)
    for q in range(8):
        gc_ref[q // 4, q % 4] = lanes(bricks, q)

    def fill(up, down):
        for q in range(4):
            up[COTS + q * 48 : COTS + (q + 1) * 48, :] = lanes(bricks, 4 + q)
            down[COTS + q * 48 : COTS + (q + 1) * 48, :] = lanes(bricks, q)
        up[0:COTS, :] = mid_ref[22 * Z :, :]
        down[0:COTS, :] = mid_ref[0:COTS, :]
        for ref in (up, down):
            ref[MASK : MASK + 96, :] = mask_ref[...]

    @pl.when(lax.axis_index("c") == 0)
    def _():
        fill(near_ref, far_ref)

    @pl.when(lax.axis_index("c") == 1)
    def _():
        fill(far_ref, near_ref)


def unfold(half_ref, other_ref, first_ref, second_ref, down_ref):
    def both(a_ref, b_ref):
        second_ref[...] = a_ref[: 27 * C, :].astype(F32)
        down_ref[:C, :] = a_ref[27 * C :, :].astype(F32)
        first_ref[...] = b_ref[: 27 * CIN, :].astype(F32)
        down_ref[C:, :] = b_ref[27 * CIN : 27 * CIN + 7 * C, :].astype(F32)

    @pl.when(lax.axis_index("c") == 0)
    def _():
        both(half_ref, other_ref)

    @pl.when(lax.axis_index("c") == 1)
    def _():
        both(other_ref, half_ref)


def swap(v, axes, first):
    n = lax.axis_size(axes)
    pairs = [(i, i + 1) for i in range(first, n - 1, 2)]
    return lax.ppermute(v, axes, pairs + [(j, i) for i, j in pairs])


def swap_cores(v):
    return lax.ppermute(v, "c", [(0, 1), (1, 0)])


def up_matrix():
    m = np.zeros((6 * Z, 96), np.float32)
    for by in range(6):
        for z in range(Z):
            m[by * Z + z, z // 2 % 2 * 48 + (12, 16, 20, 24, 28, 32)[by] + z // 4] = 1
    return jnp.asarray(m, BF)


def flip(v, axis, bits):
    return lax.ppermute(v, axis, [(i, i ^ bits) for i in range(lax.axis_size(axis))])


def per_device(features, block_mask, weight_first, weight_second, weight_down, owners, moved_grad):
    rows, own, beside, beyond, misc = call(
        prepare,
        [((128, 8 * C), BF), ((X * Y * Z, C), BF), ((224, C), BF), ((224, C), BF), ((80, C), BF)],
        (moved_grad, features, block_mask, owners.reshape(1, 16)),
        [pl.BlockSpec(memory_space=pltpu.HBM)] * 4,
        [
            ((X * Y * Z, C), F32),
            (moved_grad.shape, BF),
            (features.shape, BF),
            (block_mask.shape, jnp.int32),
            ((1, 16), jnp.int32),
            pltpu.SemaphoreType.DMA((4,)),
        ],
        vmem=60 << 20,
    )
    beyond, beside = swap(beyond, GY, 1), swap(beside, GY, 0)
    rows = lax.all_to_all(rows, GY, 0, 0, tiled=True)

    mid, mask, gc, near, far = call(
        widen,
        [((4 * 22 * Z, C), BF), ((96, C), BF), ((2, 4, 48, C), BF), ((STRIP, C), BF), ((STRIP, C), BF)],
        (own, misc, beside, beyond, rows),
        scratch=[((2, 224, C), BF)],
    )
    far, near = swap(far, GX, 1), swap(near, GX, 0)
    w1, w2, back = call(
        arrange,
        [((9 * C, 3 * C), BF), ((9 * C, 3 * C), BF), ((3 * C, 9 * C), BF)],
        (weight_first, weight_second, mask),
        flops=2_000_000_000,
    )

    grads, outgoing = call(
        section,
        [((2, HALF, C), BF), ((256, C), BF)],
        (near, mid, far, mask, gc, misc, w1, w2, back, weight_down, up_matrix()),
        scratch=[
            ((2, STRIP, C), BF),
            ((8 * 20 * Z, C), BF),
            ((X * Y * Z, C), F32),
            ((X * Y * Z, C), BF),
            ((40 * Z, 2 * C), BF),
            ((6 * 18 * Z, C), BF),
            ((X * Y * Z, 3 * C), BF),
            ((3 * C, 6 * Y * Z), BF),
        ],
        flops=8_000_000_000,
    )

    theirs = swap_cores(grads[1])
    half = (grads[0].astype(F32) + theirs.astype(F32)).astype(BF)
    pieces = lax.all_to_all(
        jnp.concatenate([half.reshape(16, PART, C), outgoing.reshape(16, 16, C)], axis=1),
        GY, 0, 0, tiled=True,
    )
    moved = pieces[:, PART:].reshape(16, 8, 2, C).transpose(0, 2, 1, 3).reshape(1, 1, 32, 8 * C)
    part = jnp.sum(pieces[:, :PART].astype(F32), axis=0).astype(BF)
    others = [flip(part, "y", n).astype(F32) for n in (1, 2, 3)]
    part = ((part.astype(F32) + others[0]) + (others[1] + others[2])).astype(BF)
    part = lax.all_to_all(jnp.broadcast_to(part[None], (16, PART, C)), GY, 0, 0, tiled=True)
    part = part.reshape(HALF, C)
    grad_first, grad_second, grad_down = call(
        unfold,
        [((27 * CIN, C), F32), ((27 * C, C), F32), ((8 * C, C), F32)],
        (part, swap_cores(part)),
    )
    return (
        moved,
        grad_first.reshape(27, CIN, C),
        grad_second.reshape(27, C, C),
        grad_down.reshape(8, C, C),
    )


def solution(mesh):
    shape = dict(mesh.shape)
    fine = Mesh(
        mesh.devices.reshape(shape["gx"] // 2, 2, 4, shape["gy"] // 4), ("y", "c", "z", "x")
    )
    whole, tiles = P(GX, GY, None), P(GX, GY, None, None)
    return jax.shard_map(
        per_device,
        mesh=fine,
        in_specs=(whole, whole, P(), P(), P(), tiles, tiles),
        out_specs=(tiles, P(), P(), P()),
        check_vma=False,
    )
```

```python
import functools

import jax
import jax.numpy as jnp
import numpy as np
from jax import lax
from jax.experimental import pallas as pl
from jax.experimental.pallas import tpu as pltpu
from jax.sharding import Mesh, PartitionSpec as P

GX, GY = ("y", "c"), ("z", "x")
F32, BF = jnp.float32, jnp.bfloat16
X, Y, Z, C, CIN = 4, 16, 16, 128, 96
HALF, PART = 3584, 224
OWN = 1024
COTS, MASK, STRIP = 1056, 1248, 1344
NN = (((1,), (0,)), ((), ()))
NT = (((1,), (1,)), ((), ()))
TN = (((0,), (0,)), ((), ()))


def mm(a, b, dims=NN):
    return lax.dot_general(a, b, dims, preferred_element_type=F32)


def iota(shape, axis):
    return lax.broadcasted_iota(jnp.int32, shape, axis)


def one(where):
    return jnp.where(where, 1.0, 0.0).astype(BF)


def z_of(rows):
    return iota((rows, C), 0) % Z


def from_above(v):
    return jnp.where(z_of(v.shape[0]) < Z - 1, pltpu.roll(v, v.shape[0] - 1, 0), 0.0)


def from_below(v):
    return jnp.where(z_of(v.shape[0]) > 0, pltpu.roll(v, 1, 0), 0.0)


def lanes(p, k):
    return p[:, k * C : (k + 1) * C]


def taps(get, x, n, w, dims=NN, flip=False, lines=(0, 1, 2)):
    wins = []
    for i in lines:
        for j in range(3):
            wins.append(get(x + 2 - i, 2 - j, n) if flip else get(x + i, j, n))
    if len(lines) < 3:
        w = w[3 * lines[0] * C : 3 * (lines[-1] + 1) * C, :]
    else:
        w = w[...]
    return mm(jnp.concatenate(wins, axis=1), w, dims)


def section(
    near_ref, mid_ref, far_ref, mask_ref, gc_ref, place_ref, part_ref, w1_ref, w2_ref, back_ref, wd_ref, up_ref,
    grads_ref, out_ref,
    sides, first, sg1, second, ge, g2, gs, vt,
):
    core = lax.axis_index("c")
    sides[1 - core] = near_ref[...]
    sides[core] = far_ref[...]
    low_ref, high_ref = sides.at[0], sides.at[1]

    def cells(x, y, n):
        ref, x = ((low_ref, x), (mid_ref, x - 3), (high_ref, x - 7))[(x > 2) + (x > 6)]
        return ref[(x * 22 + y) * Z : (x * 22 + y + n) * Z, :]

    def firsts(x, y, n):
        return first[(x * 20 + y) * Z : (x * 20 + y + n) * Z, :]

    def cots(x, y, n):
        return g2[(x * 18 + y) * Z : (x * 18 + y + n) * Z, :]

    def mask_tile(bx, by):
        ref, at = ((low_ref, MASK), (mask_ref, 0), (high_ref, MASK))[bx]
        return ref[at + by * Z : at + (by + 1) * Z, :].astype(F32)

    def cotangent(u, q):
        if u in (1, 2):
            return gc_ref[u - 1, q]
        return (low_ref if u == 0 else high_ref)[COTS + q * 48 : COTS + (q + 1) * 48, :]

    def line(x, y0, cells):
        return jnp.concatenate(
            [mask_tile((x + 4) // 4, (y + 4) // 4) for y in range(y0, y0 + cells)], axis=0
        )

    def weight_grad(get, x0, y0, rows, put):
        for j in range(3):
            for x in range(6):
                vt[j * C : (j + 1) * C, x * Y * Z : (x + 1) * Y * Z] = get(x0 + x, y0 + j, Y).T
        for i in range(3):
            p = mm(vt[:, i * Y * Z : (i + X) * Y * Z], gs[...]).astype(BF)
            for j in range(3):
                for k in range(3):
                    put(9 * i + 3 * j + k, p[j * C : j * C + rows, k * C : (k + 1) * C])

    def put_z_taps(x, g):
        at = x * Y * Z
        gs[at : at + Y * Z, 0:C] = from_above(g).astype(BF)
        gs[at : at + Y * Z, C : 2 * C] = g.astype(BF)
        gs[at : at + Y * Z, 2 * C : 3 * C] = from_below(g).astype(BF)

    for x in range(8):
        pre = jnp.zeros((20 * Z, C), F32) if x in (0, 7) else part_ref[x - 1]
        if x not in (3, 4):
            p = taps(cells, x, 20, w1_ref, lines=[i for i in range(3) if not 3 <= x + i < 7])
            pre = pre + (lanes(p, 1) + from_below(lanes(p, 0)) + from_above(lanes(p, 2)))
        act = line(x - 2, -2, 20)
        pre = act * pre
        s = jax.nn.sigmoid(pre)
        first[x * 20 * Z : (x + 1) * 20 * Z, :] = (pre * s).astype(BF)
        if 2 <= x < 6:
            d = act * (s * (1.0 + pre * (1.0 - s)))
            sg1[(x - 2) * Y * Z : (x - 1) * Y * Z, :] = d[2 * Z : 18 * Z]

    even = z_of(6 * Z) % 2 == 0
    for u in range(4):
        both = jnp.concatenate(
            [jnp.concatenate([cotangent(u, 2 * b + c) for b in range(2)], axis=1) for c in range(2)],
            axis=0,
        )
        r = mm(up_ref[...], both)
        for v in range(10):
            by, b = (v + 1) // 2, (v + 1) % 2
            t = r[by * Z : (by + 1) * Z, b * C : (b + 1) * C]
            at = (u * 10 + v) * Z
            ge[at : at + Z, 0:C] = jnp.where(even[:Z], t, 0.0).astype(BF)
            ge[at : at + Z, C : 2 * C] = jnp.where(even[:Z], 0.0, t).astype(BF)

    for x in range(6):
        p = taps(firsts, x, 18, w2_ref)
        act = line(x - 1, -1, 18)
        pre = act * (lanes(p, 1) + from_below(lanes(p, 0)) + from_above(lanes(p, 2)))
        pre = pre + firsts(x + 1, 1, 18).astype(F32)
        s = jax.nn.sigmoid(pre)
        if 1 <= x < 5:
            second[(x - 1) * Y * Z : x * Y * Z, :] = (pre * s)[Z : 17 * Z].astype(BF)
        u, a = (x + 1) // 2, (x + 1) % 2
        back = []
        for b in range(2):
            at = (u * 10 + 1 - b) * Z
            w = jnp.concatenate([wd_ref[4 * a + 2 * b], wd_ref[4 * a + 2 * b + 1]], axis=1)
            back.append(mm(ge[at : at + 9 * Z, :], w, NT))
        g = jnp.concatenate(
            [back[1 - y % 2][y // 2 * Z : (y // 2 + 1) * Z] for y in range(18)], axis=0
        )
        g = (act * g * (s * (1.0 + pre * (1.0 - s)))).astype(BF)
        g2[x * 18 * Z : (x + 1) * 18 * Z, :] = g
        if 1 <= x < 5:
            put_z_taps(x - 1, g[Z : 17 * Z].astype(F32))

    def corner(a, b):
        return jnp.concatenate(
            [
                second[((2 * u + a) * Y + 2 * v + b) * Z : ((2 * u + a) * Y + 2 * v + b + 1) * Z, :]
                for u in range(2)
                for v in range(8)
            ],
            axis=0,
        )

    corners = [corner(a, b) for a in range(2) for b in range(2)]
    wd = jnp.concatenate(
        [jnp.concatenate([wd_ref[2 * q], wd_ref[2 * q + 1]], axis=1) for q in range(4)], axis=0
    )
    p = mm(jnp.concatenate(corners, axis=1), wd)
    coarse = (lanes(p, 0) + from_above(lanes(p, 1))).astype(BF)
    row, col = iota((128, 256), 0), iota((128, 256), 1)
    a, by, b, z = col // 128, col // 32 % 4, col // 16 % 2, col % Z
    order = (row // 16 == 4 * a + 2 * b + z // 2 % 2) & (row % 16 == by * 4 + z // 4) & (z % 2 == 0)
    bricks = mm(one(order), coarse).astype(BF)
    place = jnp.concatenate([place_ref[...].astype(F32)] * 8, axis=0)
    place = jnp.concatenate([place] * 2, axis=1)
    target = (8 * (col // 16) + col % 2).astype(F32)
    out_ref[...] = mm(one((place == target) & (row // 16 == col // 2 % 8)), bricks, TN).astype(BF)

    gec = jnp.concatenate([ge[(u * 10 + 1) * Z : (u * 10 + 9) * Z, :] for u in (1, 2)], axis=0)

    def put_a(at, v):
        grads_ref[core, at : at + v.shape[0], :] = v

    def put_b(at, v):
        grads_ref[1 - core, at : at + v.shape[0], :] = v

    for q in range(4):
        r = mm(corners[q], gec, TN).astype(BF)
        for c in range(2):
            t = 2 * q + c
            if t == 0:
                put_a(27 * C, lanes(r, c))
            else:
                put_b(27 * CIN + (t - 1) * C, lanes(r, c))
    put_b(27 * CIN + 7 * C, jnp.zeros((HALF - 27 * CIN - 7 * C, C), BF))
    weight_grad(firsts, 1, 1, C, lambda t, v: put_a(t * C, v))

    for x in range(X):
        p = taps(cots, x, Y, back_ref, NT, flip=True)
        g = lanes(p, 1) + from_above(lanes(p, 0)) + from_below(lanes(p, 2))
        g = g + cots(x + 1, 1, Y).astype(F32)
        g = (g * sg1[x * Y * Z : (x + 1) * Y * Z, :]).astype(BF)
        put_z_taps(x, g.astype(F32))
    weight_grad(cells, 2, 2, CIN, lambda t, v: put_b(t * CIN, v))


VM = pl.BlockSpec(memory_space=pltpu.VMEM)


def call(kernel, outs, args, in_specs=None, scratch=(), flops=10_000_000, vmem=40 << 20, out_specs=None, aliases={}):
    return pl.pallas_call(
        kernel,
        out_shape=tuple(jax.ShapeDtypeStruct(shape, dtype) for shape, dtype in outs),
        in_specs=in_specs or [VM] * len(args),
        out_specs=tuple(out_specs or [VM] * len(outs)),
        input_output_aliases=aliases,
        scratch_shapes=[pltpu.VMEM(*s) if isinstance(s, tuple) else s for s in scratch],
        compiler_params=pltpu.CompilerParams(vmem_limit_bytes=vmem),
        cost_estimate=pl.CostEstimate(
            flops=flops, bytes_accessed=1_000_000, transcendentals=0
        ),
    )(*args)


def arrange(w1_ref, w2_ref, after_ref, first_ref, second_ref, back_ref):
    for m in range(9):
        for k in range(3):
            first_ref[m * C : m * C + CIN, k * C : (k + 1) * C] = w1_ref[3 * m + k]
            second_ref[m * C : (m + 1) * C, k * C : (k + 1) * C] = w2_ref[3 * m + k]
            back_ref[k * C : (k + 1) * C, m * C : (m + 1) * C] = w2_ref[3 * m + k]
        first_ref[m * C + CIN : (m + 1) * C, :] = jnp.zeros((C - CIN, 3 * C), BF)


def begin(mid_ref, first_ref, part_ref):
    def cells(x, y, n):
        return mid_ref[((x - 3) * 22 + y) * Z : ((x - 3) * 22 + y + n) * Z, :]

    for x in range(1, 7):
        p = taps(cells, x, 20, first_ref, lines=[i for i in range(3) if 3 <= x + i < 7])
        part_ref[x - 1] = lanes(p, 1) + from_below(lanes(p, 0)) + from_above(lanes(p, 2))


def prepare(
    grad_hbm, feat_hbm, blocks_hbm, owners_hbm, rows_ref, own_ref, near_ref, far_ref,
    wide, grad_ref, feat_ref, blocks_ref, owners_ref, sems,
):
    copies = [
        pltpu.make_async_copy(a, b, sems.at[n])
        for n, (a, b) in enumerate(
            ((grad_hbm, grad_ref), (feat_hbm, feat_ref), (blocks_hbm, blocks_ref), (owners_hbm, owners_ref))
        )
    ]
    for c in copies:
        c.start()
    copies[0].wait()
    row, col = iota((128, 32), 0), iota((128, 32), 1)
    take = one((col == 2 * (row // 8) - 2 + row % 8) & (row % 8 < 6))
    rows_ref[...] = mm(take, grad_ref[0, 0]).astype(BF)
    for c in copies[1:]:
        c.wait()
    lane = iota((Y, C), 1)
    for x in range(X):
        f = feat_ref[x].astype(F32)
        f = jnp.concatenate([f, jnp.zeros((Y, C), F32)], axis=1)
        for z in range(Z):
            t = jnp.where(lane < CIN, f[:, z * CIN : z * CIN + C], 0.0)
            wide[pl.ds(x * Y * Z + z, Y, stride=Z), :] = t
    blocks = blocks_ref[0].astype(F32)
    mine = iota((Z, 4), 0) // 4 == iota((Z, 4), 1)
    for by in range(4):
        m = jnp.sum(jnp.where(mine, blocks[by : by + 1, :], 0.0), axis=1, keepdims=True)
        m = jnp.broadcast_to(m, (Z, C))
        own_ref[OWN + by * Z : OWN + (by + 1) * Z, :] = m.astype(BF)
        for x in range(X):
            for y in range(4 * by, 4 * by + 4):
                at = (x * Y + y) * Z
                own_ref[at : at + Z, :] = (wide[at : at + Z, :] * m).astype(BF)
    row, col = iota((16, 16), 0), iota((16, 16), 1)
    across = jnp.broadcast_to(owners_ref[...].astype(F32), (16, 16))
    dest = jnp.sum(jnp.where(row == col, across, 0.0), axis=1, keepdims=True)
    rank = jnp.sum(jnp.where((col < row) & (dest == across), 1.0, 0.0), axis=1, keepdims=True)
    place = jnp.broadcast_to(dest * 8.0 + rank, (16, C)).astype(BF)
    own_ref[OWN + 4 * Z : OWN + 5 * Z, :] = place

    def fill(up, down):
        for x in range(X):
            up[x * 3 * Z : (x + 1) * 3 * Z, :] = own_ref[(x * Y + 13) * Z : (x + 1) * Y * Z, :]
            down[x * 3 * Z : (x + 1) * 3 * Z, :] = own_ref[x * Y * Z : (x * Y + 3) * Z, :]
        for ref, by in ((up, 3), (down, 0)):
            ref[192:208, :] = place
            ref[208:224, :] = own_ref[OWN + by * Z : OWN + (by + 1) * Z, :]

    @pl.when(lax.rem(lax.axis_index("x"), 2) == 0)
    def _():
        fill(near_ref, far_ref)

    @pl.when(lax.rem(lax.axis_index("x"), 2) == 1)
    def _():
        fill(far_ref, near_ref)


def widen(
    own_ref, beside_ref, beyond_ref, rows_ref, after_ref,
    mid_ref, mask_ref, gc_ref, place_ref, near_ref, far_ref,
    sides,
):
    odd = lax.rem(lax.axis_index("x"), 2)
    sides[1 - odd] = beside_ref[...]
    sides[odd] = beyond_ref[...]
    low_ref, high_ref = sides.at[0], sides.at[1]
    for x in range(X):
        at = x * 22 * Z
        mid_ref[at : at + 3 * Z, :] = low_ref[x * 3 * Z : (x + 1) * 3 * Z, :]
        mid_ref[at + 3 * Z : at + 19 * Z, :] = own_ref[x * Y * Z : (x + 1) * Y * Z, :]
        mid_ref[at + 19 * Z : at + 22 * Z, :] = high_ref[x * 3 * Z : (x + 1) * 3 * Z, :]
    mask_ref[0:Z, :] = low_ref[208:224, :]
    mask_ref[Z : 5 * Z, :] = own_ref[OWN : OWN + 4 * Z, :]
    mask_ref[5 * Z : 6 * Z, :] = high_ref[208:224, :]
    place_ref[...] = own_ref[OWN + 4 * Z : OWN + 5 * Z, :]
    place = jnp.concatenate(
        [
            low_ref[192:208, :].astype(F32),
            own_ref[OWN + 4 * Z : OWN + 5 * Z, :].astype(F32) + 2.0,
            high_ref[192:208, :].astype(F32) + 4.0,
        ],
        axis=0,
    )
    bricks = mm(one(place == iota((48, C), 1).astype(F32)), rows_ref[...]).astype(BF)
    for q in range(8):
        gc_ref[q // 4, q % 4] = lanes(bricks, q)

    def fill(up, down):
        for q in range(4):
            up[COTS + q * 48 : COTS + (q + 1) * 48, :] = lanes(bricks, 4 + q)
            down[COTS + q * 48 : COTS + (q + 1) * 48, :] = lanes(bricks, q)
        up[0:COTS, :] = mid_ref[22 * Z :, :]
        down[0:COTS, :] = mid_ref[0:COTS, :]
        for ref in (up, down):
            ref[MASK : MASK + 96, :] = mask_ref[...]

    @pl.when(lax.axis_index("c") == 0)
    def _():
        fill(near_ref, far_ref)

    @pl.when(lax.axis_index("c") == 1)
    def _():
        fill(far_ref, near_ref)


def unfold(half_ref, core, first_hbm, second_hbm, down_hbm, wide, sems):
    spans = {
        0: ((0, 27 * C, second_hbm, 0), (27 * C, 28 * C, down_hbm, 0)),
        1: ((0, 27 * CIN, first_hbm, 0), (27 * CIN, 27 * CIN + 7 * C, down_hbm, C)),
    }

    def emit(which):
        copies = []
        for lo, hi, out, to in spans[which]:
            step = 864 if hi - lo > 1024 else hi - lo
            for at in range(lo, hi, step):
                wide[at : at + step, :] = half_ref[at : at + step, :].astype(F32)
                copies.append(
                    pltpu.make_async_copy(
                        wide.at[pl.ds(at, step)],
                        out.at[pl.ds(to + at - lo, step)],
                        sems.at[len(copies)],
                    )
                )
                copies[-1].start()
        for c in copies:
            c.wait()

    for which in range(2):
        pl.when(core == which)(functools.partial(emit, which))


def unfold_own(half_ref, first_hbm, second_hbm, down_hbm, wide, sems):
    unfold(half_ref, lax.axis_index("c"), first_hbm, second_hbm, down_hbm, wide, sems)


def unfold_other(half_ref, a, b, c, first_hbm, second_hbm, down_hbm, wide, sems):
    unfold(half_ref, 1 - lax.axis_index("c"), first_hbm, second_hbm, down_hbm, wide, sems)


def swap(v, axes, first):
    n = lax.axis_size(axes)
    pairs = [(i, i + 1) for i in range(first, n - 1, 2)]
    return lax.ppermute(v, axes, pairs + [(j, i) for i, j in pairs])


def swap_cores(v):
    return lax.ppermute(v, "c", [(0, 1), (1, 0)])


def up_matrix():
    m = np.zeros((6 * Z, 96), np.float32)
    for by in range(6):
        for z in range(Z):
            m[by * Z + z, z // 2 % 2 * 48 + (12, 16, 20, 24, 28, 32)[by] + z // 4] = 1
    return jnp.asarray(m, BF)


def flip(v, axis, bits):
    return lax.ppermute(v, axis, [(i, i ^ bits) for i in range(lax.axis_size(axis))])


def per_device(features, block_mask, weight_first, weight_second, weight_down, owners, moved_grad):
    rows, own, beside, beyond = call(
        prepare,
        [((128, 8 * C), BF), ((X * Y * Z + 80, C), BF), ((224, C), BF), ((224, C), BF)],
        (moved_grad, features, block_mask, owners.reshape(1, 16)),
        [pl.BlockSpec(memory_space=pltpu.HBM)] * 4,
        [
            ((X * Y * Z, C), F32),
            (moved_grad.shape, BF),
            (features.shape, BF),
            (block_mask.shape, jnp.int32),
            ((1, 16), jnp.int32),
            pltpu.SemaphoreType.DMA((4,)),
        ],
        vmem=60 << 20,
    )
    beyond, beside = swap(beyond, GY, 1), swap(beside, GY, 0)
    w1, w2, back = call(
        arrange,
        [((9 * C, 3 * C), BF), ((9 * C, 3 * C), BF), ((3 * C, 9 * C), BF)],
        (weight_first, weight_second, own),
        flops=2_000_000_000,
    )
    rows = lax.all_to_all(rows, GY, 0, 0, tiled=True)

    mid, mask, gc, place, near, far = call(
        widen,
        [((4 * 22 * Z, C), BF), ((96, C), BF), ((2, 4, 48, C), BF), ((16, C), BF), ((STRIP, C), BF), ((STRIP, C), BF)],
        (own, beside, beyond, rows, w1),
        [VM] * 4 + [pl.BlockSpec(memory_space=pl.ANY)],
        scratch=[((2, 224, C), BF)],
    )
    far, near = swap(far, GX, 1), swap(near, GX, 0)
    (ahead,) = call(begin, [((6, 20 * Z, C), F32)], (mid, w1), flops=2_000_000_000)

    grads, outgoing = call(
        section,
        [((2, HALF, C), BF), ((256, C), BF)],
        (near, mid, far, mask, gc, place, ahead, w1, w2, back, weight_down, up_matrix()),
        scratch=[
            ((2, STRIP, C), BF),
            ((8 * 20 * Z, C), BF),
            ((X * Y * Z, C), F32),
            ((X * Y * Z, C), BF),
            ((40 * Z, 2 * C), BF),
            ((6 * 18 * Z, C), BF),
            ((X * Y * Z, 3 * C), BF),
            ((3 * C, 6 * Y * Z), BF),
        ],
        flops=8_000_000_000,
    )

    theirs = swap_cores(grads[1])
    half = (grads[0].astype(F32) + theirs.astype(F32)).astype(BF)
    pieces = lax.all_to_all(
        jnp.concatenate([half.reshape(16, PART, C), outgoing.reshape(16, 16, C)], axis=1),
        GY, 0, 0, tiled=True,
    )
    moved = pieces[:, PART:].reshape(16, 8, 2, C).transpose(0, 2, 1, 3).reshape(1, 1, 32, 8 * C)
    part = jnp.sum(pieces[:, :PART].astype(F32), axis=0).astype(BF)
    others = [flip(part, "y", n).astype(F32) for n in (1, 2, 3)]
    part = ((part.astype(F32) + others[0]) + (others[1] + others[2])).astype(BF)
    part = lax.all_to_all(jnp.broadcast_to(part[None], (16, PART, C)), GY, 0, 0, tiled=True)
    part = part.reshape(HALF, C)
    grads = [((27 * CIN, C), F32), ((27 * C, C), F32), ((8 * C, C), F32)]
    scratch = [((HALF, C), F32), pltpu.SemaphoreType.DMA((5,))]
    hbm = pl.BlockSpec(memory_space=pl.ANY)
    other = swap_cores(part)
    grads_own = call(unfold_own, grads, (part,), [VM], scratch, out_specs=[hbm] * 3)
    grad_first, grad_second, grad_down = call(
        unfold_other, grads, (other, *grads_own), [VM] + [hbm] * 3, scratch, out_specs=[hbm] * 3,
        aliases={1: 0, 2: 1, 3: 2},
    )
    return (
        moved,
        grad_first.reshape(27, CIN, C),
        grad_second.reshape(27, C, C),
        grad_down.reshape(8, C, C),
    )


def solution(mesh):
    shape = dict(mesh.shape)
    fine = Mesh(
        mesh.devices.reshape(shape["gx"] // 2, 2, 4, shape["gy"] // 4), ("y", "c", "z", "x")
    )
    whole, tiles = P(GX, GY, None), P(GX, GY, None, None)
    return jax.shard_map(
        per_device,
        mesh=fine,
        in_specs=(whole, whole, P(), P(), P(), tiles, tiles),
        out_specs=(tiles, P(), P(), P()),
        check_vma=False,
    )
```

```python
import functools

import jax
import jax.numpy as jnp
import numpy as np
from jax import lax
from jax.experimental import pallas as pl
from jax.experimental.pallas import tpu as pltpu
from jax.sharding import Mesh, PartitionSpec as P

GX, GY = ("y", "c"), ("z", "x")
F32, BF = jnp.float32, jnp.bfloat16
X, Y, Z, C, CIN = 4, 16, 16, 128, 96
HALF, PART = 3584, 224
OWN = 1024
COTS, MASK, STRIP = 1056, 1184, 1200
EARLY = {1: 0, 2: 1, 5: 2, 6: 3}
NN = (((1,), (0,)), ((), ()))
NT = (((1,), (1,)), ((), ()))
TN = (((0,), (0,)), ((), ()))


def mm(a, b, dims=NN):
    return lax.dot_general(a, b, dims, preferred_element_type=F32)


def iota(shape, axis):
    return lax.broadcasted_iota(jnp.int32, shape, axis)


def one(where):
    return jnp.where(where, 1.0, 0.0).astype(BF)


def z_of(rows):
    return iota((rows, C), 0) % Z


def from_above(v):
    return jnp.where(z_of(v.shape[0]) < Z - 1, pltpu.roll(v, v.shape[0] - 1, 0), 0.0)


def from_below(v):
    return jnp.where(z_of(v.shape[0]) > 0, pltpu.roll(v, 1, 0), 0.0)


def lanes(p, k):
    return p[:, k * C : (k + 1) * C]


def silu(v):
    s = jax.nn.sigmoid(v)
    return v * s, s * (1.0 + v * (1.0 - s))


def spread(packed, by):
    return jnp.broadcast_to(packed[:, 16 * by : 16 * by + 1].astype(F32), (Z, C))


def taps(get, x, n, w, dims=NN, flip=False, lines=(0, 1, 2)):
    wins = []
    for i in lines:
        for j in range(3):
            wins.append(get(x + 2 - i, 2 - j, n) if flip else get(x + i, j, n))
    if len(lines) < 3:
        w = w[3 * lines[0] * C : 3 * (lines[-1] + 1) * C, :]
    else:
        w = w[...]
    return mm(jnp.concatenate(wins, axis=1), w, dims)


def section(
    near_ref, mid_ref, far_ref, mask_ref, gc_ref, place_ref, part1_ref, inner_ref, slope_ref, part2_ref, w1_ref, w2_ref, back_ref, wd_ref, up_ref,
    grads_ref, out_ref,
    sides, first, sg1, second, ge, g2, gs, vt,
):
    core = lax.axis_index("c")
    sides[1 - core] = near_ref[...]
    sides[core] = far_ref[...]
    low_ref, high_ref = sides.at[0], sides.at[1]

    def cells(x, y, n):
        ref, x = ((low_ref, x), (mid_ref, x - 3), (high_ref, x - 7))[(x > 2) + (x > 6)]
        return ref[(x * 22 + y) * Z : (x * 22 + y + n) * Z, :]

    def firsts(x, y, n):
        return first[(x * 20 + y) * Z : (x * 20 + y + n) * Z, :]

    def cots(x, y, n):
        return g2[(x * 18 + y) * Z : (x * 18 + y + n) * Z, :]

    packed = low_ref[MASK:, :], mask_ref[...], high_ref[MASK:, :]
    masks = [[spread(t, by) for by in range(6)] for t in packed]

    def cotangent(u, q):
        if u in (1, 2):
            return gc_ref[u - 1, q]
        return (low_ref if u == 0 else high_ref)[COTS + q * 32 : COTS + (q + 1) * 32, :]

    def line(x, y0, cells):
        return jnp.concatenate(
            [masks[(x + 4) // 4][(y + 4) // 4] for y in range(y0, y0 + cells)], axis=0
        )

    def weight_grad(get, x0, y0, rows, put):
        for j in range(3):
            for x in range(6):
                vt[j * C : (j + 1) * C, x * Y * Z : (x + 1) * Y * Z] = get(x0 + x, y0 + j, Y).T
        for i in range(3):
            p = mm(vt[:, i * Y * Z : (i + X) * Y * Z], gs[...]).astype(BF)
            for j in range(3):
                for k in range(3):
                    put(9 * i + 3 * j + k, p[j * C : j * C + rows, k * C : (k + 1) * C])

    def put_z_taps(x, g):
        at = x * Y * Z
        gs[at : at + Y * Z, 0:C] = from_above(g).astype(BF)
        gs[at : at + Y * Z, C : 2 * C] = g.astype(BF)
        gs[at : at + Y * Z, 2 * C : 3 * C] = from_below(g).astype(BF)

    first[3 * 20 * Z : 5 * 20 * Z, :] = inner_ref[...]
    sg1[Y * Z : 3 * Y * Z, :] = slope_ref[...]
    for x in (0, 1, 2, 5, 6, 7):
        p = taps(cells, x, 20, w1_ref, lines=[i for i in range(3) if not 3 <= x + i < 7])
        pre = lanes(p, 1) + from_below(lanes(p, 0)) + from_above(lanes(p, 2))
        if x in EARLY:
            pre = pre + part1_ref[EARLY[x]]
        act = line(x - 2, -2, 20)
        value, slope = silu(act * pre)
        first[x * 20 * Z : (x + 1) * 20 * Z, :] = value.astype(BF)
        if x in (2, 5):
            sg1[(x - 2) * Y * Z : (x - 1) * Y * Z, :] = (act * slope)[2 * Z : 18 * Z]

    even = z_of(6 * Z) % 2 == 0
    for u in range(4):
        both = jnp.concatenate(
            [jnp.concatenate([cotangent(u, 2 * b + c) for b in range(2)], axis=1) for c in range(2)],
            axis=0,
        )
        r = mm(up_ref[...], both)
        for v in range(10):
            by, b = (v + 1) // 2, (v + 1) % 2
            t = r[by * Z : (by + 1) * Z, b * C : (b + 1) * C]
            at = (u * 10 + v) * Z
            ge[at : at + Z, 0:C] = jnp.where(even[:Z], t, 0.0).astype(BF)
            ge[at : at + Z, C : 2 * C] = jnp.where(even[:Z], 0.0, t).astype(BF)

    for x in range(6):
        p = taps(firsts, x, 18, w2_ref, lines=[i for i in range(3) if not 3 <= x + i < 5])
        act = line(x - 1, -1, 18)
        pre = lanes(p, 1) + from_below(lanes(p, 0)) + from_above(lanes(p, 2))
        if 1 <= x < 5:
            pre = pre + part2_ref[x - 1]
        value, slope = silu(act * pre + firsts(x + 1, 1, 18).astype(F32))
        if 1 <= x < 5:
            second[(x - 1) * Y * Z : x * Y * Z, :] = value[Z : 17 * Z].astype(BF)
        u, a = (x + 1) // 2, (x + 1) % 2
        back = []
        for b in range(2):
            at = (u * 10 + 1 - b) * Z
            w = jnp.concatenate([wd_ref[4 * a + 2 * b], wd_ref[4 * a + 2 * b + 1]], axis=1)
            back.append(mm(ge[at : at + 9 * Z, :], w, NT))
        g = jnp.concatenate(
            [back[1 - y % 2][y // 2 * Z : (y // 2 + 1) * Z] for y in range(18)], axis=0
        )
        g = (act * g * slope).astype(BF)
        g2[x * 18 * Z : (x + 1) * 18 * Z, :] = g
        if 1 <= x < 5:
            put_z_taps(x - 1, g[Z : 17 * Z].astype(F32))

    def corner(a, b):
        return jnp.concatenate(
            [
                second[((2 * u + a) * Y + 2 * v + b) * Z : ((2 * u + a) * Y + 2 * v + b + 1) * Z, :]
                for u in range(2)
                for v in range(8)
            ],
            axis=0,
        )

    corners = [corner(a, b) for a in range(2) for b in range(2)]
    wd = jnp.concatenate(
        [jnp.concatenate([wd_ref[2 * q], wd_ref[2 * q + 1]], axis=1) for q in range(4)], axis=0
    )
    p = mm(jnp.concatenate(corners, axis=1), wd)
    coarse = (lanes(p, 0) + from_above(lanes(p, 1))).astype(BF)
    row, col = iota((128, 256), 0), iota((128, 256), 1)
    a, by, b, z = col // 128, col // 32 % 4, col // 16 % 2, col % Z
    order = (row // 16 == 4 * a + 2 * b + z // 2 % 2) & (row % 16 == by * 4 + z // 4) & (z % 2 == 0)
    bricks = mm(one(order), coarse).astype(BF)
    place = jnp.concatenate([place_ref[...].astype(F32)] * 8, axis=0)
    place = jnp.concatenate([place] * 2, axis=1)
    target = (8 * (col // 16) + col % 2).astype(F32)
    out_ref[...] = mm(one((place == target) & (row // 16 == col // 2 % 8)), bricks, TN).astype(BF)

    gec = jnp.concatenate([ge[(u * 10 + 1) * Z : (u * 10 + 9) * Z, :] for u in (1, 2)], axis=0)

    def put_a(at, v):
        grads_ref[core, at : at + v.shape[0], :] = v

    def put_b(at, v):
        grads_ref[1 - core, at : at + v.shape[0], :] = v

    for q in range(4):
        r = mm(corners[q], gec, TN).astype(BF)
        for c in range(2):
            t = 2 * q + c
            if t == 0:
                put_a(27 * C, lanes(r, c))
            else:
                put_b(27 * CIN + (t - 1) * C, lanes(r, c))
    put_b(27 * CIN + 7 * C, jnp.zeros((HALF - 27 * CIN - 7 * C, C), BF))
    weight_grad(firsts, 1, 1, C, lambda t, v: put_a(t * C, v))

    for x in range(X):
        p = taps(cots, x, Y, back_ref, NT, flip=True)
        g = lanes(p, 1) + from_above(lanes(p, 0)) + from_below(lanes(p, 2))
        g = g + cots(x + 1, 1, Y).astype(F32)
        g = (g * sg1[x * Y * Z : (x + 1) * Y * Z, :]).astype(BF)
        put_z_taps(x, g.astype(F32))
    weight_grad(cells, 2, 2, CIN, lambda t, v: put_b(t * CIN, v))


VM = pl.BlockSpec(memory_space=pltpu.VMEM)


def call(kernel, outs, args, in_specs=None, scratch=(), flops=10_000_000, vmem=40 << 20, out_specs=None, aliases={}):
    return pl.pallas_call(
        kernel,
        out_shape=tuple(jax.ShapeDtypeStruct(shape, dtype) for shape, dtype in outs),
        in_specs=in_specs or [VM] * len(args),
        out_specs=tuple(out_specs or [VM] * len(outs)),
        input_output_aliases=aliases,
        scratch_shapes=[pltpu.VMEM(*s) if isinstance(s, tuple) else s for s in scratch],
        compiler_params=pltpu.CompilerParams(vmem_limit_bytes=vmem),
        cost_estimate=pl.CostEstimate(
            flops=flops, bytes_accessed=1_000_000, transcendentals=0
        ),
    )(*args)


def arrange(w1_ref, w2_ref, after_ref, first_ref, second_ref, back_ref):
    for m in range(9):
        for k in range(3):
            first_ref[m * C : m * C + CIN, k * C : (k + 1) * C] = w1_ref[3 * m + k]
            second_ref[m * C : (m + 1) * C, k * C : (k + 1) * C] = w2_ref[3 * m + k]
            back_ref[k * C : (k + 1) * C, m * C : (m + 1) * C] = w2_ref[3 * m + k]
        first_ref[m * C + CIN : (m + 1) * C, :] = jnp.zeros((C - CIN, 3 * C), BF)


def begin(mid_ref, mask_ref, w1_ref, w2_ref, part1_ref, first_ref, sg1_ref, part2_ref):
    def cells(x, y, n):
        return mid_ref[((x - 3) * 22 + y) * Z : ((x - 3) * 22 + y + n) * Z, :]

    def firsts(x, y, n):
        return first_ref[((x - 3) * 20 + y) * Z : ((x - 3) * 20 + y + n) * Z, :]

    masks = [spread(mask_ref[...], by) for by in range(6)]
    act = jnp.concatenate([masks[(y + 4) // 4] for y in range(-2, 18)], axis=0)
    for x in (3, 4, 1, 2, 5, 6):
        p = taps(cells, x, 20, w1_ref, lines=[i for i in range(3) if 3 <= x + i < 7])
        pre = lanes(p, 1) + from_below(lanes(p, 0)) + from_above(lanes(p, 2))
        if x in (3, 4):
            value, slope = silu(act * pre)
            first_ref[(x - 3) * 20 * Z : (x - 2) * 20 * Z, :] = value.astype(BF)
            sg1_ref[(x - 3) * Y * Z : (x - 2) * Y * Z, :] = (act * slope)[2 * Z : 18 * Z]
        else:
            part1_ref[EARLY[x]] = pre
    for x in range(1, 5):
        p = taps(firsts, x, 18, w2_ref, lines=[i for i in range(3) if 3 <= x + i < 5])
        part2_ref[x - 1] = lanes(p, 1) + from_below(lanes(p, 0)) + from_above(lanes(p, 2))


def prepare(
    grad_hbm, feat_hbm, blocks_hbm, owners_hbm, rows_ref, own_ref, near_ref, far_ref,
    wide, grad_ref, feat_ref, blocks_ref, owners_ref, sems,
):
    copies = [
        pltpu.make_async_copy(a, b, sems.at[n])
        for n, (a, b) in enumerate(
            ((grad_hbm, grad_ref), (feat_hbm, feat_ref), (blocks_hbm, blocks_ref), (owners_hbm, owners_ref))
        )
    ]
    for c in copies:
        c.start()
    copies[0].wait()
    row, col = iota((128, 32), 0), iota((128, 32), 1)
    take = one((col == 2 * (row // 8) - 2 + row % 8) & (row % 8 < 6))
    rows_ref[...] = mm(take, grad_ref[0, 0]).astype(BF)
    for c in copies[1:]:
        c.wait()
    lane = iota((Y, C), 1)
    for x in range(X):
        f = feat_ref[x].astype(F32)
        f = jnp.concatenate([f, jnp.zeros((Y, C), F32)], axis=1)
        for z in range(Z):
            t = jnp.where(lane < CIN, f[:, z * CIN : z * CIN + C], 0.0)
            wide[pl.ds(x * Y * Z + z, Y, stride=Z), :] = t
    blocks = blocks_ref[0].astype(F32)
    mine = iota((Z, 4), 0) // 4 == iota((Z, 4), 1)
    for by in range(4):
        m = jnp.sum(jnp.where(mine, blocks[by : by + 1, :], 0.0), axis=1, keepdims=True)
        m = jnp.broadcast_to(m, (Z, C))
        own_ref[OWN + by * Z : OWN + (by + 1) * Z, :] = m.astype(BF)
        for x in range(X):
            for y in range(4 * by, 4 * by + 4):
                at = (x * Y + y) * Z
                own_ref[at : at + Z, :] = (wide[at : at + Z, :] * m).astype(BF)
    row, col = iota((16, 16), 0), iota((16, 16), 1)
    across = jnp.broadcast_to(owners_ref[...].astype(F32), (16, 16))
    dest = jnp.sum(jnp.where(row == col, across, 0.0), axis=1, keepdims=True)
    rank = jnp.sum(jnp.where((col < row) & (dest == across), 1.0, 0.0), axis=1, keepdims=True)
    place = jnp.broadcast_to(dest * 8.0 + rank, (16, C)).astype(BF)
    own_ref[OWN + 4 * Z : OWN + 5 * Z, :] = place

    def fill(up, down):
        for x in range(X):
            up[x * 3 * Z : (x + 1) * 3 * Z, :] = own_ref[(x * Y + 13) * Z : (x + 1) * Y * Z, :]
            down[x * 3 * Z : (x + 1) * 3 * Z, :] = own_ref[x * Y * Z : (x * Y + 3) * Z, :]
        for ref, by in ((up, 3), (down, 0)):
            ref[192:208, :] = place
            ref[208:224, :] = own_ref[OWN + by * Z : OWN + (by + 1) * Z, :]

    @pl.when(lax.rem(lax.axis_index("x"), 2) == 0)
    def _():
        fill(near_ref, far_ref)

    @pl.when(lax.rem(lax.axis_index("x"), 2) == 1)
    def _():
        fill(far_ref, near_ref)


def widen(
    own_ref, beside_ref, beyond_ref, rows_ref, after_ref,
    mid_ref, mask_ref, gc_ref, place_ref, near_ref, far_ref,
    sides,
):
    odd = lax.rem(lax.axis_index("x"), 2)
    sides[1 - odd] = beside_ref[...]
    sides[odd] = beyond_ref[...]
    low_ref, high_ref = sides.at[0], sides.at[1]
    for x in range(X):
        at = x * 22 * Z
        mid_ref[at : at + 3 * Z, :] = low_ref[x * 3 * Z : (x + 1) * 3 * Z, :]
        mid_ref[at + 3 * Z : at + 19 * Z, :] = own_ref[x * Y * Z : (x + 1) * Y * Z, :]
        mid_ref[at + 19 * Z : at + 22 * Z, :] = high_ref[x * 3 * Z : (x + 1) * 3 * Z, :]
    tiles = [low_ref[208:224, :]]
    tiles += [own_ref[OWN + by * Z : OWN + (by + 1) * Z, :] for by in range(4)]
    tiles += [high_ref[208:224, :]]
    which = iota((Z, C), 1) // 16
    packed = jnp.zeros((Z, C), F32)
    for by in range(6):
        packed = jnp.where(which == by, tiles[by].astype(F32), packed)
    mask_ref[...] = packed.astype(BF)
    place_ref[...] = own_ref[OWN + 4 * Z : OWN + 5 * Z, :]
    place = jnp.concatenate(
        [
            low_ref[192:208, :].astype(F32),
            own_ref[OWN + 4 * Z : OWN + 5 * Z, :].astype(F32) + 2.0,
            high_ref[192:208, :].astype(F32) + 4.0,
        ],
        axis=0,
    )
    bricks = mm(one(place == iota((48, C), 1).astype(F32)), rows_ref[...])[12:44].astype(BF)
    for q in range(8):
        gc_ref[q // 4, q % 4] = lanes(bricks, q)

    def fill(up, down):
        for q in range(4):
            up[COTS + q * 32 : COTS + (q + 1) * 32, :] = lanes(bricks, 4 + q)
            down[COTS + q * 32 : COTS + (q + 1) * 32, :] = lanes(bricks, q)
        up[0:COTS, :] = mid_ref[22 * Z :, :]
        down[0:COTS, :] = mid_ref[0:COTS, :]
        for ref in (up, down):
            ref[MASK:, :] = mask_ref[...]

    @pl.when(lax.axis_index("c") == 0)
    def _():
        fill(near_ref, far_ref)

    @pl.when(lax.axis_index("c") == 1)
    def _():
        fill(far_ref, near_ref)


def unfold(half_ref, core, first_hbm, second_hbm, down_hbm, wide, sems):
    spans = {
        0: ((0, 27 * C, second_hbm, 0), (27 * C, 28 * C, down_hbm, 0)),
        1: ((0, 27 * CIN, first_hbm, 0), (27 * CIN, 27 * CIN + 7 * C, down_hbm, C)),
    }

    def emit(which):
        copies = []
        for lo, hi, out, to in spans[which]:
            step = 864 if hi - lo > 1024 else hi - lo
            for at in range(lo, hi, step):
                wide[at : at + step, :] = half_ref[at : at + step, :].astype(F32)
                copies.append(
                    pltpu.make_async_copy(
                        wide.at[pl.ds(at, step)],
                        out.at[pl.ds(to + at - lo, step)],
                        sems.at[len(copies)],
                    )
                )
                copies[-1].start()
        for c in copies:
            c.wait()

    for which in range(2):
        pl.when(core == which)(functools.partial(emit, which))


def unfold_own(half_ref, first_hbm, second_hbm, down_hbm, wide, sems):
    unfold(half_ref, lax.axis_index("c"), first_hbm, second_hbm, down_hbm, wide, sems)


def unfold_other(half_ref, a, b, c, first_hbm, second_hbm, down_hbm, wide, sems):
    unfold(half_ref, 1 - lax.axis_index("c"), first_hbm, second_hbm, down_hbm, wide, sems)


def swap(v, axes, first):
    n = lax.axis_size(axes)
    pairs = [(i, i + 1) for i in range(first, n - 1, 2)]
    return lax.ppermute(v, axes, pairs + [(j, i) for i, j in pairs])


def swap_cores(v):
    return lax.ppermute(v, "c", [(0, 1), (1, 0)])


def up_matrix():
    m = np.zeros((6 * Z, 64), np.float32)
    for by in range(6):
        for z in range(Z):
            m[by * Z + z, z // 2 % 2 * 32 + by * 4 + z // 4] = 1
    return jnp.asarray(m, BF)


def flip(v, axis, bits):
    return lax.ppermute(v, axis, [(i, i ^ bits) for i in range(lax.axis_size(axis))])


def per_device(features, block_mask, weight_first, weight_second, weight_down, owners, moved_grad):
    rows, own, beside, beyond = call(
        prepare,
        [((128, 8 * C), BF), ((X * Y * Z + 80, C), BF), ((224, C), BF), ((224, C), BF)],
        (moved_grad, features, block_mask, owners.reshape(1, 16)),
        [pl.BlockSpec(memory_space=pltpu.HBM)] * 4,
        [
            ((X * Y * Z, C), F32),
            (moved_grad.shape, BF),
            (features.shape, BF),
            (block_mask.shape, jnp.int32),
            ((1, 16), jnp.int32),
            pltpu.SemaphoreType.DMA((4,)),
        ],
        vmem=60 << 20,
    )
    beyond, beside = swap(beyond, GY, 1), swap(beside, GY, 0)
    w1, w2, back = call(
        arrange,
        [((9 * C, 3 * C), BF), ((9 * C, 3 * C), BF), ((3 * C, 9 * C), BF)],
        (weight_first, weight_second, own),
        flops=2_000_000_000,
    )
    rows = lax.all_to_all(rows, GY, 0, 0, tiled=True)

    mid, mask, gc, place, near, far = call(
        widen,
        [((4 * 22 * Z, C), BF), ((16, C), BF), ((2, 4, 32, C), BF), ((16, C), BF), ((STRIP, C), BF), ((STRIP, C), BF)],
        (own, beside, beyond, rows, w1),
        [VM] * 4 + [pl.BlockSpec(memory_space=pl.ANY)],
        scratch=[((2, 224, C), BF)],
    )
    far, near = swap(far, GX, 1), swap(near, GX, 0)
    ahead = call(
        begin,
        [((4, 20 * Z, C), F32), ((40 * Z, C), BF), ((2 * Y * Z, C), F32), ((4, 18 * Z, C), F32)],
        (mid, mask, w1, w2),
        flops=3_000_000_000,
    )

    grads, outgoing = call(
        section,
        [((2, HALF, C), BF), ((256, C), BF)],
        (near, mid, far, mask, gc, place, *ahead, w1, w2, back, weight_down, up_matrix()),
        scratch=[
            ((2, STRIP, C), BF),
            ((8 * 20 * Z, C), BF),
            ((X * Y * Z, C), F32),
            ((X * Y * Z, C), BF),
            ((40 * Z, 2 * C), BF),
            ((6 * 18 * Z, C), BF),
            ((X * Y * Z, 3 * C), BF),
            ((3 * C, 6 * Y * Z), BF),
        ],
        flops=8_000_000_000,
    )

    theirs = swap_cores(grads[1])
    half = (grads[0].astype(F32) + theirs.astype(F32)).astype(BF)
    pieces = lax.all_to_all(
        jnp.concatenate([half.reshape(16, PART, C), outgoing.reshape(16, 16, C)], axis=1),
        GY, 0, 0, tiled=True,
    )
    moved = pieces[:, PART:].reshape(16, 8, 2, C).transpose(0, 2, 1, 3).reshape(1, 1, 32, 8 * C)
    part = jnp.sum(pieces[:, :PART].astype(F32), axis=0).astype(BF)
    others = [flip(part, "y", n).astype(F32) for n in (1, 2, 3)]
    part = ((part.astype(F32) + others[0]) + (others[1] + others[2])).astype(BF)
    part = lax.all_to_all(jnp.broadcast_to(part[None], (16, PART, C)), GY, 0, 0, tiled=True)
    part = part.reshape(HALF, C)
    grads = [((27 * CIN, C), F32), ((27 * C, C), F32), ((8 * C, C), F32)]
    scratch = [((HALF, C), F32), pltpu.SemaphoreType.DMA((5,))]
    hbm = pl.BlockSpec(memory_space=pl.ANY)
    other = swap_cores(part)
    grads_own = call(unfold_own, grads, (part,), [VM], scratch, out_specs=[hbm] * 3)
    grad_first, grad_second, grad_down = call(
        unfold_other, grads, (other, *grads_own), [VM] + [hbm] * 3, scratch, out_specs=[hbm] * 3,
        aliases={1: 0, 2: 1, 3: 2},
    )
    return (
        moved,
        grad_first.reshape(27, CIN, C),
        grad_second.reshape(27, C, C),
        grad_down.reshape(8, C, C),
    )


def solution(mesh):
    shape = dict(mesh.shape)
    fine = Mesh(
        mesh.devices.reshape(shape["gx"] // 2, 2, 4, shape["gy"] // 4), ("y", "c", "z", "x")
    )
    whole, tiles = P(GX, GY, None), P(GX, GY, None, None)
    return jax.shard_map(
        per_device,
        mesh=fine,
        in_specs=(whole, whole, P(), P(), P(), tiles, tiles),
        out_specs=(tiles, P(), P(), P()),
        check_vma=False,
    )
```

```python
import functools

import jax
import jax.numpy as jnp
import numpy as np
from jax import lax
from jax.experimental import pallas as pl
from jax.experimental.pallas import tpu as pltpu
from jax.sharding import Mesh, PartitionSpec as P

GX, GY = ("y", "c"), ("z", "x")
F32, BF = jnp.float32, jnp.bfloat16
X, Y, Z, C, CIN = 4, 16, 16, 128, 96
HALF, PART = 3584, 224
OWN = 1024
COTS, MASK, STRIP = 1056, 1184, 1200
EARLY = {1: 0, 2: 1, 5: 2, 6: 3}
NN = (((1,), (0,)), ((), ()))
NT = (((1,), (1,)), ((), ()))
TN = (((0,), (0,)), ((), ()))


def mm(a, b, dims=NN):
    return lax.dot_general(a, b, dims, preferred_element_type=F32)


def iota(shape, axis):
    return lax.broadcasted_iota(jnp.int32, shape, axis)


def one(where):
    return jnp.where(where, 1.0, 0.0).astype(BF)


def z_of(rows):
    return iota((rows, C), 0) % Z


def from_above(v):
    return jnp.where(z_of(v.shape[0]) < Z - 1, pltpu.roll(v, v.shape[0] - 1, 0), 0.0)


def from_below(v):
    return jnp.where(z_of(v.shape[0]) > 0, pltpu.roll(v, 1, 0), 0.0)


def lanes(p, k):
    return p[:, k * C : (k + 1) * C]


def silu(v):
    s = jax.nn.sigmoid(v)
    return v * s, s * (1.0 + v * (1.0 - s))


def spread(packed, by):
    return jnp.broadcast_to(packed[:, 16 * by : 16 * by + 1].astype(F32), (Z, C))


def taps(get, x, n, w, dims=NN, flip=False, lines=(0, 1, 2)):
    wins = []
    for i in lines:
        for j in range(3):
            wins.append(get(x + 2 - i, 2 - j, n) if flip else get(x + i, j, n))
    if len(lines) < 3:
        w = w[3 * lines[0] * C : 3 * (lines[-1] + 1) * C, :]
    else:
        w = w[...]
    return mm(jnp.concatenate(wins, axis=1), w, dims)


def section(
    near_ref, mid_ref, far_ref, mask_ref, gc_ref, place_ref, part1_ref, inner_ref, slope_ref, part2_ref, w1_ref, w2_ref, back_ref, wd_ref, up_ref,
    grads_ref, out_ref,
    sides, first, sg1, second, ge, g2, gs, vt,
):
    core = lax.axis_index("c")
    sides[1 - core] = near_ref[...]
    sides[core] = far_ref[...]
    low_ref, high_ref = sides.at[0], sides.at[1]

    def cells(x, y, n):
        ref, x = ((low_ref, x), (mid_ref, x - 3), (high_ref, x - 7))[(x > 2) + (x > 6)]
        return ref[(x * 22 + y) * Z : (x * 22 + y + n) * Z, :]

    def firsts(x, y, n):
        return first[(x * 20 + y) * Z : (x * 20 + y + n) * Z, :]

    def cots(x, y, n):
        return g2[(x * 18 + y) * Z : (x * 18 + y + n) * Z, :]

    packed = low_ref[MASK:, :], mask_ref[...], high_ref[MASK:, :]
    masks = [[spread(t, by) for by in range(6)] for t in packed]

    def cotangent(u, q):
        if u in (1, 2):
            return gc_ref[u - 1, q]
        return (low_ref if u == 0 else high_ref)[COTS + q * 32 : COTS + (q + 1) * 32, :]

    def line(x, y0, cells):
        return jnp.concatenate(
            [masks[(x + 4) // 4][(y + 4) // 4] for y in range(y0, y0 + cells)], axis=0
        )

    def weight_grad(get, x0, y0, rows, put):
        for j in range(3):
            for x in range(6):
                vt[j * C : (j + 1) * C, x * Y * Z : (x + 1) * Y * Z] = get(x0 + x, y0 + j, Y).T
        for i in range(3):
            p = mm(vt[:, i * Y * Z : (i + X) * Y * Z], gs[...]).astype(BF)
            for j in range(3):
                for k in range(3):
                    put(9 * i + 3 * j + k, p[j * C : j * C + rows, k * C : (k + 1) * C])

    def put_z_taps(x, g):
        at = x * Y * Z
        gs[at : at + Y * Z, 0:C] = from_above(g).astype(BF)
        gs[at : at + Y * Z, C : 2 * C] = g.astype(BF)
        gs[at : at + Y * Z, 2 * C : 3 * C] = from_below(g).astype(BF)

    first[3 * 20 * Z : 5 * 20 * Z, :] = inner_ref[...]
    sg1[Y * Z : 3 * Y * Z, :] = slope_ref[...]
    for x in (0, 1, 2, 5, 6, 7):
        p = taps(cells, x, 20, w1_ref, lines=[i for i in range(3) if not 3 <= x + i < 7])
        pre = lanes(p, 1) + from_below(lanes(p, 0)) + from_above(lanes(p, 2))
        if x in EARLY:
            pre = pre + part1_ref[EARLY[x]]
        act = line(x - 2, -2, 20)
        value, slope = silu(act * pre)
        first[x * 20 * Z : (x + 1) * 20 * Z, :] = value.astype(BF)
        if x in (2, 5):
            sg1[(x - 2) * Y * Z : (x - 1) * Y * Z, :] = (act * slope)[2 * Z : 18 * Z]

    even = z_of(6 * Z) % 2 == 0
    for u in range(4):
        both = jnp.concatenate(
            [jnp.concatenate([cotangent(u, 2 * b + c) for b in range(2)], axis=1) for c in range(2)],
            axis=0,
        )
        r = mm(up_ref[...], both)
        for v in range(10):
            by, b = (v + 1) // 2, (v + 1) % 2
            t = r[by * Z : (by + 1) * Z, b * C : (b + 1) * C]
            at = (u * 10 + v) * Z
            ge[at : at + Z, 0:C] = jnp.where(even[:Z], t, 0.0).astype(BF)
            ge[at : at + Z, C : 2 * C] = jnp.where(even[:Z], 0.0, t).astype(BF)

    for x in range(6):
        p = taps(firsts, x, 18, w2_ref, lines=[i for i in range(3) if not 3 <= x + i < 5])
        act = line(x - 1, -1, 18)
        pre = lanes(p, 1) + from_below(lanes(p, 0)) + from_above(lanes(p, 2))
        if 1 <= x < 5:
            pre = pre + part2_ref[x - 1]
        value, slope = silu(act * pre + firsts(x + 1, 1, 18).astype(F32))
        if 1 <= x < 5:
            second[(x - 1) * Y * Z : x * Y * Z, :] = value[Z : 17 * Z].astype(BF)
        u, a = (x + 1) // 2, (x + 1) % 2
        back = []
        for b in range(2):
            at = (u * 10 + 1 - b) * Z
            w = jnp.concatenate([wd_ref[4 * a + 2 * b], wd_ref[4 * a + 2 * b + 1]], axis=1)
            back.append(mm(ge[at : at + 9 * Z, :], w, NT))
        g = jnp.concatenate(
            [back[1 - y % 2][y // 2 * Z : (y // 2 + 1) * Z] for y in range(18)], axis=0
        )
        g = (act * g * slope).astype(BF)
        g2[x * 18 * Z : (x + 1) * 18 * Z, :] = g
        if 1 <= x < 5:
            put_z_taps(x - 1, g[Z : 17 * Z].astype(F32))

    def corner(a, b):
        return jnp.concatenate(
            [
                second[((2 * u + a) * Y + 2 * v + b) * Z : ((2 * u + a) * Y + 2 * v + b + 1) * Z, :]
                for u in range(2)
                for v in range(8)
            ],
            axis=0,
        )

    corners = [corner(a, b) for a in range(2) for b in range(2)]
    wd = jnp.concatenate(
        [jnp.concatenate([wd_ref[2 * q], wd_ref[2 * q + 1]], axis=1) for q in range(4)], axis=0
    )
    p = mm(jnp.concatenate(corners, axis=1), wd)
    coarse = (lanes(p, 0) + from_above(lanes(p, 1))).astype(BF)
    row, col = iota((128, 256), 0), iota((128, 256), 1)
    a, by, b, z = col // 128, col // 32 % 4, col // 16 % 2, col % Z
    order = (row // 16 == 4 * a + 2 * b + z // 2 % 2) & (row % 16 == by * 4 + z // 4) & (z % 2 == 0)
    bricks = mm(one(order), coarse).astype(BF)
    place = jnp.concatenate([place_ref[...].astype(F32)] * 8, axis=0)
    place = jnp.concatenate([place] * 2, axis=1)
    target = (8 * (col // 16) + col % 2).astype(F32)
    out_ref[...] = mm(one((place == target) & (row // 16 == col // 2 % 8)), bricks, TN).astype(BF)

    gec = jnp.concatenate([ge[(u * 10 + 1) * Z : (u * 10 + 9) * Z, :] for u in (1, 2)], axis=0)

    def put_a(at, v):
        grads_ref[core, at : at + v.shape[0], :] = v

    def put_b(at, v):
        grads_ref[1 - core, at : at + v.shape[0], :] = v

    for q in range(4):
        r = mm(corners[q], gec, TN).astype(BF)
        for c in range(2):
            t = 2 * q + c
            if t == 0:
                put_a(27 * C, lanes(r, c))
            else:
                put_b(27 * CIN + (t - 1) * C, lanes(r, c))
    put_b(27 * CIN + 7 * C, jnp.zeros((HALF - 27 * CIN - 7 * C, C), BF))
    weight_grad(firsts, 1, 1, C, lambda t, v: put_a(t * C, v))

    for x in range(X):
        p = taps(cots, x, Y, back_ref, NT, flip=True)
        g = lanes(p, 1) + from_above(lanes(p, 0)) + from_below(lanes(p, 2))
        g = g + cots(x + 1, 1, Y).astype(F32)
        g = (g * sg1[x * Y * Z : (x + 1) * Y * Z, :]).astype(BF)
        put_z_taps(x, g.astype(F32))
    weight_grad(cells, 2, 2, CIN, lambda t, v: put_b(t * CIN, v))


VM = pl.BlockSpec(memory_space=pltpu.VMEM)


def call(kernel, outs, args, in_specs=None, scratch=(), flops=10_000_000, vmem=40 << 20, out_specs=None, aliases={}):
    return pl.pallas_call(
        kernel,
        out_shape=tuple(jax.ShapeDtypeStruct(shape, dtype) for shape, dtype in outs),
        in_specs=in_specs or [VM] * len(args),
        out_specs=tuple(out_specs or [VM] * len(outs)),
        input_output_aliases=aliases,
        scratch_shapes=[pltpu.VMEM(*s) if isinstance(s, tuple) else s for s in scratch],
        compiler_params=pltpu.CompilerParams(vmem_limit_bytes=vmem),
        cost_estimate=pl.CostEstimate(
            flops=flops, bytes_accessed=1_000_000, transcendentals=0
        ),
    )(*args)


def arrange(w1_ref, w2_ref, after_ref, first_ref, second_ref, back_ref):
    for m in range(9):
        for k in range(3):
            first_ref[m * C : m * C + CIN, k * C : (k + 1) * C] = w1_ref[3 * m + k]
            second_ref[m * C : (m + 1) * C, k * C : (k + 1) * C] = w2_ref[3 * m + k]
            back_ref[k * C : (k + 1) * C, m * C : (m + 1) * C] = w2_ref[3 * m + k]
        first_ref[m * C + CIN : (m + 1) * C, :] = jnp.zeros((C - CIN, 3 * C), BF)


def begin(mid_ref, mask_ref, w1_ref, w2_ref, part1_ref, first_ref, sg1_ref, part2_ref):
    def cells(x, y, n):
        return mid_ref[((x - 3) * 22 + y) * Z : ((x - 3) * 22 + y + n) * Z, :]

    def firsts(x, y, n):
        return first_ref[((x - 3) * 20 + y) * Z : ((x - 3) * 20 + y + n) * Z, :]

    masks = [spread(mask_ref[...], by) for by in range(6)]
    act = jnp.concatenate([masks[(y + 4) // 4] for y in range(-2, 18)], axis=0)
    for x in (3, 4, 1, 2, 5, 6):
        p = taps(cells, x, 20, w1_ref, lines=[i for i in range(3) if 3 <= x + i < 7])
        pre = lanes(p, 1) + from_below(lanes(p, 0)) + from_above(lanes(p, 2))
        if x in (3, 4):
            value, slope = silu(act * pre)
            first_ref[(x - 3) * 20 * Z : (x - 2) * 20 * Z, :] = value.astype(BF)
            sg1_ref[(x - 3) * Y * Z : (x - 2) * Y * Z, :] = (act * slope)[2 * Z : 18 * Z]
        else:
            part1_ref[EARLY[x]] = pre
    for x in range(1, 5):
        p = taps(firsts, x, 18, w2_ref, lines=[i for i in range(3) if 3 <= x + i < 5])
        part2_ref[x - 1] = lanes(p, 1) + from_below(lanes(p, 0)) + from_above(lanes(p, 2))


def prepare(
    grad_hbm, feat_hbm, blocks_hbm, owners_hbm, rows_ref, own_ref, near_ref, far_ref,
    wide, grad_ref, feat_ref, blocks_ref, owners_ref, sems,
):
    copies = [
        pltpu.make_async_copy(a, b, sems.at[n])
        for n, (a, b) in enumerate(
            ((grad_hbm, grad_ref), (feat_hbm, feat_ref), (blocks_hbm, blocks_ref), (owners_hbm, owners_ref))
        )
    ]
    for c in copies:
        c.start()
    copies[0].wait()
    row, col = iota((128, 32), 0), iota((128, 32), 1)
    take = one((col == 2 * (row // 8) - 2 + row % 8) & (row % 8 < 6))
    rows_ref[...] = mm(take, grad_ref[0, 0]).astype(BF)
    for c in copies[1:]:
        c.wait()
    lane = iota((Y, C), 1)
    for x in range(X):
        f = feat_ref[x].astype(F32)
        f = jnp.concatenate([f, jnp.zeros((Y, C), F32)], axis=1)
        for z in range(Z):
            t = jnp.where(lane < CIN, f[:, z * CIN : z * CIN + C], 0.0)
            wide[pl.ds(x * Y * Z + z, Y, stride=Z), :] = t
    blocks = blocks_ref[0].astype(F32)
    mine = iota((Z, 4), 0) // 4 == iota((Z, 4), 1)
    for by in range(4):
        m = jnp.sum(jnp.where(mine, blocks[by : by + 1, :], 0.0), axis=1, keepdims=True)
        m = jnp.broadcast_to(m, (Z, C))
        own_ref[OWN + by * Z : OWN + (by + 1) * Z, :] = m.astype(BF)
        for x in range(X):
            for y in range(4 * by, 4 * by + 4):
                at = (x * Y + y) * Z
                own_ref[at : at + Z, :] = (wide[at : at + Z, :] * m).astype(BF)
    row, col = iota((16, 16), 0), iota((16, 16), 1)
    across = jnp.broadcast_to(owners_ref[...].astype(F32), (16, 16))
    dest = jnp.sum(jnp.where(row == col, across, 0.0), axis=1, keepdims=True)
    rank = jnp.sum(jnp.where((col < row) & (dest == across), 1.0, 0.0), axis=1, keepdims=True)
    place = jnp.broadcast_to(dest * 8.0 + rank, (16, C)).astype(BF)
    own_ref[OWN + 4 * Z : OWN + 5 * Z, :] = place

    def fill(up, down):
        for x in range(X):
            up[x * 3 * Z : (x + 1) * 3 * Z, :] = own_ref[(x * Y + 13) * Z : (x + 1) * Y * Z, :]
            down[x * 3 * Z : (x + 1) * 3 * Z, :] = own_ref[x * Y * Z : (x * Y + 3) * Z, :]
        for ref, by in ((up, 3), (down, 0)):
            ref[192:208, :] = place
            ref[208:224, :] = own_ref[OWN + by * Z : OWN + (by + 1) * Z, :]

    @pl.when(lax.rem(lax.axis_index("x"), 2) == 0)
    def _():
        fill(near_ref, far_ref)

    @pl.when(lax.rem(lax.axis_index("x"), 2) == 1)
    def _():
        fill(far_ref, near_ref)


def widen(
    own_ref, beside_ref, beyond_ref, rows_ref, after_ref,
    mid_ref, mask_ref, gc_ref, place_ref, near_ref, far_ref,
    sides,
):
    odd = lax.rem(lax.axis_index("x"), 2)
    sides[1 - odd] = beside_ref[...]
    sides[odd] = beyond_ref[...]
    low_ref, high_ref = sides.at[0], sides.at[1]
    for x in range(X):
        at = x * 22 * Z
        mid_ref[at : at + 3 * Z, :] = low_ref[x * 3 * Z : (x + 1) * 3 * Z, :]
        mid_ref[at + 3 * Z : at + 19 * Z, :] = own_ref[x * Y * Z : (x + 1) * Y * Z, :]
        mid_ref[at + 19 * Z : at + 22 * Z, :] = high_ref[x * 3 * Z : (x + 1) * 3 * Z, :]
    tiles = [low_ref[208:224, :]]
    tiles += [own_ref[OWN + by * Z : OWN + (by + 1) * Z, :] for by in range(4)]
    tiles += [high_ref[208:224, :]]
    which = iota((Z, C), 1) // 16
    packed = jnp.zeros((Z, C), F32)
    for by in range(6):
        packed = jnp.where(which == by, tiles[by].astype(F32), packed)
    mask_ref[...] = packed.astype(BF)
    place_ref[...] = own_ref[OWN + 4 * Z : OWN + 5 * Z, :]
    place = jnp.concatenate(
        [
            low_ref[192:208, :].astype(F32),
            own_ref[OWN + 4 * Z : OWN + 5 * Z, :].astype(F32) + 2.0,
            high_ref[192:208, :].astype(F32) + 4.0,
        ],
        axis=0,
    )
    bricks = mm(one(place == iota((48, C), 1).astype(F32)), rows_ref[...])[12:44].astype(BF)
    for q in range(8):
        gc_ref[q // 4, q % 4] = lanes(bricks, q)

    def fill(up, down):
        for q in range(4):
            up[COTS + q * 32 : COTS + (q + 1) * 32, :] = lanes(bricks, 4 + q)
            down[COTS + q * 32 : COTS + (q + 1) * 32, :] = lanes(bricks, q)
        up[0:COTS, :] = mid_ref[22 * Z :, :]
        down[0:COTS, :] = mid_ref[0:COTS, :]
        for ref in (up, down):
            ref[MASK:, :] = mask_ref[...]

    @pl.when(lax.axis_index("c") == 0)
    def _():
        fill(near_ref, far_ref)

    @pl.when(lax.axis_index("c") == 1)
    def _():
        fill(far_ref, near_ref)


def places():
    core, z, x = lax.axis_index("c"), lax.axis_index("z"), lax.axis_index("x")
    pick = lambda a, b: jnp.where(core == 0, a, b)
    return pick(z, x), pick(x, z), pick(4, 1), pick(1, 4)


def fold_cores(grads_ref, theirs_ref, bricks_ref, *out_refs):
    first, _, a, b = places()
    for n, out in enumerate(out_refs):
        for t in range(4):
            to = (first ^ n) * a + t * b
            rows = pl.ds(pl.multiple_of(to * PART, 16), PART)
            out[t * PART : (t + 1) * PART, :] = (
                grads_ref[0, rows, :].astype(F32) + theirs_ref[rows, :].astype(F32)
            ).astype(BF)
            rows = pl.ds(pl.multiple_of(to * 16, 16), 16)
            out[4 * PART + t * 16 : 4 * PART + (t + 1) * 16, :] = bricks_ref[rows, :]


def fold_first(*refs):
    got, outs = refs[:4], refs[4:]
    _, second, _, _ = places()
    for m, out in enumerate(outs):
        to = second ^ m
        rows = pl.ds(pl.multiple_of(to * PART, 16), PART)
        v = [g[rows, :].astype(F32) for g in got]
        out[:PART, :] = ((v[0] + v[1]) + (v[2] + v[3])).astype(BF)
        rows = pl.ds(pl.multiple_of(4 * PART + to * 16, 16), 16)
        for n, g in enumerate(got):
            out[PART + n * 16 : PART + (n + 1) * 16, :] = g[rows, :]


def fold_second(*refs):
    got, (part_ref, bricks_ref) = refs[:4], refs[4:]
    first, second, a, b = places()
    v = [g[:PART, :].astype(F32) for g in got]
    part_ref[...] = ((v[0] + v[1]) + (v[2] + v[3])).astype(BF)
    for m, g in enumerate(got):
        for n in range(4):
            at = pl.multiple_of(((first ^ n) * a + (second ^ m) * b) * 16, 16)
            bricks_ref[pl.ds(at, 16), :] = g[PART + n * 16 : PART + (n + 1) * 16, :]


def unfold(half_ref, core, first_hbm, second_hbm, down_hbm, wide, sems):
    spans = {
        0: ((0, 27 * C, second_hbm, 0), (27 * C, 28 * C, down_hbm, 0)),
        1: ((0, 27 * CIN, first_hbm, 0), (27 * CIN, 27 * CIN + 7 * C, down_hbm, C)),
    }

    def emit(which):
        copies = []
        for lo, hi, out, to in spans[which]:
            step = 864 if hi - lo > 1024 else hi - lo
            for at in range(lo, hi, step):
                wide[at : at + step, :] = half_ref[at : at + step, :].astype(F32)
                copies.append(
                    pltpu.make_async_copy(
                        wide.at[pl.ds(at, step)],
                        out.at[pl.ds(to + at - lo, step)],
                        sems.at[len(copies)],
                    )
                )
                copies[-1].start()
        for c in copies:
            c.wait()

    for which in range(2):
        pl.when(core == which)(functools.partial(emit, which))


def unfold_own(half_ref, first_hbm, second_hbm, down_hbm, wide, sems):
    unfold(half_ref, lax.axis_index("c"), first_hbm, second_hbm, down_hbm, wide, sems)


def unfold_other(half_ref, a, b, c, first_hbm, second_hbm, down_hbm, wide, sems):
    unfold(half_ref, 1 - lax.axis_index("c"), first_hbm, second_hbm, down_hbm, wide, sems)


def swap(v, axes, first):
    n = lax.axis_size(axes)
    pairs = [(i, i + 1) for i in range(first, n - 1, 2)]
    return lax.ppermute(v, axes, pairs + [(j, i) for i, j in pairs])


def swap_cores(v):
    return lax.ppermute(v, "c", [(0, 1), (1, 0)])


def up_matrix():
    m = np.zeros((6 * Z, 64), np.float32)
    for by in range(6):
        for z in range(Z):
            m[by * Z + z, z // 2 % 2 * 32 + by * 4 + z // 4] = 1
    return jnp.asarray(m, BF)


def flip(v, axis, bits):
    return lax.ppermute(v, axis, [(i, i ^ bits) for i in range(lax.axis_size(axis))])


def flip_by_core(v, axes, bits):
    every = ("c", "z", "x")
    size = [lax.axis_size(n) for n in every]
    pairs = []
    for d in range(size[0] * size[1] * size[2]):
        at = [int(i) for i in np.unravel_index(d, size)]
        at[every.index(axes[at[0]])] ^= bits
        pairs.append((d, int(np.ravel_multi_index(at, size))))
    return lax.ppermute(v, every, pairs)


def per_device(features, block_mask, weight_first, weight_second, weight_down, owners, moved_grad):
    rows, own, beside, beyond = call(
        prepare,
        [((128, 8 * C), BF), ((X * Y * Z + 80, C), BF), ((224, C), BF), ((224, C), BF)],
        (moved_grad, features, block_mask, owners.reshape(1, 16)),
        [pl.BlockSpec(memory_space=pltpu.HBM)] * 4,
        [
            ((X * Y * Z, C), F32),
            (moved_grad.shape, BF),
            (features.shape, BF),
            (block_mask.shape, jnp.int32),
            ((1, 16), jnp.int32),
            pltpu.SemaphoreType.DMA((4,)),
        ],
        vmem=60 << 20,
    )
    beyond, beside = swap(beyond, GY, 1), swap(beside, GY, 0)
    w1, w2, back = call(
        arrange,
        [((9 * C, 3 * C), BF), ((9 * C, 3 * C), BF), ((3 * C, 9 * C), BF)],
        (weight_first, weight_second, own),
        flops=2_000_000_000,
    )
    rows = lax.all_to_all(rows, GY, 0, 0, tiled=True)

    mid, mask, gc, place, near, far = call(
        widen,
        [((4 * 22 * Z, C), BF), ((16, C), BF), ((2, 4, 32, C), BF), ((16, C), BF), ((STRIP, C), BF), ((STRIP, C), BF)],
        (own, beside, beyond, rows, w1),
        [VM] * 4 + [pl.BlockSpec(memory_space=pl.ANY)],
        scratch=[((2, 224, C), BF)],
    )
    far, near = swap(far, GX, 1), swap(near, GX, 0)
    ahead = call(
        begin,
        [((4, 20 * Z, C), F32), ((40 * Z, C), BF), ((2 * Y * Z, C), F32), ((4, 18 * Z, C), F32)],
        (mid, mask, w1, w2),
        flops=3_000_000_000,
    )

    grads, outgoing = call(
        section,
        [((2, HALF, C), BF), ((256, C), BF)],
        (near, mid, far, mask, gc, place, *ahead, w1, w2, back, weight_down, up_matrix()),
        scratch=[
            ((2, STRIP, C), BF),
            ((8 * 20 * Z, C), BF),
            ((X * Y * Z, C), F32),
            ((X * Y * Z, C), BF),
            ((40 * Z, 2 * C), BF),
            ((6 * 18 * Z, C), BF),
            ((X * Y * Z, 3 * C), BF),
            ((3 * C, 6 * Y * Z), BF),
        ],
        flops=8_000_000_000,
    )

    blocks = call(
        fold_cores, [((4 * PART + 64, C), BF)] * 4, (grads, swap_cores(grads[1]), outgoing)
    )
    blocks = [blocks[0]] + [flip_by_core(blocks[n], ("z", "x"), n) for n in (1, 2, 3)]
    blocks = call(fold_first, [((PART + 64, C), BF)] * 4, blocks)
    blocks = [blocks[0]] + [flip_by_core(blocks[n], ("x", "z"), n) for n in (1, 2, 3)]
    part, arrived = call(fold_second, [((PART, C), BF), ((256, C), BF)], blocks)
    moved = arrived.reshape(16, 8, 2, C).transpose(0, 2, 1, 3).reshape(1, 1, 32, 8 * C)
    others = [flip(part, "y", n).astype(F32) for n in (1, 2, 3)]
    part = ((part.astype(F32) + others[0]) + (others[1] + others[2])).astype(BF)
    part = lax.all_to_all(jnp.broadcast_to(part[None], (16, PART, C)), GY, 0, 0, tiled=True)
    part = part.reshape(HALF, C)
    grads = [((27 * CIN, C), F32), ((27 * C, C), F32), ((8 * C, C), F32)]
    scratch = [((HALF, C), F32), pltpu.SemaphoreType.DMA((5,))]
    hbm = pl.BlockSpec(memory_space=pl.ANY)
    other = swap_cores(part)
    grads_own = call(unfold_own, grads, (part,), [VM], scratch, out_specs=[hbm] * 3)
    grad_first, grad_second, grad_down = call(
        unfold_other, grads, (other, *grads_own), [VM] + [hbm] * 3, scratch, out_specs=[hbm] * 3,
        aliases={1: 0, 2: 1, 3: 2},
    )
    return (
        moved,
        grad_first.reshape(27, CIN, C),
        grad_second.reshape(27, C, C),
        grad_down.reshape(8, C, C),
    )


def solution(mesh):
    shape = dict(mesh.shape)
    fine = Mesh(
        mesh.devices.reshape(shape["gx"] // 2, 2, 4, shape["gy"] // 4), ("y", "c", "z", "x")
    )
    whole, tiles = P(GX, GY, None), P(GX, GY, None, None)
    return jax.shard_map(
        per_device,
        mesh=fine,
        in_specs=(whole, whole, P(), P(), P(), tiles, tiles),
        out_specs=(tiles, P(), P(), P()),
        check_vma=False,
    )
```

```python
import functools

import jax
import jax.numpy as jnp
import numpy as np
from jax import lax
from jax.experimental import pallas as pl
from jax.experimental.pallas import tpu as pltpu
from jax.sharding import Mesh, PartitionSpec as P

GX, GY = ("y", "c"), ("z", "x")
F32, BF = jnp.float32, jnp.bfloat16
X, Y, Z, C, CIN = 4, 16, 16, 128, 96
HALF, PART = 3584, 224
OWN = 1024
COTS, MASK, STRIP = 1056, 1184, 1200
EARLY = {1: 0, 2: 1, 5: 2, 6: 3}
NN = (((1,), (0,)), ((), ()))
NT = (((1,), (1,)), ((), ()))
TN = (((0,), (0,)), ((), ()))


def mm(a, b, dims=NN):
    return lax.dot_general(a, b, dims, preferred_element_type=F32)


def iota(shape, axis):
    return lax.broadcasted_iota(jnp.int32, shape, axis)


def one(where):
    return jnp.where(where, 1.0, 0.0).astype(BF)


def z_of(rows):
    return iota((rows, C), 0) % Z


def from_above(v):
    return jnp.where(z_of(v.shape[0]) < Z - 1, pltpu.roll(v, v.shape[0] - 1, 0), 0.0)


def from_below(v):
    return jnp.where(z_of(v.shape[0]) > 0, pltpu.roll(v, 1, 0), 0.0)


def lanes(p, k):
    return p[:, k * C : (k + 1) * C]


def silu(v):
    s = jax.nn.sigmoid(v)
    return v * s, s * (1.0 + v * (1.0 - s))


def spread(packed, by):
    return jnp.broadcast_to(packed[:, 16 * by : 16 * by + 1].astype(F32), (Z, C))


def taps(get, x, n, w, dims=NN, flip=False, lines=(0, 1, 2)):
    wins = []
    for i in lines:
        for j in range(3):
            wins.append(get(x + 2 - i, 2 - j, n) if flip else get(x + i, j, n))
    if len(lines) < 3:
        w = w[3 * lines[0] * C : 3 * (lines[-1] + 1) * C, :]
    else:
        w = w[...]
    return mm(jnp.concatenate(wins, axis=1), w, dims)


def section(
    near_ref, mid_ref, far_ref, mask_ref, gc_ref, place_ref, part1_ref, inner_ref, slope_ref, part2_ref, w1_ref, w2_ref, back_ref, wd_ref, up_ref,
    grads_ref, out_ref,
    sides, first, sg1, second, ge, g2, gs, vt,
):
    core = lax.axis_index("c")
    sides[1 - core] = near_ref[...]
    sides[core] = far_ref[...]
    low_ref, high_ref = sides.at[0], sides.at[1]

    def cells(x, y, n):
        ref, x = ((low_ref, x), (mid_ref, x - 3), (high_ref, x - 7))[(x > 2) + (x > 6)]
        return ref[(x * 22 + y) * Z : (x * 22 + y + n) * Z, :]

    def firsts(x, y, n):
        return first[(x * 20 + y) * Z : (x * 20 + y + n) * Z, :]

    def cots(x, y, n):
        return g2[(x * 18 + y) * Z : (x * 18 + y + n) * Z, :]

    packed = low_ref[MASK:, :], mask_ref[...], high_ref[MASK:, :]
    masks = [[spread(t, by) for by in range(6)] for t in packed]

    def cotangent(u, q):
        if u in (1, 2):
            return gc_ref[u - 1, q]
        return (low_ref if u == 0 else high_ref)[COTS + q * 32 : COTS + (q + 1) * 32, :]

    def line(x, y0, cells):
        return jnp.concatenate(
            [masks[(x + 4) // 4][(y + 4) // 4] for y in range(y0, y0 + cells)], axis=0
        )

    def weight_grad(get, x0, y0, rows, put):
        for j in range(3):
            for x in range(6):
                vt[j * C : (j + 1) * C, x * Y * Z : (x + 1) * Y * Z] = get(x0 + x, y0 + j, Y).T
        for i in range(3):
            p = mm(vt[:, i * Y * Z : (i + X) * Y * Z], gs[...]).astype(BF)
            for j in range(3):
                for k in range(3):
                    put(9 * i + 3 * j + k, p[j * C : j * C + rows, k * C : (k + 1) * C])

    def put_z_taps(x, g):
        at = x * Y * Z
        gs[at : at + Y * Z, 0:C] = from_above(g).astype(BF)
        gs[at : at + Y * Z, C : 2 * C] = g.astype(BF)
        gs[at : at + Y * Z, 2 * C : 3 * C] = from_below(g).astype(BF)

    first[3 * 20 * Z : 5 * 20 * Z, :] = inner_ref[...]
    sg1[Y * Z : 3 * Y * Z, :] = slope_ref[...]
    for x in (0, 1, 2, 5, 6, 7):
        p = taps(cells, x, 20, w1_ref, lines=[i for i in range(3) if not 3 <= x + i < 7])
        pre = lanes(p, 1) + from_below(lanes(p, 0)) + from_above(lanes(p, 2))
        if x in EARLY:
            pre = pre + part1_ref[EARLY[x]]
        act = line(x - 2, -2, 20)
        value, slope = silu(act * pre)
        first[x * 20 * Z : (x + 1) * 20 * Z, :] = value.astype(BF)
        if x in (2, 5):
            sg1[(x - 2) * Y * Z : (x - 1) * Y * Z, :] = (act * slope)[2 * Z : 18 * Z]

    even = z_of(6 * Z) % 2 == 0
    for u in range(4):
        both = jnp.concatenate(
            [jnp.concatenate([cotangent(u, 2 * b + c) for b in range(2)], axis=1) for c in range(2)],
            axis=0,
        )
        r = mm(up_ref[...], both)
        for v in range(10):
            by, b = (v + 1) // 2, (v + 1) % 2
            t = r[by * Z : (by + 1) * Z, b * C : (b + 1) * C]
            at = (u * 10 + v) * Z
            ge[at : at + Z, 0:C] = jnp.where(even[:Z], t, 0.0).astype(BF)
            ge[at : at + Z, C : 2 * C] = jnp.where(even[:Z], 0.0, t).astype(BF)

    for x in range(6):
        p = taps(firsts, x, 18, w2_ref, lines=[i for i in range(3) if not 3 <= x + i < 5])
        act = line(x - 1, -1, 18)
        pre = lanes(p, 1) + from_below(lanes(p, 0)) + from_above(lanes(p, 2))
        if 1 <= x < 5:
            pre = pre + part2_ref[x - 1]
        value, slope = silu(act * pre + firsts(x + 1, 1, 18).astype(F32))
        if 1 <= x < 5:
            second[(x - 1) * Y * Z : x * Y * Z, :] = value[Z : 17 * Z].astype(BF)
        u, a = (x + 1) // 2, (x + 1) % 2
        back = []
        for b in range(2):
            at = (u * 10 + 1 - b) * Z
            w = jnp.concatenate([wd_ref[4 * a + 2 * b], wd_ref[4 * a + 2 * b + 1]], axis=1)
            back.append(mm(ge[at : at + 9 * Z, :], w, NT))
        g = jnp.concatenate(
            [back[1 - y % 2][y // 2 * Z : (y // 2 + 1) * Z] for y in range(18)], axis=0
        )
        g = (act * g * slope).astype(BF)
        g2[x * 18 * Z : (x + 1) * 18 * Z, :] = g
        if 1 <= x < 5:
            put_z_taps(x - 1, g[Z : 17 * Z].astype(F32))

    def corner(a, b):
        return jnp.concatenate(
            [
                second[((2 * u + a) * Y + 2 * v + b) * Z : ((2 * u + a) * Y + 2 * v + b + 1) * Z, :]
                for u in range(2)
                for v in range(8)
            ],
            axis=0,
        )

    corners = [corner(a, b) for a in range(2) for b in range(2)]
    wd = jnp.concatenate(
        [jnp.concatenate([wd_ref[2 * q], wd_ref[2 * q + 1]], axis=1) for q in range(4)], axis=0
    )
    p = mm(jnp.concatenate(corners, axis=1), wd)
    coarse = (lanes(p, 0) + from_above(lanes(p, 1))).astype(BF)
    row, col = iota((128, 256), 0), iota((128, 256), 1)
    a, by, b, z = col // 128, col // 32 % 4, col // 16 % 2, col % Z
    order = (row // 16 == 4 * a + 2 * b + z // 2 % 2) & (row % 16 == by * 4 + z // 4) & (z % 2 == 0)
    bricks = mm(one(order), coarse).astype(BF)
    place = jnp.concatenate([place_ref[...].astype(F32)] * 8, axis=0)
    place = jnp.concatenate([place] * 2, axis=1)
    target = (8 * (col // 16) + col % 2).astype(F32)
    out_ref[...] = mm(one((place == target) & (row // 16 == col // 2 % 8)), bricks, TN).astype(BF)

    gec = jnp.concatenate([ge[(u * 10 + 1) * Z : (u * 10 + 9) * Z, :] for u in (1, 2)], axis=0)

    def put_a(at, v):
        grads_ref[core, at : at + v.shape[0], :] = v

    def put_b(at, v):
        grads_ref[1 - core, at : at + v.shape[0], :] = v

    for q in range(4):
        r = mm(corners[q], gec, TN).astype(BF)
        for c in range(2):
            t = 2 * q + c
            if t == 0:
                put_a(27 * C, lanes(r, c))
            else:
                put_b(27 * CIN + (t - 1) * C, lanes(r, c))
    put_b(27 * CIN + 7 * C, jnp.zeros((HALF - 27 * CIN - 7 * C, C), BF))
    weight_grad(firsts, 1, 1, C, lambda t, v: put_a(t * C, v))

    for x in range(X):
        p = taps(cots, x, Y, back_ref, NT, flip=True)
        g = lanes(p, 1) + from_above(lanes(p, 0)) + from_below(lanes(p, 2))
        g = g + cots(x + 1, 1, Y).astype(F32)
        g = (g * sg1[x * Y * Z : (x + 1) * Y * Z, :]).astype(BF)
        put_z_taps(x, g.astype(F32))
    weight_grad(cells, 2, 2, CIN, lambda t, v: put_b(t * CIN, v))


VM = pl.BlockSpec(memory_space=pltpu.VMEM)


def call(kernel, outs, args, in_specs=None, scratch=(), flops=10_000_000, vmem=40 << 20, out_specs=None, aliases={}):
    return pl.pallas_call(
        kernel,
        out_shape=tuple(jax.ShapeDtypeStruct(shape, dtype) for shape, dtype in outs),
        in_specs=in_specs or [VM] * len(args),
        out_specs=tuple(out_specs or [VM] * len(outs)),
        input_output_aliases=aliases,
        scratch_shapes=[pltpu.VMEM(*s) if isinstance(s, tuple) else s for s in scratch],
        compiler_params=pltpu.CompilerParams(vmem_limit_bytes=vmem),
        cost_estimate=pl.CostEstimate(
            flops=flops, bytes_accessed=1_000_000, transcendentals=0
        ),
    )(*args)


def arrange(w1_ref, w2_ref, after_ref, first_ref, second_ref, back_ref):
    for m in range(9):
        for k in range(3):
            first_ref[m * C : m * C + CIN, k * C : (k + 1) * C] = w1_ref[3 * m + k]
            second_ref[m * C : (m + 1) * C, k * C : (k + 1) * C] = w2_ref[3 * m + k]
            back_ref[k * C : (k + 1) * C, m * C : (m + 1) * C] = w2_ref[3 * m + k]
        first_ref[m * C + CIN : (m + 1) * C, :] = jnp.zeros((C - CIN, 3 * C), BF)


def begin(mid_ref, mask_ref, w1_ref, w2_ref, part1_ref, first_ref, sg1_ref, part2_ref):
    def cells(x, y, n):
        return mid_ref[((x - 3) * 22 + y) * Z : ((x - 3) * 22 + y + n) * Z, :]

    def firsts(x, y, n):
        return first_ref[((x - 3) * 20 + y) * Z : ((x - 3) * 20 + y + n) * Z, :]

    masks = [spread(mask_ref[...], by) for by in range(6)]
    act = jnp.concatenate([masks[(y + 4) // 4] for y in range(-2, 18)], axis=0)
    for x in (3, 4, 1, 2, 5, 6):
        p = taps(cells, x, 20, w1_ref, lines=[i for i in range(3) if 3 <= x + i < 7])
        pre = lanes(p, 1) + from_below(lanes(p, 0)) + from_above(lanes(p, 2))
        if x in (3, 4):
            value, slope = silu(act * pre)
            first_ref[(x - 3) * 20 * Z : (x - 2) * 20 * Z, :] = value.astype(BF)
            sg1_ref[(x - 3) * Y * Z : (x - 2) * Y * Z, :] = (act * slope)[2 * Z : 18 * Z]
        else:
            part1_ref[EARLY[x]] = pre
    for x in range(1, 5):
        p = taps(firsts, x, 18, w2_ref, lines=[i for i in range(3) if 3 <= x + i < 5])
        part2_ref[x - 1] = lanes(p, 1) + from_below(lanes(p, 0)) + from_above(lanes(p, 2))


def prepare(
    grad_hbm, feat_hbm, blocks_hbm, owners_hbm, rows_ref, own_ref, near_ref, far_ref,
    wide, grad_ref, feat_ref, blocks_ref, owners_ref, sems,
):
    copies = [
        pltpu.make_async_copy(a, b, sems.at[n])
        for n, (a, b) in enumerate(
            ((grad_hbm, grad_ref), (feat_hbm, feat_ref), (blocks_hbm, blocks_ref), (owners_hbm, owners_ref))
        )
    ]
    for c in copies:
        c.start()
    copies[0].wait()
    row, col = iota((128, 32), 0), iota((128, 32), 1)
    take = one((col == 2 * (row // 8) - 2 + row % 8) & (row % 8 < 6))
    rows_ref[...] = mm(take, grad_ref[0, 0]).astype(BF)
    for c in copies[1:]:
        c.wait()
    lane = iota((Y, C), 1)
    for x in range(X):
        f = feat_ref[x].astype(F32)
        f = jnp.concatenate([f, jnp.zeros((Y, C), F32)], axis=1)
        for z in range(Z):
            t = jnp.where(lane < CIN, f[:, z * CIN : z * CIN + C], 0.0)
            wide[pl.ds(x * Y * Z + z, Y, stride=Z), :] = t
    blocks = blocks_ref[0].astype(F32)
    mine = iota((Z, 4), 0) // 4 == iota((Z, 4), 1)
    for by in range(4):
        m = jnp.sum(jnp.where(mine, blocks[by : by + 1, :], 0.0), axis=1, keepdims=True)
        m = jnp.broadcast_to(m, (Z, C))
        own_ref[OWN + by * Z : OWN + (by + 1) * Z, :] = m.astype(BF)
        for x in range(X):
            for y in range(4 * by, 4 * by + 4):
                at = (x * Y + y) * Z
                own_ref[at : at + Z, :] = (wide[at : at + Z, :] * m).astype(BF)
    row, col = iota((16, 16), 0), iota((16, 16), 1)
    across = jnp.broadcast_to(owners_ref[...].astype(F32), (16, 16))
    dest = jnp.sum(jnp.where(row == col, across, 0.0), axis=1, keepdims=True)
    rank = jnp.sum(jnp.where((col < row) & (dest == across), 1.0, 0.0), axis=1, keepdims=True)
    place = jnp.broadcast_to(dest * 8.0 + rank, (16, C)).astype(BF)
    own_ref[OWN + 4 * Z : OWN + 5 * Z, :] = place

    def fill(up, down):
        for x in range(X):
            up[x * 3 * Z : (x + 1) * 3 * Z, :] = own_ref[(x * Y + 13) * Z : (x + 1) * Y * Z, :]
            down[x * 3 * Z : (x + 1) * 3 * Z, :] = own_ref[x * Y * Z : (x * Y + 3) * Z, :]
        for ref, by in ((up, 3), (down, 0)):
            ref[192:208, :] = place
            ref[208:224, :] = own_ref[OWN + by * Z : OWN + (by + 1) * Z, :]

    @pl.when(lax.rem(lax.axis_index("x"), 2) == 0)
    def _():
        fill(near_ref, far_ref)

    @pl.when(lax.rem(lax.axis_index("x"), 2) == 1)
    def _():
        fill(far_ref, near_ref)


def widen(
    own_ref, beside_ref, beyond_ref, rows_ref, after_ref,
    mid_ref, mask_ref, gc_ref, place_ref, near_ref, far_ref,
    sides,
):
    odd = lax.rem(lax.axis_index("x"), 2)
    sides[1 - odd] = beside_ref[...]
    sides[odd] = beyond_ref[...]
    low_ref, high_ref = sides.at[0], sides.at[1]
    for x in range(X):
        at = x * 22 * Z
        mid_ref[at : at + 3 * Z, :] = low_ref[x * 3 * Z : (x + 1) * 3 * Z, :]
        mid_ref[at + 3 * Z : at + 19 * Z, :] = own_ref[x * Y * Z : (x + 1) * Y * Z, :]
        mid_ref[at + 19 * Z : at + 22 * Z, :] = high_ref[x * 3 * Z : (x + 1) * 3 * Z, :]
    tiles = [low_ref[208:224, :]]
    tiles += [own_ref[OWN + by * Z : OWN + (by + 1) * Z, :] for by in range(4)]
    tiles += [high_ref[208:224, :]]
    which = iota((Z, C), 1) // 16
    packed = jnp.zeros((Z, C), F32)
    for by in range(6):
        packed = jnp.where(which == by, tiles[by].astype(F32), packed)
    mask_ref[...] = packed.astype(BF)
    place_ref[...] = own_ref[OWN + 4 * Z : OWN + 5 * Z, :]
    place = jnp.concatenate(
        [
            low_ref[192:208, :].astype(F32),
            own_ref[OWN + 4 * Z : OWN + 5 * Z, :].astype(F32) + 2.0,
            high_ref[192:208, :].astype(F32) + 4.0,
        ],
        axis=0,
    )
    bricks = mm(one(place == iota((48, C), 1).astype(F32)), rows_ref[...])[12:44].astype(BF)
    for q in range(8):
        gc_ref[q // 4, q % 4] = lanes(bricks, q)

    def fill(up, down):
        for q in range(4):
            up[COTS + q * 32 : COTS + (q + 1) * 32, :] = lanes(bricks, 4 + q)
            down[COTS + q * 32 : COTS + (q + 1) * 32, :] = lanes(bricks, q)
        up[0:COTS, :] = mid_ref[22 * Z :, :]
        down[0:COTS, :] = mid_ref[0:COTS, :]
        for ref in (up, down):
            ref[MASK:, :] = mask_ref[...]

    @pl.when(lax.axis_index("c") == 0)
    def _():
        fill(near_ref, far_ref)

    @pl.when(lax.axis_index("c") == 1)
    def _():
        fill(far_ref, near_ref)


def places():
    core, z, x = lax.axis_index("c"), lax.axis_index("z"), lax.axis_index("x")
    pick = lambda a, b: jnp.where(core == 0, a, b)
    return pick(z, x), pick(x, z), pick(4, 1), pick(1, 4)


def fold_cores(grads_ref, theirs_ref, bricks_ref, *out_refs):
    first, _, a, b = places()
    for n, out in enumerate(out_refs):
        for t in range(4):
            to = (first ^ n) * a + t * b
            rows = pl.ds(pl.multiple_of(to * PART, 16), PART)
            out[t * PART : (t + 1) * PART, :] = (
                grads_ref[0, rows, :].astype(F32) + theirs_ref[rows, :].astype(F32)
            ).astype(BF)
            rows = pl.ds(pl.multiple_of(to * 16, 16), 16)
            out[4 * PART + t * 16 : 4 * PART + (t + 1) * 16, :] = bricks_ref[rows, :]


def fold_first(*refs):
    got, outs = [refs[i] for i in (0, 1, 3, 2)], refs[4:]
    _, second, _, _ = places()
    for m, out in enumerate(outs):
        to = second ^ m
        rows = pl.ds(pl.multiple_of(to * PART, 16), PART)
        v = [g[rows, :].astype(F32) for g in got]
        out[:PART, :] = ((v[0] + v[1]) + (v[2] + v[3])).astype(BF)
        rows = pl.ds(pl.multiple_of(4 * PART + to * 16, 16), 16)
        for n, g in enumerate(got):
            out[PART + n * 16 : PART + (n + 1) * 16, :] = g[rows, :]


def fold_second(*refs):
    got, (part_ref, bricks_ref) = [refs[i] for i in (0, 1, 3, 2)], refs[4:]
    first, second, a, b = places()
    v = [g[:PART, :].astype(F32) for g in got]
    part_ref[...] = ((v[0] + v[1]) + (v[2] + v[3])).astype(BF)
    for m, g in enumerate(got):
        for n in range(4):
            at = pl.multiple_of(((first ^ n) * a + (second ^ m) * b) * 16, 16)
            bricks_ref[pl.ds(at, 16), :] = g[PART + n * 16 : PART + (n + 1) * 16, :]


def unfold(half_ref, core, first_hbm, second_hbm, down_hbm, wide, sems):
    spans = {
        0: ((0, 27 * C, second_hbm, 0), (27 * C, 28 * C, down_hbm, 0)),
        1: ((0, 27 * CIN, first_hbm, 0), (27 * CIN, 27 * CIN + 7 * C, down_hbm, C)),
    }

    def emit(which):
        copies = []
        for lo, hi, out, to in spans[which]:
            step = 864 if hi - lo > 1024 else hi - lo
            for at in range(lo, hi, step):
                wide[at : at + step, :] = half_ref[at : at + step, :].astype(F32)
                copies.append(
                    pltpu.make_async_copy(
                        wide.at[pl.ds(at, step)],
                        out.at[pl.ds(to + at - lo, step)],
                        sems.at[len(copies)],
                    )
                )
                copies[-1].start()
        for c in copies:
            c.wait()

    for which in range(2):
        pl.when(core == which)(functools.partial(emit, which))


def unfold_own(half_ref, first_hbm, second_hbm, down_hbm, wide, sems):
    unfold(half_ref, lax.axis_index("c"), first_hbm, second_hbm, down_hbm, wide, sems)


def unfold_other(half_ref, a, b, c, first_hbm, second_hbm, down_hbm, wide, sems):
    unfold(half_ref, 1 - lax.axis_index("c"), first_hbm, second_hbm, down_hbm, wide, sems)


def swap(v, axes, first):
    n = lax.axis_size(axes)
    pairs = [(i, i + 1) for i in range(first, n - 1, 2)]
    return lax.ppermute(v, axes, pairs + [(j, i) for i, j in pairs])


def swap_cores(v):
    return lax.ppermute(v, "c", [(0, 1), (1, 0)])


def up_matrix():
    m = np.zeros((6 * Z, 64), np.float32)
    for by in range(6):
        for z in range(Z):
            m[by * Z + z, z // 2 % 2 * 32 + by * 4 + z // 4] = 1
    return jnp.asarray(m, BF)


def flip(v, axis, bits):
    return lax.ppermute(v, axis, [(i, i ^ bits) for i in range(lax.axis_size(axis))])


def flip_by_core(v, axes, bits):
    every = ("c", "z", "x")
    size = [lax.axis_size(n) for n in every]
    pairs = []
    for d in range(size[0] * size[1] * size[2]):
        at = [int(i) for i in np.unravel_index(d, size)]
        at[every.index(axes[at[0]])] ^= bits
        pairs.append((d, int(np.ravel_multi_index(at, size))))
    return lax.ppermute(v, every, pairs)


def per_device(features, block_mask, weight_first, weight_second, weight_down, owners, moved_grad):
    rows, own, beside, beyond = call(
        prepare,
        [((128, 8 * C), BF), ((X * Y * Z + 80, C), BF), ((224, C), BF), ((224, C), BF)],
        (moved_grad, features, block_mask, owners.reshape(1, 16)),
        [pl.BlockSpec(memory_space=pltpu.HBM)] * 4,
        [
            ((X * Y * Z, C), F32),
            (moved_grad.shape, BF),
            (features.shape, BF),
            (block_mask.shape, jnp.int32),
            ((1, 16), jnp.int32),
            pltpu.SemaphoreType.DMA((4,)),
        ],
        vmem=60 << 20,
    )
    beyond, beside = swap(beyond, GY, 1), swap(beside, GY, 0)
    w1, w2, back = call(
        arrange,
        [((9 * C, 3 * C), BF), ((9 * C, 3 * C), BF), ((3 * C, 9 * C), BF)],
        (weight_first, weight_second, own),
        flops=2_000_000_000,
    )
    rows = lax.all_to_all(rows, GY, 0, 0, tiled=True)

    mid, mask, gc, place, near, far = call(
        widen,
        [((4 * 22 * Z, C), BF), ((16, C), BF), ((2, 4, 32, C), BF), ((16, C), BF), ((STRIP, C), BF), ((STRIP, C), BF)],
        (own, beside, beyond, rows, w1),
        [VM] * 4 + [pl.BlockSpec(memory_space=pl.ANY)],
        scratch=[((2, 224, C), BF)],
    )
    far, near = swap(far, GX, 1), swap(near, GX, 0)
    ahead = call(
        begin,
        [((4, 20 * Z, C), F32), ((40 * Z, C), BF), ((2 * Y * Z, C), F32), ((4, 18 * Z, C), F32)],
        (mid, mask, w1, w2),
        flops=3_000_000_000,
    )

    grads, outgoing = call(
        section,
        [((2, HALF, C), BF), ((256, C), BF)],
        (near, mid, far, mask, gc, place, *ahead, w1, w2, back, weight_down, up_matrix()),
        scratch=[
            ((2, STRIP, C), BF),
            ((8 * 20 * Z, C), BF),
            ((X * Y * Z, C), F32),
            ((X * Y * Z, C), BF),
            ((40 * Z, 2 * C), BF),
            ((6 * 18 * Z, C), BF),
            ((X * Y * Z, 3 * C), BF),
            ((3 * C, 6 * Y * Z), BF),
        ],
        flops=8_000_000_000,
    )

    blocks = call(
        fold_cores, [((4 * PART + 64, C), BF)] * 4, (grads, swap_cores(grads[1]), outgoing)
    )
    far = flip_by_core(blocks[2], ("z", "x"), 2)
    blocks = [blocks[0]] + [flip_by_core(blocks[n], ("z", "x"), n) for n in (1, 3)] + [far]
    blocks = call(fold_first, [((PART + 64, C), BF)] * 4, blocks)
    far = flip_by_core(blocks[2], ("x", "z"), 2)
    blocks = [blocks[0]] + [flip_by_core(blocks[n], ("x", "z"), n) for n in (1, 3)] + [far]
    part, arrived = call(fold_second, [((PART, C), BF), ((256, C), BF)], blocks)
    moved = arrived.reshape(16, 8, 2, C).transpose(0, 2, 1, 3).reshape(1, 1, 32, 8 * C)
    others = [flip(part, "y", n).astype(F32) for n in (1, 2, 3)]
    part = ((part.astype(F32) + others[0]) + (others[1] + others[2])).astype(BF)
    part = lax.all_to_all(jnp.broadcast_to(part[None], (16, PART, C)), GY, 0, 0, tiled=True)
    part = part.reshape(HALF, C)
    grads = [((27 * CIN, C), F32), ((27 * C, C), F32), ((8 * C, C), F32)]
    scratch = [((HALF, C), F32), pltpu.SemaphoreType.DMA((5,))]
    hbm = pl.BlockSpec(memory_space=pl.ANY)
    other = swap_cores(part)
    grads_own = call(unfold_own, grads, (part,), [VM], scratch, out_specs=[hbm] * 3)
    grad_first, grad_second, grad_down = call(
        unfold_other, grads, (other, *grads_own), [VM] + [hbm] * 3, scratch, out_specs=[hbm] * 3,
        aliases={1: 0, 2: 1, 3: 2},
    )
    return (
        moved,
        grad_first.reshape(27, CIN, C),
        grad_second.reshape(27, C, C),
        grad_down.reshape(8, C, C),
    )


def solution(mesh):
    shape = dict(mesh.shape)
    fine = Mesh(
        mesh.devices.reshape(shape["gx"] // 2, 2, 4, shape["gy"] // 4), ("y", "c", "z", "x")
    )
    whole, tiles = P(GX, GY, None), P(GX, GY, None, None)
    return jax.shard_map(
        per_device,
        mesh=fine,
        in_specs=(whole, whole, P(), P(), P(), tiles, tiles),
        out_specs=(tiles, P(), P(), P()),
        check_vma=False,
    )
```

```python
import functools

import jax
import jax.numpy as jnp
import numpy as np
from jax import lax
from jax.experimental import pallas as pl
from jax.experimental.pallas import tpu as pltpu
from jax.sharding import Mesh, PartitionSpec as P

GX, GY = ("y", "c"), ("z", "x")
F32, BF = jnp.float32, jnp.bfloat16
X, Y, Z, C, CIN = 4, 16, 16, 128, 96
HALF, PART = 3584, 224
OWN = 1024
COTS, MASK, STRIP = 1056, 1184, 1200
EARLY = {1: 0, 2: 1, 5: 2, 6: 3}
NN = (((1,), (0,)), ((), ()))
NT = (((1,), (1,)), ((), ()))
TN = (((0,), (0,)), ((), ()))


def mm(a, b, dims=NN):
    return lax.dot_general(a, b, dims, preferred_element_type=F32)


def iota(shape, axis):
    return lax.broadcasted_iota(jnp.int32, shape, axis)


def one(where):
    return jnp.where(where, 1.0, 0.0).astype(BF)


def z_of(rows):
    return iota((rows, C), 0) % Z


def from_above(v):
    return jnp.where(z_of(v.shape[0]) < Z - 1, pltpu.roll(v, v.shape[0] - 1, 0), 0.0)


def from_below(v):
    return jnp.where(z_of(v.shape[0]) > 0, pltpu.roll(v, 1, 0), 0.0)


def lanes(p, k):
    return p[:, k * C : (k + 1) * C]


def silu(v):
    s = jax.nn.sigmoid(v)
    return v * s, s * (1.0 + v * (1.0 - s))


def spread(packed, by):
    return jnp.broadcast_to(packed[:, 16 * by : 16 * by + 1].astype(F32), (Z, C))


def taps(get, x, n, w, dims=NN, flip=False, lines=(0, 1, 2)):
    wins = []
    for i in lines:
        for j in range(3):
            wins.append(get(x + 2 - i, 2 - j, n) if flip else get(x + i, j, n))
    if len(lines) < 3:
        w = w[3 * lines[0] * C : 3 * (lines[-1] + 1) * C, :]
    else:
        w = w[...]
    return mm(jnp.concatenate(wins, axis=1), w, dims)


def section(
    near_ref, mid_ref, far_ref, mask_ref, gc_ref, place_ref, part1_ref, inner_ref, inner_sg1_ref, part2_ref,
    near_first_ref, near_sg1_ref, near_second_ref, near_slope_ref, w1_ref, w2_ref, back_ref, wd_ref, up_ref,
    grads_ref, out_ref,
    sides, first, sg1, second, slopes, ge, g2, gs, vt,
):
    core = lax.axis_index("c")
    sides[1 - core] = near_ref[...]
    sides[core] = far_ref[...]
    low_ref, high_ref = sides.at[0], sides.at[1]

    def cells(x, y, n):
        ref, x = ((low_ref, x), (mid_ref, x - 3), (high_ref, x - 7))[(x > 2) + (x > 6)]
        return ref[(x * 22 + y) * Z : (x * 22 + y + n) * Z, :]

    def firsts(x, y, n):
        return first[(x * 20 + y) * Z : (x * 20 + y + n) * Z, :]

    def cots(x, y, n):
        return g2[(x * 18 + y) * Z : (x * 18 + y + n) * Z, :]

    packed = low_ref[MASK:, :], mask_ref[...], high_ref[MASK:, :]
    masks = [[spread(t, by) for by in range(6)] for t in packed]

    def cotangent(u, q):
        if u in (1, 2):
            return gc_ref[u - 1, q]
        return (low_ref if u == 0 else high_ref)[COTS + q * 32 : COTS + (q + 1) * 32, :]

    def line(x, y0, cells):
        return jnp.concatenate(
            [masks[(x + 4) // 4][(y + 4) // 4] for y in range(y0, y0 + cells)], axis=0
        )

    def weight_grad(get, x0, y0, rows, put):
        for j in range(3):
            for x in range(6):
                vt[j * C : (j + 1) * C, x * Y * Z : (x + 1) * Y * Z] = get(x0 + x, y0 + j, Y).T
        for i in range(3):
            p = mm(vt[:, i * Y * Z : (i + X) * Y * Z], gs[...]).astype(BF)
            for j in range(3):
                for k in range(3):
                    put(9 * i + 3 * j + k, p[j * C : j * C + rows, k * C : (k + 1) * C])

    def put_z_taps(x, g):
        at = x * Y * Z
        gs[at : at + Y * Z, 0:C] = from_above(g).astype(BF)
        gs[at : at + Y * Z, C : 2 * C] = g.astype(BF)
        gs[at : at + Y * Z, 2 * C : 3 * C] = from_below(g).astype(BF)

    first[3 * 20 * Z : 5 * 20 * Z, :] = inner_ref[...]
    sg1[Y * Z : 3 * Y * Z, :] = inner_sg1_ref[...]
    for ref, got, unit, at in (
        (first, near_first_ref, 20 * Z, 5),
        (sg1, near_sg1_ref, Y * Z, 3),
        (second, near_second_ref, Y * Z, 2),
        (slopes, near_slope_ref, 18 * Z, 3),
    ):
        at = pl.multiple_of((1 - core) * (at * unit), 16)
        ref[pl.ds(at, got.shape[0]), :] = got[...]

    def put(ref, size):
        def store(x, v):
            ref[x * size : (x + 1) * size, :] = v

        return store

    for which in range(2):
        pl.when(core == which)(
            functools.partial(
                half_forward, which == 1, cells, firsts, line, w1_ref, w2_ref, part1_ref, part2_ref,
                put(first, 20 * Z), put(sg1, Y * Z), put(second, Y * Z), put(slopes, 18 * Z),
            )
        )

    even = z_of(6 * Z) % 2 == 0
    for u in range(4):
        both = jnp.concatenate(
            [jnp.concatenate([cotangent(u, 2 * b + c) for b in range(2)], axis=1) for c in range(2)],
            axis=0,
        )
        r = mm(up_ref[...], both)
        for v in range(10):
            by, b = (v + 1) // 2, (v + 1) % 2
            t = r[by * Z : (by + 1) * Z, b * C : (b + 1) * C]
            at = (u * 10 + v) * Z
            ge[at : at + Z, 0:C] = jnp.where(even[:Z], t, 0.0).astype(BF)
            ge[at : at + Z, C : 2 * C] = jnp.where(even[:Z], 0.0, t).astype(BF)

    for x in range(6):
        u, a = (x + 1) // 2, (x + 1) % 2
        back = []
        for b in range(2):
            at = (u * 10 + 1 - b) * Z
            w = jnp.concatenate([wd_ref[4 * a + 2 * b], wd_ref[4 * a + 2 * b + 1]], axis=1)
            back.append(mm(ge[at : at + 9 * Z, :], w, NT))
        g = jnp.concatenate(
            [back[1 - y % 2][y // 2 * Z : (y // 2 + 1) * Z] for y in range(18)], axis=0
        )
        g = (g * slopes[x * 18 * Z : (x + 1) * 18 * Z, :]).astype(BF)
        g2[x * 18 * Z : (x + 1) * 18 * Z, :] = g
        if 1 <= x < 5:
            put_z_taps(x - 1, g[Z : 17 * Z].astype(F32))

    def corner(a, b):
        return jnp.concatenate(
            [
                second[((2 * u + a) * Y + 2 * v + b) * Z : ((2 * u + a) * Y + 2 * v + b + 1) * Z, :]
                for u in range(2)
                for v in range(8)
            ],
            axis=0,
        )

    corners = [corner(a, b) for a in range(2) for b in range(2)]
    wd = jnp.concatenate(
        [jnp.concatenate([wd_ref[2 * q], wd_ref[2 * q + 1]], axis=1) for q in range(4)], axis=0
    )
    p = mm(jnp.concatenate(corners, axis=1), wd)
    coarse = (lanes(p, 0) + from_above(lanes(p, 1))).astype(BF)
    row, col = iota((128, 256), 0), iota((128, 256), 1)
    a, by, b, z = col // 128, col // 32 % 4, col // 16 % 2, col % Z
    order = (row // 16 == 4 * a + 2 * b + z // 2 % 2) & (row % 16 == by * 4 + z // 4) & (z % 2 == 0)
    bricks = mm(one(order), coarse).astype(BF)
    place = jnp.concatenate([place_ref[...].astype(F32)] * 8, axis=0)
    place = jnp.concatenate([place] * 2, axis=1)
    target = (8 * (col // 16) + col % 2).astype(F32)
    out_ref[...] = mm(one((place == target) & (row // 16 == col // 2 % 8)), bricks, TN).astype(BF)

    gec = jnp.concatenate([ge[(u * 10 + 1) * Z : (u * 10 + 9) * Z, :] for u in (1, 2)], axis=0)

    def put_a(at, v):
        grads_ref[core, at : at + v.shape[0], :] = v

    def put_b(at, v):
        grads_ref[1 - core, at : at + v.shape[0], :] = v

    for q in range(4):
        r = mm(corners[q], gec, TN).astype(BF)
        for c in range(2):
            t = 2 * q + c
            if t == 0:
                put_a(27 * C, lanes(r, c))
            else:
                put_b(27 * CIN + (t - 1) * C, lanes(r, c))
    put_b(27 * CIN + 7 * C, jnp.zeros((HALF - 27 * CIN - 7 * C, C), BF))
    weight_grad(firsts, 1, 1, C, lambda t, v: put_a(t * C, v))

    for x in range(X):
        p = taps(cots, x, Y, back_ref, NT, flip=True)
        g = lanes(p, 1) + from_above(lanes(p, 0)) + from_below(lanes(p, 2))
        g = g + cots(x + 1, 1, Y).astype(F32)
        g = (g * sg1[x * Y * Z : (x + 1) * Y * Z, :]).astype(BF)
        put_z_taps(x, g.astype(F32))
    weight_grad(cells, 2, 2, CIN, lambda t, v: put_b(t * CIN, v))


VM = pl.BlockSpec(memory_space=pltpu.VMEM)


def call(kernel, outs, args, in_specs=None, scratch=(), flops=10_000_000, vmem=40 << 20, out_specs=None, aliases={}):
    return pl.pallas_call(
        kernel,
        out_shape=tuple(jax.ShapeDtypeStruct(shape, dtype) for shape, dtype in outs),
        in_specs=in_specs or [VM] * len(args),
        out_specs=tuple(out_specs or [VM] * len(outs)),
        input_output_aliases=aliases,
        scratch_shapes=[pltpu.VMEM(*s) if isinstance(s, tuple) else s for s in scratch],
        compiler_params=pltpu.CompilerParams(vmem_limit_bytes=vmem),
        cost_estimate=pl.CostEstimate(
            flops=flops, bytes_accessed=1_000_000, transcendentals=0
        ),
    )(*args)


def arrange(w1_ref, w2_ref, after_ref, first_ref, second_ref, back_ref):
    for m in range(9):
        for k in range(3):
            first_ref[m * C : m * C + CIN, k * C : (k + 1) * C] = w1_ref[3 * m + k]
            second_ref[m * C : (m + 1) * C, k * C : (k + 1) * C] = w2_ref[3 * m + k]
            back_ref[k * C : (k + 1) * C, m * C : (m + 1) * C] = w2_ref[3 * m + k]
        first_ref[m * C + CIN : (m + 1) * C, :] = jnp.zeros((C - CIN, 3 * C), BF)


def half_forward(
    high, cells, firsts, act, w1_ref, w2_ref, part1_ref, part2_ref, put_first, put_sg1, put_second, put_slope
):
    for x in (5, 6, 7) if high else (0, 1, 2):
        p = taps(cells, x, 20, w1_ref, lines=[i for i in range(3) if not 3 <= x + i < 7])
        pre = lanes(p, 1) + from_below(lanes(p, 0)) + from_above(lanes(p, 2))
        if x in EARLY:
            pre = pre + part1_ref[EARLY[x]]
        on = act(x - 2, -2, 20)
        value, slope = silu(on * pre)
        put_first(x, value.astype(BF))
        if x in (2, 5):
            put_sg1(x - 2, (on * slope)[2 * Z : 18 * Z])
    for x in (3, 4, 5) if high else (0, 1, 2):
        p = taps(firsts, x, 18, w2_ref, lines=[i for i in range(3) if not 3 <= x + i < 5])
        on = act(x - 1, -1, 18)
        pre = lanes(p, 1) + from_below(lanes(p, 0)) + from_above(lanes(p, 2))
        if 1 <= x < 5:
            pre = pre + part2_ref[x - 1]
        value, slope = silu(on * pre + firsts(x + 1, 1, 18).astype(F32))
        if 1 <= x < 5:
            put_second(x - 1, value[Z : 17 * Z].astype(BF))
        put_slope(x, on * slope)


def near_side(
    near_ref, mask_ref, part1_ref, inner_ref, part2_ref, w1_ref, w2_ref,
    first_ref, sg1_ref, second_ref, slope_ref,
):
    def run(high):
        base = 5 if high else 0
        tiles = near_ref[MASK:, :], mask_ref[...]
        masks = [[spread(t, by) for by in range(6)] for t in tiles]

        def cells(x, y, n):
            x = x - 7 if high else x
            return near_ref[(x * 22 + y) * Z : (x * 22 + y + n) * Z, :]

        def firsts(x, y, n):
            ref, x = (inner_ref, x - 3) if x in (3, 4) else (first_ref, x - base)
            return ref[(x * 20 + y) * Z : (x * 20 + y + n) * Z, :]

        def act(x, y0, n):
            here = masks[1 if (x + 4) // 4 == 1 else 0]
            return jnp.concatenate([here[(y + 4) // 4] for y in range(y0, y0 + n)], axis=0)

        def put(ref, size, start):
            def store(x, v):
                ref[(x - start) * size : (x - start + 1) * size, :] = v

            return store

        half_forward(
            high, cells, firsts, act, w1_ref, w2_ref, part1_ref, part2_ref,
            put(first_ref, 20 * Z, base), put(sg1_ref, Y * Z, 3 if high else 0),
            put(second_ref, Y * Z, 2 if high else 0), put(slope_ref, 18 * Z, 3 if high else 0),
        )

    for core in range(2):
        pl.when(lax.axis_index("c") == core)(functools.partial(run, core == 0))


def begin(mid_ref, mask_ref, w1_ref, w2_ref, part1_ref, first_ref, sg1_ref, part2_ref):
    def cells(x, y, n):
        return mid_ref[((x - 3) * 22 + y) * Z : ((x - 3) * 22 + y + n) * Z, :]

    def firsts(x, y, n):
        return first_ref[((x - 3) * 20 + y) * Z : ((x - 3) * 20 + y + n) * Z, :]

    masks = [spread(mask_ref[...], by) for by in range(6)]
    act = jnp.concatenate([masks[(y + 4) // 4] for y in range(-2, 18)], axis=0)
    for x in (3, 4, 1, 2, 5, 6):
        p = taps(cells, x, 20, w1_ref, lines=[i for i in range(3) if 3 <= x + i < 7])
        pre = lanes(p, 1) + from_below(lanes(p, 0)) + from_above(lanes(p, 2))
        if x in (3, 4):
            value, slope = silu(act * pre)
            first_ref[(x - 3) * 20 * Z : (x - 2) * 20 * Z, :] = value.astype(BF)
            sg1_ref[(x - 3) * Y * Z : (x - 2) * Y * Z, :] = (act * slope)[2 * Z : 18 * Z]
        else:
            part1_ref[EARLY[x]] = pre
    for x in range(1, 5):
        p = taps(firsts, x, 18, w2_ref, lines=[i for i in range(3) if 3 <= x + i < 5])
        part2_ref[x - 1] = lanes(p, 1) + from_below(lanes(p, 0)) + from_above(lanes(p, 2))


def prepare(
    grad_hbm, feat_hbm, blocks_hbm, owners_hbm, rows_ref, own_ref, near_ref, far_ref,
    wide, grad_ref, feat_ref, blocks_ref, owners_ref, sems,
):
    copies = [
        pltpu.make_async_copy(a, b, sems.at[n])
        for n, (a, b) in enumerate(
            ((grad_hbm, grad_ref), (feat_hbm, feat_ref), (blocks_hbm, blocks_ref), (owners_hbm, owners_ref))
        )
    ]
    for c in copies:
        c.start()
    copies[0].wait()
    row, col = iota((128, 32), 0), iota((128, 32), 1)
    take = one((col == 2 * (row // 8) - 2 + row % 8) & (row % 8 < 6))
    rows_ref[...] = mm(take, grad_ref[0, 0]).astype(BF)
    for c in copies[1:]:
        c.wait()
    lane = iota((Y, C), 1)
    for x in range(X):
        f = feat_ref[x].astype(F32)
        f = jnp.concatenate([f, jnp.zeros((Y, C), F32)], axis=1)
        for z in range(Z):
            t = jnp.where(lane < CIN, f[:, z * CIN : z * CIN + C], 0.0)
            wide[pl.ds(x * Y * Z + z, Y, stride=Z), :] = t
    blocks = blocks_ref[0].astype(F32)
    mine = iota((Z, 4), 0) // 4 == iota((Z, 4), 1)
    for by in range(4):
        m = jnp.sum(jnp.where(mine, blocks[by : by + 1, :], 0.0), axis=1, keepdims=True)
        m = jnp.broadcast_to(m, (Z, C))
        own_ref[OWN + by * Z : OWN + (by + 1) * Z, :] = m.astype(BF)
        for x in range(X):
            for y in range(4 * by, 4 * by + 4):
                at = (x * Y + y) * Z
                own_ref[at : at + Z, :] = (wide[at : at + Z, :] * m).astype(BF)
    row, col = iota((16, 16), 0), iota((16, 16), 1)
    across = jnp.broadcast_to(owners_ref[...].astype(F32), (16, 16))
    dest = jnp.sum(jnp.where(row == col, across, 0.0), axis=1, keepdims=True)
    rank = jnp.sum(jnp.where((col < row) & (dest == across), 1.0, 0.0), axis=1, keepdims=True)
    place = jnp.broadcast_to(dest * 8.0 + rank, (16, C)).astype(BF)
    own_ref[OWN + 4 * Z : OWN + 5 * Z, :] = place

    def fill(up, down):
        for x in range(X):
            up[x * 3 * Z : (x + 1) * 3 * Z, :] = own_ref[(x * Y + 13) * Z : (x + 1) * Y * Z, :]
            down[x * 3 * Z : (x + 1) * 3 * Z, :] = own_ref[x * Y * Z : (x * Y + 3) * Z, :]
        for ref, by in ((up, 3), (down, 0)):
            ref[192:208, :] = place
            ref[208:224, :] = own_ref[OWN + by * Z : OWN + (by + 1) * Z, :]

    @pl.when(lax.rem(lax.axis_index("x"), 2) == 0)
    def _():
        fill(near_ref, far_ref)

    @pl.when(lax.rem(lax.axis_index("x"), 2) == 1)
    def _():
        fill(far_ref, near_ref)


def widen(
    own_ref, beside_ref, beyond_ref, rows_ref, after_ref,
    mid_ref, mask_ref, gc_ref, place_ref, near_ref, far_ref,
    sides,
):
    odd = lax.rem(lax.axis_index("x"), 2)
    sides[1 - odd] = beside_ref[...]
    sides[odd] = beyond_ref[...]
    low_ref, high_ref = sides.at[0], sides.at[1]
    for x in range(X):
        at = x * 22 * Z
        mid_ref[at : at + 3 * Z, :] = low_ref[x * 3 * Z : (x + 1) * 3 * Z, :]
        mid_ref[at + 3 * Z : at + 19 * Z, :] = own_ref[x * Y * Z : (x + 1) * Y * Z, :]
        mid_ref[at + 19 * Z : at + 22 * Z, :] = high_ref[x * 3 * Z : (x + 1) * 3 * Z, :]
    tiles = [low_ref[208:224, :]]
    tiles += [own_ref[OWN + by * Z : OWN + (by + 1) * Z, :] for by in range(4)]
    tiles += [high_ref[208:224, :]]
    which = iota((Z, C), 1) // 16
    packed = jnp.zeros((Z, C), F32)
    for by in range(6):
        packed = jnp.where(which == by, tiles[by].astype(F32), packed)
    mask_ref[...] = packed.astype(BF)
    place_ref[...] = own_ref[OWN + 4 * Z : OWN + 5 * Z, :]
    place = jnp.concatenate(
        [
            low_ref[192:208, :].astype(F32),
            own_ref[OWN + 4 * Z : OWN + 5 * Z, :].astype(F32) + 2.0,
            high_ref[192:208, :].astype(F32) + 4.0,
        ],
        axis=0,
    )
    bricks = mm(one(place == iota((48, C), 1).astype(F32)), rows_ref[...])[12:44].astype(BF)
    for q in range(8):
        gc_ref[q // 4, q % 4] = lanes(bricks, q)

    def fill(up, down):
        for q in range(4):
            up[COTS + q * 32 : COTS + (q + 1) * 32, :] = lanes(bricks, 4 + q)
            down[COTS + q * 32 : COTS + (q + 1) * 32, :] = lanes(bricks, q)
        up[0:COTS, :] = mid_ref[22 * Z :, :]
        down[0:COTS, :] = mid_ref[0:COTS, :]
        for ref in (up, down):
            ref[MASK:, :] = mask_ref[...]

    @pl.when(lax.axis_index("c") == 0)
    def _():
        fill(near_ref, far_ref)

    @pl.when(lax.axis_index("c") == 1)
    def _():
        fill(far_ref, near_ref)


def places():
    core, z, x = lax.axis_index("c"), lax.axis_index("z"), lax.axis_index("x")
    pick = lambda a, b: jnp.where(core == 0, a, b)
    return pick(z, x), pick(x, z), pick(4, 1), pick(1, 4)


def fold_cores(grads_ref, theirs_ref, bricks_ref, *out_refs):
    first, _, a, b = places()
    for n, out in enumerate(out_refs):
        for t in range(4):
            to = (first ^ n) * a + t * b
            rows = pl.ds(pl.multiple_of(to * PART, 16), PART)
            out[t * PART : (t + 1) * PART, :] = (
                grads_ref[0, rows, :].astype(F32) + theirs_ref[rows, :].astype(F32)
            ).astype(BF)
            rows = pl.ds(pl.multiple_of(to * 16, 16), 16)
            out[4 * PART + t * 16 : 4 * PART + (t + 1) * 16, :] = bricks_ref[rows, :]


def fold_first(*refs):
    got, outs = [refs[i] for i in (0, 1, 3, 2)], refs[4:]
    _, second, _, _ = places()
    for m, out in enumerate(outs):
        to = second ^ m
        rows = pl.ds(pl.multiple_of(to * PART, 16), PART)
        v = [g[rows, :].astype(F32) for g in got]
        out[:PART, :] = ((v[0] + v[1]) + (v[2] + v[3])).astype(BF)
        rows = pl.ds(pl.multiple_of(4 * PART + to * 16, 16), 16)
        for n, g in enumerate(got):
            out[PART + n * 16 : PART + (n + 1) * 16, :] = g[rows, :]


def fold_second(*refs):
    got, (part_ref, bricks_ref) = [refs[i] for i in (0, 1, 3, 2)], refs[4:]
    first, second, a, b = places()
    v = [g[:PART, :].astype(F32) for g in got]
    part_ref[...] = ((v[0] + v[1]) + (v[2] + v[3])).astype(BF)
    for m, g in enumerate(got):
        for n in range(4):
            at = pl.multiple_of(((first ^ n) * a + (second ^ m) * b) * 16, 16)
            bricks_ref[pl.ds(at, 16), :] = g[PART + n * 16 : PART + (n + 1) * 16, :]


def unfold(half_ref, core, first_hbm, second_hbm, down_hbm, wide, sems):
    spans = {
        0: ((0, 27 * C, second_hbm, 0), (27 * C, 28 * C, down_hbm, 0)),
        1: ((0, 27 * CIN, first_hbm, 0), (27 * CIN, 27 * CIN + 7 * C, down_hbm, C)),
    }

    def emit(which):
        copies = []
        for lo, hi, out, to in spans[which]:
            step = 864 if hi - lo > 1024 else hi - lo
            for at in range(lo, hi, step):
                wide[at : at + step, :] = half_ref[at : at + step, :].astype(F32)
                copies.append(
                    pltpu.make_async_copy(
                        wide.at[pl.ds(at, step)],
                        out.at[pl.ds(to + at - lo, step)],
                        sems.at[len(copies)],
                    )
                )
                copies[-1].start()
        for c in copies:
            c.wait()

    for which in range(2):
        pl.when(core == which)(functools.partial(emit, which))


def unfold_own(half_ref, first_hbm, second_hbm, down_hbm, wide, sems):
    unfold(half_ref, lax.axis_index("c"), first_hbm, second_hbm, down_hbm, wide, sems)


def unfold_other(half_ref, a, b, c, first_hbm, second_hbm, down_hbm, wide, sems):
    unfold(half_ref, 1 - lax.axis_index("c"), first_hbm, second_hbm, down_hbm, wide, sems)


def swap(v, axes, first):
    n = lax.axis_size(axes)
    pairs = [(i, i + 1) for i in range(first, n - 1, 2)]
    return lax.ppermute(v, axes, pairs + [(j, i) for i, j in pairs])


def swap_cores(v):
    return lax.ppermute(v, "c", [(0, 1), (1, 0)])


def up_matrix():
    m = np.zeros((6 * Z, 64), np.float32)
    for by in range(6):
        for z in range(Z):
            m[by * Z + z, z // 2 % 2 * 32 + by * 4 + z // 4] = 1
    return jnp.asarray(m, BF)


def flip(v, axis, bits):
    return lax.ppermute(v, axis, [(i, i ^ bits) for i in range(lax.axis_size(axis))])


def flip_by_core(v, axes, bits):
    every = ("c", "z", "x")
    size = [lax.axis_size(n) for n in every]
    pairs = []
    for d in range(size[0] * size[1] * size[2]):
        at = [int(i) for i in np.unravel_index(d, size)]
        at[every.index(axes[at[0]])] ^= bits
        pairs.append((d, int(np.ravel_multi_index(at, size))))
    return lax.ppermute(v, every, pairs)


def per_device(features, block_mask, weight_first, weight_second, weight_down, owners, moved_grad):
    rows, own, beside, beyond = call(
        prepare,
        [((128, 8 * C), BF), ((X * Y * Z + 80, C), BF), ((224, C), BF), ((224, C), BF)],
        (moved_grad, features, block_mask, owners.reshape(1, 16)),
        [pl.BlockSpec(memory_space=pltpu.HBM)] * 4,
        [
            ((X * Y * Z, C), F32),
            (moved_grad.shape, BF),
            (features.shape, BF),
            (block_mask.shape, jnp.int32),
            ((1, 16), jnp.int32),
            pltpu.SemaphoreType.DMA((4,)),
        ],
        vmem=60 << 20,
    )
    beyond, beside = swap(beyond, GY, 1), swap(beside, GY, 0)
    w1, w2, back = call(
        arrange,
        [((9 * C, 3 * C), BF), ((9 * C, 3 * C), BF), ((3 * C, 9 * C), BF)],
        (weight_first, weight_second, own),
        flops=2_000_000_000,
    )
    rows = lax.all_to_all(rows, GY, 0, 0, tiled=True)

    mid, mask, gc, place, near, far = call(
        widen,
        [((4 * 22 * Z, C), BF), ((16, C), BF), ((2, 4, 32, C), BF), ((16, C), BF), ((STRIP, C), BF), ((STRIP, C), BF)],
        (own, beside, beyond, rows, w1),
        [VM] * 4 + [pl.BlockSpec(memory_space=pl.ANY)],
        scratch=[((2, 224, C), BF)],
    )
    far, near = swap(far, GX, 1), swap(near, GX, 0)
    ahead = call(
        begin,
        [((4, 20 * Z, C), F32), ((40 * Z, C), BF), ((2 * Y * Z, C), F32), ((4, 18 * Z, C), F32)],
        (mid, mask, w1, w2),
        flops=3_000_000_000,
    )

    part1, inner, _, part2 = ahead
    beside = call(
        near_side,
        [((60 * Z, C), BF), ((Y * Z, C), F32), ((2 * Y * Z, C), BF), ((3 * 18 * Z, C), F32)],
        (near, mask, part1, inner, part2, w1, w2),
        flops=3_000_000_000,
    )
    grads, outgoing = call(
        section,
        [((2, HALF, C), BF), ((256, C), BF)],
        (near, mid, far, mask, gc, place, *ahead, *beside, w1, w2, back, weight_down, up_matrix()),
        scratch=[
            ((2, STRIP, C), BF),
            ((8 * 20 * Z, C), BF),
            ((X * Y * Z, C), F32),
            ((X * Y * Z, C), BF),
            ((6 * 18 * Z, C), F32),
            ((40 * Z, 2 * C), BF),
            ((6 * 18 * Z, C), BF),
            ((X * Y * Z, 3 * C), BF),
            ((3 * C, 6 * Y * Z), BF),
        ],
        flops=8_000_000_000,
    )

    blocks = call(
        fold_cores, [((4 * PART + 64, C), BF)] * 4, (grads, swap_cores(grads[1]), outgoing)
    )
    far = flip_by_core(blocks[2], ("z", "x"), 2)
    blocks = [blocks[0]] + [flip_by_core(blocks[n], ("z", "x"), n) for n in (1, 3)] + [far]
    blocks = call(fold_first, [((PART + 64, C), BF)] * 4, blocks)
    far = flip_by_core(blocks[2], ("x", "z"), 2)
    blocks = [blocks[0]] + [flip_by_core(blocks[n], ("x", "z"), n) for n in (1, 3)] + [far]
    part, arrived = call(fold_second, [((PART, C), BF), ((256, C), BF)], blocks)
    moved = arrived.reshape(16, 8, 2, C).transpose(0, 2, 1, 3).reshape(1, 1, 32, 8 * C)
    others = [flip(part, "y", n).astype(F32) for n in (1, 2, 3)]
    part = ((part.astype(F32) + others[0]) + (others[1] + others[2])).astype(BF)
    part = lax.all_to_all(jnp.broadcast_to(part[None], (16, PART, C)), GY, 0, 0, tiled=True)
    part = part.reshape(HALF, C)
    grads = [((27 * CIN, C), F32), ((27 * C, C), F32), ((8 * C, C), F32)]
    scratch = [((HALF, C), F32), pltpu.SemaphoreType.DMA((5,))]
    hbm = pl.BlockSpec(memory_space=pl.ANY)
    other = swap_cores(part)
    grads_own = call(unfold_own, grads, (part,), [VM], scratch, out_specs=[hbm] * 3)
    grad_first, grad_second, grad_down = call(
        unfold_other, grads, (other, *grads_own), [VM] + [hbm] * 3, scratch, out_specs=[hbm] * 3,
        aliases={1: 0, 2: 1, 3: 2},
    )
    return (
        moved,
        grad_first.reshape(27, CIN, C),
        grad_second.reshape(27, C, C),
        grad_down.reshape(8, C, C),
    )


def solution(mesh):
    shape = dict(mesh.shape)
    fine = Mesh(
        mesh.devices.reshape(shape["gx"] // 2, 2, 4, shape["gy"] // 4), ("y", "c", "z", "x")
    )
    whole, tiles = P(GX, GY, None), P(GX, GY, None, None)
    return jax.shard_map(
        per_device,
        mesh=fine,
        in_specs=(whole, whole, P(), P(), P(), tiles, tiles),
        out_specs=(tiles, P(), P(), P()),
        check_vma=False,
    )
```

```python
import functools

import jax
import jax.numpy as jnp
import numpy as np
from jax import lax
from jax.experimental import pallas as pl
from jax.experimental.pallas import tpu as pltpu
from jax.sharding import Mesh, PartitionSpec as P

GX, GY = ("y", "c"), ("z", "x")
F32, BF = jnp.float32, jnp.bfloat16
X, Y, Z, C, CIN = 4, 16, 16, 128, 96
HALF, PART = 3584, 224
OWN = 1024
COTS, MASK, STRIP = 1056, 1184, 1200
EARLY = {1: 0, 2: 1, 5: 2, 6: 3}
NN = (((1,), (0,)), ((), ()))
NT = (((1,), (1,)), ((), ()))
TN = (((0,), (0,)), ((), ()))


def mm(a, b, dims=NN):
    return lax.dot_general(a, b, dims, preferred_element_type=F32)


def iota(shape, axis):
    return lax.broadcasted_iota(jnp.int32, shape, axis)


def one(where):
    return jnp.where(where, 1.0, 0.0).astype(BF)


def z_of(rows):
    return iota((rows, C), 0) % Z


def from_above(v):
    return jnp.where(z_of(v.shape[0]) < Z - 1, pltpu.roll(v, v.shape[0] - 1, 0), 0.0)


def from_below(v):
    return jnp.where(z_of(v.shape[0]) > 0, pltpu.roll(v, 1, 0), 0.0)


def lanes(p, k):
    return p[:, k * C : (k + 1) * C]


def silu(v):
    s = jax.nn.sigmoid(v)
    return v * s, s * (1.0 + v * (1.0 - s))


def spread(packed, by):
    return jnp.broadcast_to(packed[:, 16 * by : 16 * by + 1].astype(F32), (Z, C))


def taps(get, x, n, w, dims=NN, flip=False, lines=(0, 1, 2)):
    wins = []
    for i in lines:
        for j in range(3):
            wins.append(get(x + 2 - i, 2 - j, n) if flip else get(x + i, j, n))
    if len(lines) < 3:
        w = w[3 * lines[0] * C : 3 * (lines[-1] + 1) * C, :]
    else:
        w = w[...]
    return mm(jnp.concatenate(wins, axis=1), w, dims)


def section(
    near_ref, mid_ref, far_ref, mask_ref, own_ge_ref, place_ref, part1_ref, inner_ref, inner_sg1_ref, part2_ref,
    near_first_ref, near_sg1_ref, near_second_ref, near_slope_ref, w1_ref, w2_ref, back_ref, wd_ref, up_ref,
    grads_ref, out_ref,
    sides, first, sg1, second, slopes, ge, g2, gs, vt,
):
    core = lax.axis_index("c")
    sides[1 - core] = near_ref[...]
    sides[core] = far_ref[...]
    low_ref, high_ref = sides.at[0], sides.at[1]

    def cells(x, y, n):
        ref, x = ((low_ref, x), (mid_ref, x - 3), (high_ref, x - 7))[(x > 2) + (x > 6)]
        return ref[(x * 22 + y) * Z : (x * 22 + y + n) * Z, :]

    def firsts(x, y, n):
        return first[(x * 20 + y) * Z : (x * 20 + y + n) * Z, :]

    def cots(x, y, n):
        return g2[(x * 18 + y) * Z : (x * 18 + y + n) * Z, :]

    packed = low_ref[MASK:, :], mask_ref[...], high_ref[MASK:, :]
    masks = [[spread(t, by) for by in range(6)] for t in packed]

    def cotangent(u, q):
        return (low_ref if u == 0 else high_ref)[COTS + q * 32 : COTS + (q + 1) * 32, :]

    def line(x, y0, cells):
        return jnp.concatenate(
            [masks[(x + 4) // 4][(y + 4) // 4] for y in range(y0, y0 + cells)], axis=0
        )

    def weight_grad(get, x0, y0, rows, put):
        for j in range(3):
            for x in range(6):
                vt[j * C : (j + 1) * C, x * Y * Z : (x + 1) * Y * Z] = get(x0 + x, y0 + j, Y).T
        for i in range(3):
            p = mm(vt[:, i * Y * Z : (i + X) * Y * Z], gs[...]).astype(BF)
            for j in range(3):
                for k in range(3):
                    put(9 * i + 3 * j + k, p[j * C : j * C + rows, k * C : (k + 1) * C])

    def put_z_taps(x, g):
        at = x * Y * Z
        gs[at : at + Y * Z, 0:C] = from_above(g).astype(BF)
        gs[at : at + Y * Z, C : 2 * C] = g.astype(BF)
        gs[at : at + Y * Z, 2 * C : 3 * C] = from_below(g).astype(BF)

    first[3 * 20 * Z : 5 * 20 * Z, :] = inner_ref[...]
    sg1[Y * Z : 3 * Y * Z, :] = inner_sg1_ref[...]
    for ref, got, unit, at in (
        (first, near_first_ref, 20 * Z, 5),
        (sg1, near_sg1_ref, Y * Z, 3),
        (second, near_second_ref, Y * Z, 2),
        (slopes, near_slope_ref, 18 * Z, 3),
    ):
        at = pl.multiple_of((1 - core) * (at * unit), 16)
        ref[pl.ds(at, got.shape[0]), :] = got[...]

    def put(ref, size):
        def store(x, v):
            ref[x * size : (x + 1) * size, :] = v

        return store

    for which in range(2):
        pl.when(core == which)(
            functools.partial(
                half_forward, which == 1, cells, firsts, line, w1_ref, w2_ref, part1_ref, part2_ref,
                put(first, 20 * Z), put(sg1, Y * Z), put(second, Y * Z), put(slopes, 18 * Z),
            )
        )

    for u in (0, 3):
        repeat_along_z([cotangent(u, q) for q in range(4)], up_ref, ge, u * 160)
    ge[160:480, :] = own_ge_ref[...]

    for x in range(6):
        u, a = (x + 1) // 2, (x + 1) % 2
        back = []
        for b in range(2):
            at = (u * 10 + 1 - b) * Z
            w = jnp.concatenate([wd_ref[4 * a + 2 * b], wd_ref[4 * a + 2 * b + 1]], axis=1)
            back.append(mm(ge[at : at + 9 * Z, :], w, NT))
        g = jnp.concatenate(
            [back[1 - y % 2][y // 2 * Z : (y // 2 + 1) * Z] for y in range(18)], axis=0
        )
        g = (g * slopes[x * 18 * Z : (x + 1) * 18 * Z, :]).astype(BF)
        g2[x * 18 * Z : (x + 1) * 18 * Z, :] = g
        if 1 <= x < 5:
            put_z_taps(x - 1, g[Z : 17 * Z].astype(F32))

    def corner(a, b):
        return jnp.concatenate(
            [
                second[((2 * u + a) * Y + 2 * v + b) * Z : ((2 * u + a) * Y + 2 * v + b + 1) * Z, :]
                for u in range(2)
                for v in range(8)
            ],
            axis=0,
        )

    corners = [corner(a, b) for a in range(2) for b in range(2)]
    wd = jnp.concatenate(
        [jnp.concatenate([wd_ref[2 * q], wd_ref[2 * q + 1]], axis=1) for q in range(4)], axis=0
    )
    p = mm(jnp.concatenate(corners, axis=1), wd)
    coarse = (lanes(p, 0) + from_above(lanes(p, 1))).astype(BF)
    row, col = iota((128, 256), 0), iota((128, 256), 1)
    a, by, b, z = col // 128, col // 32 % 4, col // 16 % 2, col % Z
    order = (row // 16 == 4 * a + 2 * b + z // 2 % 2) & (row % 16 == by * 4 + z // 4) & (z % 2 == 0)
    bricks = mm(one(order), coarse).astype(BF)
    place = jnp.concatenate([place_ref[...].astype(F32)] * 8, axis=0)
    place = jnp.concatenate([place] * 2, axis=1)
    target = (8 * (col // 16) + col % 2).astype(F32)
    out_ref[...] = mm(one((place == target) & (row // 16 == col // 2 % 8)), bricks, TN).astype(BF)

    gec = jnp.concatenate([ge[(u * 10 + 1) * Z : (u * 10 + 9) * Z, :] for u in (1, 2)], axis=0)

    def put_a(at, v):
        grads_ref[core, at : at + v.shape[0], :] = v

    def put_b(at, v):
        grads_ref[1 - core, at : at + v.shape[0], :] = v

    for q in range(4):
        r = mm(corners[q], gec, TN).astype(BF)
        for c in range(2):
            t = 2 * q + c
            if t == 0:
                put_a(27 * C, lanes(r, c))
            else:
                put_b(27 * CIN + (t - 1) * C, lanes(r, c))
    put_b(27 * CIN + 7 * C, jnp.zeros((HALF - 27 * CIN - 7 * C, C), BF))
    weight_grad(firsts, 1, 1, C, lambda t, v: put_a(t * C, v))

    for x in range(X):
        p = taps(cots, x, Y, back_ref, NT, flip=True)
        g = lanes(p, 1) + from_above(lanes(p, 0)) + from_below(lanes(p, 2))
        g = g + cots(x + 1, 1, Y).astype(F32)
        g = (g * sg1[x * Y * Z : (x + 1) * Y * Z, :]).astype(BF)
        put_z_taps(x, g.astype(F32))
    weight_grad(cells, 2, 2, CIN, lambda t, v: put_b(t * CIN, v))


VM = pl.BlockSpec(memory_space=pltpu.VMEM)


def call(kernel, outs, args, in_specs=None, scratch=(), flops=10_000_000, vmem=40 << 20, out_specs=None, aliases={}):
    return pl.pallas_call(
        kernel,
        out_shape=tuple(jax.ShapeDtypeStruct(shape, dtype) for shape, dtype in outs),
        in_specs=in_specs or [VM] * len(args),
        out_specs=tuple(out_specs or [VM] * len(outs)),
        input_output_aliases=aliases,
        scratch_shapes=[pltpu.VMEM(*s) if isinstance(s, tuple) else s for s in scratch],
        compiler_params=pltpu.CompilerParams(vmem_limit_bytes=vmem),
        cost_estimate=pl.CostEstimate(
            flops=flops, bytes_accessed=1_000_000, transcendentals=0
        ),
    )(*args)


def arrange(w1_ref, w2_ref, after_ref, first_ref, second_ref, back_ref):
    for m in range(9):
        for k in range(3):
            first_ref[m * C : m * C + CIN, k * C : (k + 1) * C] = w1_ref[3 * m + k]
            second_ref[m * C : (m + 1) * C, k * C : (k + 1) * C] = w2_ref[3 * m + k]
            back_ref[k * C : (k + 1) * C, m * C : (m + 1) * C] = w2_ref[3 * m + k]
        first_ref[m * C + CIN : (m + 1) * C, :] = jnp.zeros((C - CIN, 3 * C), BF)


def half_forward(
    high, cells, firsts, act, w1_ref, w2_ref, part1_ref, part2_ref, put_first, put_sg1, put_second, put_slope
):
    for x in (5, 6, 7) if high else (0, 1, 2):
        p = taps(cells, x, 20, w1_ref, lines=[i for i in range(3) if not 3 <= x + i < 7])
        pre = lanes(p, 1) + from_below(lanes(p, 0)) + from_above(lanes(p, 2))
        if x in EARLY:
            pre = pre + part1_ref[EARLY[x]]
        on = act(x - 2, -2, 20)
        value, slope = silu(on * pre)
        put_first(x, value.astype(BF))
        if x in (2, 5):
            put_sg1(x - 2, (on * slope)[2 * Z : 18 * Z])
    for x in (3, 4, 5) if high else (0, 1, 2):
        p = taps(firsts, x, 18, w2_ref, lines=[i for i in range(3) if not 3 <= x + i < 5])
        on = act(x - 1, -1, 18)
        pre = lanes(p, 1) + from_below(lanes(p, 0)) + from_above(lanes(p, 2))
        if 1 <= x < 5:
            pre = pre + part2_ref[x - 1]
        value, slope = silu(on * pre + firsts(x + 1, 1, 18).astype(F32))
        if 1 <= x < 5:
            put_second(x - 1, value[Z : 17 * Z].astype(BF))
        put_slope(x, on * slope)


def near_side(
    near_ref, mask_ref, part1_ref, inner_ref, part2_ref, w1_ref, w2_ref,
    first_ref, sg1_ref, second_ref, slope_ref,
):
    def run(high):
        base = 5 if high else 0
        tiles = near_ref[MASK:, :], mask_ref[...]
        masks = [[spread(t, by) for by in range(6)] for t in tiles]

        def cells(x, y, n):
            x = x - 7 if high else x
            return near_ref[(x * 22 + y) * Z : (x * 22 + y + n) * Z, :]

        def firsts(x, y, n):
            ref, x = (inner_ref, x - 3) if x in (3, 4) else (first_ref, x - base)
            return ref[(x * 20 + y) * Z : (x * 20 + y + n) * Z, :]

        def act(x, y0, n):
            here = masks[1 if (x + 4) // 4 == 1 else 0]
            return jnp.concatenate([here[(y + 4) // 4] for y in range(y0, y0 + n)], axis=0)

        def put(ref, size, start):
            def store(x, v):
                ref[(x - start) * size : (x - start + 1) * size, :] = v

            return store

        half_forward(
            high, cells, firsts, act, w1_ref, w2_ref, part1_ref, part2_ref,
            put(first_ref, 20 * Z, base), put(sg1_ref, Y * Z, 3 if high else 0),
            put(second_ref, Y * Z, 2 if high else 0), put(slope_ref, 18 * Z, 3 if high else 0),
        )

    for core in range(2):
        pl.when(lax.axis_index("c") == core)(functools.partial(run, core == 0))


def repeat_along_z(cots, up_ref, out_ref, at):
    both = jnp.concatenate(
        [jnp.concatenate([cots[2 * b + c] for b in range(2)], axis=1) for c in range(2)], axis=0
    )
    r = mm(up_ref[...], both)
    even = z_of(Z) % 2 == 0
    for v in range(10):
        by, b = (v + 1) // 2, (v + 1) % 2
        t = r[by * Z : (by + 1) * Z, b * C : (b + 1) * C]
        rows = slice(at + v * Z, at + (v + 1) * Z)
        out_ref[rows, 0:C] = jnp.where(even, t, 0.0).astype(BF)
        out_ref[rows, C : 2 * C] = jnp.where(even, 0.0, t).astype(BF)


def begin(
    mid_ref, mask_ref, w1_ref, w2_ref, gc_ref, up_ref,
    part1_ref, first_ref, sg1_ref, part2_ref, ge_ref,
):
    def cells(x, y, n):
        return mid_ref[((x - 3) * 22 + y) * Z : ((x - 3) * 22 + y + n) * Z, :]

    def firsts(x, y, n):
        return first_ref[((x - 3) * 20 + y) * Z : ((x - 3) * 20 + y + n) * Z, :]

    for u in range(2):
        repeat_along_z([gc_ref[u, q] for q in range(4)], up_ref, ge_ref, u * 160)
    masks = [spread(mask_ref[...], by) for by in range(6)]
    act = jnp.concatenate([masks[(y + 4) // 4] for y in range(-2, 18)], axis=0)
    for x in (3, 4, 1, 2, 5, 6):
        p = taps(cells, x, 20, w1_ref, lines=[i for i in range(3) if 3 <= x + i < 7])
        pre = lanes(p, 1) + from_below(lanes(p, 0)) + from_above(lanes(p, 2))
        if x in (3, 4):
            value, slope = silu(act * pre)
            first_ref[(x - 3) * 20 * Z : (x - 2) * 20 * Z, :] = value.astype(BF)
            sg1_ref[(x - 3) * Y * Z : (x - 2) * Y * Z, :] = (act * slope)[2 * Z : 18 * Z]
        else:
            part1_ref[EARLY[x]] = pre
    for x in range(1, 5):
        p = taps(firsts, x, 18, w2_ref, lines=[i for i in range(3) if 3 <= x + i < 5])
        part2_ref[x - 1] = lanes(p, 1) + from_below(lanes(p, 0)) + from_above(lanes(p, 2))


def prepare(
    grad_hbm, feat_hbm, blocks_hbm, owners_hbm, rows_ref, own_ref, near_ref, far_ref,
    wide, grad_ref, feat_ref, blocks_ref, owners_ref, sems,
):
    copies = [
        pltpu.make_async_copy(a, b, sems.at[n])
        for n, (a, b) in enumerate(
            ((grad_hbm, grad_ref), (feat_hbm, feat_ref), (blocks_hbm, blocks_ref), (owners_hbm, owners_ref))
        )
    ]
    for c in copies:
        c.start()
    copies[0].wait()
    row, col = iota((128, 32), 0), iota((128, 32), 1)
    take = one((col == 2 * (row // 8) - 2 + row % 8) & (row % 8 < 6))
    rows_ref[...] = mm(take, grad_ref[0, 0]).astype(BF)
    for c in copies[1:]:
        c.wait()
    lane = iota((Y, C), 1)
    for x in range(X):
        f = feat_ref[x].astype(F32)
        f = jnp.concatenate([f, jnp.zeros((Y, C), F32)], axis=1)
        for z in range(Z):
            t = jnp.where(lane < CIN, f[:, z * CIN : z * CIN + C], 0.0)
            wide[pl.ds(x * Y * Z + z, Y, stride=Z), :] = t
    blocks = blocks_ref[0].astype(F32)
    mine = iota((Z, 4), 0) // 4 == iota((Z, 4), 1)
    for by in range(4):
        m = jnp.sum(jnp.where(mine, blocks[by : by + 1, :], 0.0), axis=1, keepdims=True)
        m = jnp.broadcast_to(m, (Z, C))
        own_ref[OWN + by * Z : OWN + (by + 1) * Z, :] = m.astype(BF)
        for x in range(X):
            for y in range(4 * by, 4 * by + 4):
                at = (x * Y + y) * Z
                own_ref[at : at + Z, :] = (wide[at : at + Z, :] * m).astype(BF)
    row, col = iota((16, 16), 0), iota((16, 16), 1)
    across = jnp.broadcast_to(owners_ref[...].astype(F32), (16, 16))
    dest = jnp.sum(jnp.where(row == col, across, 0.0), axis=1, keepdims=True)
    rank = jnp.sum(jnp.where((col < row) & (dest == across), 1.0, 0.0), axis=1, keepdims=True)
    place = jnp.broadcast_to(dest * 8.0 + rank, (16, C)).astype(BF)
    own_ref[OWN + 4 * Z : OWN + 5 * Z, :] = place

    def fill(up, down):
        for x in range(X):
            up[x * 3 * Z : (x + 1) * 3 * Z, :] = own_ref[(x * Y + 13) * Z : (x + 1) * Y * Z, :]
            down[x * 3 * Z : (x + 1) * 3 * Z, :] = own_ref[x * Y * Z : (x * Y + 3) * Z, :]
        for ref, by in ((up, 3), (down, 0)):
            ref[192:208, :] = place
            ref[208:224, :] = own_ref[OWN + by * Z : OWN + (by + 1) * Z, :]

    @pl.when(lax.rem(lax.axis_index("x"), 2) == 0)
    def _():
        fill(near_ref, far_ref)

    @pl.when(lax.rem(lax.axis_index("x"), 2) == 1)
    def _():
        fill(far_ref, near_ref)


def widen(
    own_ref, beside_ref, beyond_ref, rows_ref, after_ref,
    mid_ref, mask_ref, gc_ref, place_ref, near_ref, far_ref,
    sides,
):
    odd = lax.rem(lax.axis_index("x"), 2)
    sides[1 - odd] = beside_ref[...]
    sides[odd] = beyond_ref[...]
    low_ref, high_ref = sides.at[0], sides.at[1]
    for x in range(X):
        at = x * 22 * Z
        mid_ref[at : at + 3 * Z, :] = low_ref[x * 3 * Z : (x + 1) * 3 * Z, :]
        mid_ref[at + 3 * Z : at + 19 * Z, :] = own_ref[x * Y * Z : (x + 1) * Y * Z, :]
        mid_ref[at + 19 * Z : at + 22 * Z, :] = high_ref[x * 3 * Z : (x + 1) * 3 * Z, :]
    tiles = [low_ref[208:224, :]]
    tiles += [own_ref[OWN + by * Z : OWN + (by + 1) * Z, :] for by in range(4)]
    tiles += [high_ref[208:224, :]]
    which = iota((Z, C), 1) // 16
    packed = jnp.zeros((Z, C), F32)
    for by in range(6):
        packed = jnp.where(which == by, tiles[by].astype(F32), packed)
    mask_ref[...] = packed.astype(BF)
    place_ref[...] = own_ref[OWN + 4 * Z : OWN + 5 * Z, :]
    place = jnp.concatenate(
        [
            low_ref[192:208, :].astype(F32),
            own_ref[OWN + 4 * Z : OWN + 5 * Z, :].astype(F32) + 2.0,
            high_ref[192:208, :].astype(F32) + 4.0,
        ],
        axis=0,
    )
    bricks = mm(one(place == iota((48, C), 1).astype(F32)), rows_ref[...])[12:44].astype(BF)
    for q in range(8):
        gc_ref[q // 4, q % 4] = lanes(bricks, q)

    def fill(up, down):
        for q in range(4):
            up[COTS + q * 32 : COTS + (q + 1) * 32, :] = lanes(bricks, 4 + q)
            down[COTS + q * 32 : COTS + (q + 1) * 32, :] = lanes(bricks, q)
        up[0:COTS, :] = mid_ref[22 * Z :, :]
        down[0:COTS, :] = mid_ref[0:COTS, :]
        for ref in (up, down):
            ref[MASK:, :] = mask_ref[...]

    @pl.when(lax.axis_index("c") == 0)
    def _():
        fill(near_ref, far_ref)

    @pl.when(lax.axis_index("c") == 1)
    def _():
        fill(far_ref, near_ref)


def places():
    core, z, x = lax.axis_index("c"), lax.axis_index("z"), lax.axis_index("x")
    pick = lambda a, b: jnp.where(core == 0, a, b)
    return pick(z, x), pick(x, z), pick(4, 1), pick(1, 4)


def fold_cores(grads_ref, theirs_ref, bricks_ref, *out_refs):
    first, _, a, b = places()
    for n, out in enumerate(out_refs):
        for t in range(4):
            to = (first ^ n) * a + t * b
            rows = pl.ds(pl.multiple_of(to * PART, 16), PART)
            out[t * PART : (t + 1) * PART, :] = (
                grads_ref[0, rows, :].astype(F32) + theirs_ref[rows, :].astype(F32)
            ).astype(BF)
            rows = pl.ds(pl.multiple_of(to * 16, 16), 16)
            out[4 * PART + t * 16 : 4 * PART + (t + 1) * 16, :] = bricks_ref[rows, :]


def fold_first(*refs):
    got, outs = [refs[i] for i in (0, 1, 3, 2)], refs[4:]
    _, second, _, _ = places()
    for m, out in enumerate(outs):
        to = second ^ m
        rows = pl.ds(pl.multiple_of(to * PART, 16), PART)
        v = [g[rows, :].astype(F32) for g in got]
        out[:PART, :] = ((v[0] + v[1]) + (v[2] + v[3])).astype(BF)
        rows = pl.ds(pl.multiple_of(4 * PART + to * 16, 16), 16)
        for n, g in enumerate(got):
            out[PART + n * 16 : PART + (n + 1) * 16, :] = g[rows, :]


def fold_second(*refs):
    got, (part_ref, bricks_ref) = [refs[i] for i in (0, 1, 3, 2)], refs[4:]
    first, second, a, b = places()
    v = [g[:PART, :].astype(F32) for g in got]
    part_ref[...] = ((v[0] + v[1]) + (v[2] + v[3])).astype(BF)
    for m, g in enumerate(got):
        for n in range(4):
            at = pl.multiple_of(((first ^ n) * a + (second ^ m) * b) * 16, 16)
            bricks_ref[pl.ds(at, 16), :] = g[PART + n * 16 : PART + (n + 1) * 16, :]


def unfold(half_ref, core, first_hbm, second_hbm, down_hbm, wide, sems):
    spans = {
        0: ((0, 27 * C, second_hbm, 0), (27 * C, 28 * C, down_hbm, 0)),
        1: ((0, 27 * CIN, first_hbm, 0), (27 * CIN, 27 * CIN + 7 * C, down_hbm, C)),
    }

    def emit(which):
        copies = []
        for lo, hi, out, to in spans[which]:
            step = 864 if hi - lo > 1024 else hi - lo
            for at in range(lo, hi, step):
                wide[at : at + step, :] = half_ref[at : at + step, :].astype(F32)
                copies.append(
                    pltpu.make_async_copy(
                        wide.at[pl.ds(at, step)],
                        out.at[pl.ds(to + at - lo, step)],
                        sems.at[len(copies)],
                    )
                )
                copies[-1].start()
        for c in copies:
            c.wait()

    for which in range(2):
        pl.when(core == which)(functools.partial(emit, which))


def unfold_own(half_ref, first_hbm, second_hbm, down_hbm, wide, sems):
    unfold(half_ref, lax.axis_index("c"), first_hbm, second_hbm, down_hbm, wide, sems)


def unfold_other(half_ref, a, b, c, first_hbm, second_hbm, down_hbm, wide, sems):
    unfold(half_ref, 1 - lax.axis_index("c"), first_hbm, second_hbm, down_hbm, wide, sems)


def swap(v, axes, first):
    n = lax.axis_size(axes)
    pairs = [(i, i + 1) for i in range(first, n - 1, 2)]
    return lax.ppermute(v, axes, pairs + [(j, i) for i, j in pairs])


def swap_cores(v):
    return lax.ppermute(v, "c", [(0, 1), (1, 0)])


def up_matrix():
    m = np.zeros((6 * Z, 64), np.float32)
    for by in range(6):
        for z in range(Z):
            m[by * Z + z, z // 2 % 2 * 32 + by * 4 + z // 4] = 1
    return jnp.asarray(m, BF)


def flip(v, axis, bits):
    return lax.ppermute(v, axis, [(i, i ^ bits) for i in range(lax.axis_size(axis))])


def flip_by_core(v, axes, bits):
    every = ("c", "z", "x")
    size = [lax.axis_size(n) for n in every]
    pairs = []
    for d in range(size[0] * size[1] * size[2]):
        at = [int(i) for i in np.unravel_index(d, size)]
        at[every.index(axes[at[0]])] ^= bits
        pairs.append((d, int(np.ravel_multi_index(at, size))))
    return lax.ppermute(v, every, pairs)


def per_device(features, block_mask, weight_first, weight_second, weight_down, owners, moved_grad):
    rows, own, beside, beyond = call(
        prepare,
        [((128, 8 * C), BF), ((X * Y * Z + 80, C), BF), ((224, C), BF), ((224, C), BF)],
        (moved_grad, features, block_mask, owners.reshape(1, 16)),
        [pl.BlockSpec(memory_space=pltpu.HBM)] * 4,
        [
            ((X * Y * Z, C), F32),
            (moved_grad.shape, BF),
            (features.shape, BF),
            (block_mask.shape, jnp.int32),
            ((1, 16), jnp.int32),
            pltpu.SemaphoreType.DMA((4,)),
        ],
        vmem=60 << 20,
    )
    beyond, beside = swap(beyond, GY, 1), swap(beside, GY, 0)
    w1, w2, back = call(
        arrange,
        [((9 * C, 3 * C), BF), ((9 * C, 3 * C), BF), ((3 * C, 9 * C), BF)],
        (weight_first, weight_second, own),
        flops=2_000_000_000,
    )
    rows = lax.all_to_all(rows, GY, 0, 0, tiled=True)

    mid, mask, gc, place, near, far = call(
        widen,
        [((4 * 22 * Z, C), BF), ((16, C), BF), ((2, 4, 32, C), BF), ((16, C), BF), ((STRIP, C), BF), ((STRIP, C), BF)],
        (own, beside, beyond, rows, w1),
        [VM] * 4 + [pl.BlockSpec(memory_space=pl.ANY)],
        scratch=[((2, 224, C), BF)],
    )
    far, near = swap(far, GX, 1), swap(near, GX, 0)
    ahead = call(
        begin,
        [((4, 20 * Z, C), F32), ((40 * Z, C), BF), ((2 * Y * Z, C), F32), ((4, 18 * Z, C), F32), ((320, 2 * C), BF)],
        (mid, mask, w1, w2, gc, up_matrix()),
        flops=3_000_000_000,
    )

    *ahead, own_ge = ahead
    part1, inner, _, part2 = ahead
    beside = call(
        near_side,
        [((60 * Z, C), BF), ((Y * Z, C), F32), ((2 * Y * Z, C), BF), ((3 * 18 * Z, C), F32)],
        (near, mask, part1, inner, part2, w1, w2),
        flops=3_000_000_000,
    )
    grads, outgoing = call(
        section,
        [((2, HALF, C), BF), ((256, C), BF)],
        (near, mid, far, mask, own_ge, place, *ahead, *beside, w1, w2, back, weight_down, up_matrix()),
        scratch=[
            ((2, STRIP, C), BF),
            ((8 * 20 * Z, C), BF),
            ((X * Y * Z, C), F32),
            ((X * Y * Z, C), BF),
            ((6 * 18 * Z, C), F32),
            ((40 * Z, 2 * C), BF),
            ((6 * 18 * Z, C), BF),
            ((X * Y * Z, 3 * C), BF),
            ((3 * C, 6 * Y * Z), BF),
        ],
        flops=8_000_000_000,
    )

    blocks = call(
        fold_cores, [((4 * PART + 64, C), BF)] * 4, (grads, swap_cores(grads[1]), outgoing)
    )
    far = flip_by_core(blocks[2], ("z", "x"), 2)
    blocks = [blocks[0]] + [flip_by_core(blocks[n], ("z", "x"), n) for n in (1, 3)] + [far]
    blocks = call(fold_first, [((PART + 64, C), BF)] * 4, blocks)
    far = flip_by_core(blocks[2], ("x", "z"), 2)
    blocks = [blocks[0]] + [flip_by_core(blocks[n], ("x", "z"), n) for n in (1, 3)] + [far]
    part, arrived = call(fold_second, [((PART, C), BF), ((256, C), BF)], blocks)
    moved = arrived.reshape(16, 8, 2, C).transpose(0, 2, 1, 3).reshape(1, 1, 32, 8 * C)
    others = [flip(part, "y", n).astype(F32) for n in (1, 2, 3)]
    part = ((part.astype(F32) + others[0]) + (others[1] + others[2])).astype(BF)
    part = lax.all_to_all(jnp.broadcast_to(part[None], (16, PART, C)), GY, 0, 0, tiled=True)
    part = part.reshape(HALF, C)
    grads = [((27 * CIN, C), F32), ((27 * C, C), F32), ((8 * C, C), F32)]
    scratch = [((HALF, C), F32), pltpu.SemaphoreType.DMA((5,))]
    hbm = pl.BlockSpec(memory_space=pl.ANY)
    other = swap_cores(part)
    grads_own = call(unfold_own, grads, (part,), [VM], scratch, out_specs=[hbm] * 3)
    grad_first, grad_second, grad_down = call(
        unfold_other, grads, (other, *grads_own), [VM] + [hbm] * 3, scratch, out_specs=[hbm] * 3,
        aliases={1: 0, 2: 1, 3: 2},
    )
    return (
        moved,
        grad_first.reshape(27, CIN, C),
        grad_second.reshape(27, C, C),
        grad_down.reshape(8, C, C),
    )


def solution(mesh):
    shape = dict(mesh.shape)
    fine = Mesh(
        mesh.devices.reshape(shape["gx"] // 2, 2, 4, shape["gy"] // 4), ("y", "c", "z", "x")
    )
    whole, tiles = P(GX, GY, None), P(GX, GY, None, None)
    return jax.shard_map(
        per_device,
        mesh=fine,
        in_specs=(whole, whole, P(), P(), P(), tiles, tiles),
        out_specs=(tiles, P(), P(), P()),
        check_vma=False,
    )
```

```python
import functools

import jax
import jax.numpy as jnp
import numpy as np
from jax import lax
from jax.experimental import pallas as pl
from jax.experimental.pallas import tpu as pltpu
from jax.sharding import Mesh, PartitionSpec as P

GX, GY = ("y", "c"), ("z", "x")
F32, BF = jnp.float32, jnp.bfloat16
X, Y, Z, C, CIN = 4, 16, 16, 128, 96
HALF, PART = 3584, 224
OWN = 1024
COTS, MASK, STRIP = 1056, 1184, 1200
EARLY = {1: 0, 2: 1, 5: 2, 6: 3}
NN = (((1,), (0,)), ((), ()))
NT = (((1,), (1,)), ((), ()))
TN = (((0,), (0,)), ((), ()))


def mm(a, b, dims=NN):
    return lax.dot_general(a, b, dims, preferred_element_type=F32)


def iota(shape, axis):
    return lax.broadcasted_iota(jnp.int32, shape, axis)


def one(where):
    return jnp.where(where, 1.0, 0.0).astype(BF)


def z_of(rows):
    return iota((rows, C), 0) % Z


def from_above(v):
    return jnp.where(z_of(v.shape[0]) < Z - 1, pltpu.roll(v, v.shape[0] - 1, 0), 0.0)


def from_below(v):
    return jnp.where(z_of(v.shape[0]) > 0, pltpu.roll(v, 1, 0), 0.0)


def lanes(p, k):
    return p[:, k * C : (k + 1) * C]


def silu(v):
    s = jax.nn.sigmoid(v)
    return v * s, s * (1.0 + v * (1.0 - s))


def spread(packed, by):
    return jnp.broadcast_to(packed[:, 16 * by : 16 * by + 1].astype(F32), (Z, C))


def taps(get, x, n, w, dims=NN, flip=False, lines=(0, 1, 2)):
    wins = []
    for i in lines:
        for j in range(3):
            wins.append(get(x + 2 - i, 2 - j, n) if flip else get(x + i, j, n))
    if len(lines) < 3:
        w = w[3 * lines[0] * C : 3 * (lines[-1] + 1) * C, :]
    else:
        w = w[...]
    return mm(jnp.concatenate(wins, axis=1), w, dims)


def section(
    near_ref, mid_ref, far_ref, mask_ref, own_ge_ref, place_ref, part1_ref, inner_ref, inner_sg1_ref, part2_ref,
    near_first_ref, near_sg1_ref, near_second_ref, near_slope_ref, near_ge_ref, w1_ref, w2_ref, back_ref, wd_ref, up_ref,
    grads_ref, out_ref,
    sides, first, sg1, second, slopes, ge, g2, gs, vt,
):
    core = lax.axis_index("c")
    sides[1 - core] = near_ref[...]
    sides[core] = far_ref[...]
    low_ref, high_ref = sides.at[0], sides.at[1]

    def cells(x, y, n):
        ref, x = ((low_ref, x), (mid_ref, x - 3), (high_ref, x - 7))[(x > 2) + (x > 6)]
        return ref[(x * 22 + y) * Z : (x * 22 + y + n) * Z, :]

    def firsts(x, y, n):
        return first[(x * 20 + y) * Z : (x * 20 + y + n) * Z, :]

    def cots(x, y, n):
        return g2[(x * 18 + y) * Z : (x * 18 + y + n) * Z, :]

    packed = low_ref[MASK:, :], mask_ref[...], high_ref[MASK:, :]
    masks = [[spread(t, by) for by in range(6)] for t in packed]

    def cotangent(u, q):
        return (low_ref if u == 0 else high_ref)[COTS + q * 32 : COTS + (q + 1) * 32, :]

    def line(x, y0, cells):
        return jnp.concatenate(
            [masks[(x + 4) // 4][(y + 4) // 4] for y in range(y0, y0 + cells)], axis=0
        )

    def weight_grad(get, x0, y0, rows, put):
        for j in range(3):
            for x in range(6):
                vt[j * C : (j + 1) * C, x * Y * Z : (x + 1) * Y * Z] = get(x0 + x, y0 + j, Y).T
        for i in range(3):
            p = mm(vt[:, i * Y * Z : (i + X) * Y * Z], gs[...]).astype(BF)
            for j in range(3):
                for k in range(3):
                    put(9 * i + 3 * j + k, p[j * C : j * C + rows, k * C : (k + 1) * C])

    def put_z_taps(x, g):
        at = x * Y * Z
        gs[at : at + Y * Z, 0:C] = from_above(g).astype(BF)
        gs[at : at + Y * Z, C : 2 * C] = g.astype(BF)
        gs[at : at + Y * Z, 2 * C : 3 * C] = from_below(g).astype(BF)

    first[3 * 20 * Z : 5 * 20 * Z, :] = inner_ref[...]
    sg1[Y * Z : 3 * Y * Z, :] = inner_sg1_ref[...]
    for ref, got, unit, at in (
        (first, near_first_ref, 20 * Z, 5),
        (sg1, near_sg1_ref, Y * Z, 3),
        (second, near_second_ref, Y * Z, 2),
        (slopes, near_slope_ref, 18 * Z, 3),
    ):
        at = pl.multiple_of((1 - core) * (at * unit), 16)
        ref[pl.ds(at, got.shape[0]), :] = got[...]

    def put(ref, size):
        def store(x, v):
            ref[x * size : (x + 1) * size, :] = v

        return store

    for which in range(2):
        pl.when(core == which)(
            functools.partial(
                half_forward, which == 1, cells, firsts, line, w1_ref, w2_ref, part1_ref, part2_ref,
                put(first, 20 * Z), put(sg1, Y * Z), put(second, Y * Z), put(slopes, 18 * Z),
            )
        )

    for which in range(2):
        u = 3 * which
        cots_far = [cotangent(u, q) for q in range(4)]
        pl.when(core == which)(functools.partial(repeat_along_z, cots_far, up_ref, ge, u * 160))
    ge[pl.ds(pl.multiple_of((1 - core) * 480, 16), 160), :] = near_ge_ref[...]
    ge[160:480, :] = own_ge_ref[...]

    for x in range(6):
        u, a = (x + 1) // 2, (x + 1) % 2
        back = []
        for b in range(2):
            at = (u * 10 + 1 - b) * Z
            w = jnp.concatenate([wd_ref[4 * a + 2 * b], wd_ref[4 * a + 2 * b + 1]], axis=1)
            back.append(mm(ge[at : at + 9 * Z, :], w, NT))
        g = jnp.concatenate(
            [back[1 - y % 2][y // 2 * Z : (y // 2 + 1) * Z] for y in range(18)], axis=0
        )
        g = (g * slopes[x * 18 * Z : (x + 1) * 18 * Z, :]).astype(BF)
        g2[x * 18 * Z : (x + 1) * 18 * Z, :] = g
        if 1 <= x < 5:
            put_z_taps(x - 1, g[Z : 17 * Z].astype(F32))

    def corner(a, b):
        return jnp.concatenate(
            [
                second[((2 * u + a) * Y + 2 * v + b) * Z : ((2 * u + a) * Y + 2 * v + b + 1) * Z, :]
                for u in range(2)
                for v in range(8)
            ],
            axis=0,
        )

    corners = [corner(a, b) for a in range(2) for b in range(2)]
    wd = jnp.concatenate(
        [jnp.concatenate([wd_ref[2 * q], wd_ref[2 * q + 1]], axis=1) for q in range(4)], axis=0
    )
    p = mm(jnp.concatenate(corners, axis=1), wd)
    coarse = (lanes(p, 0) + from_above(lanes(p, 1))).astype(BF)
    row, col = iota((128, 256), 0), iota((128, 256), 1)
    a, by, b, z = col // 128, col // 32 % 4, col // 16 % 2, col % Z
    order = (row // 16 == 4 * a + 2 * b + z // 2 % 2) & (row % 16 == by * 4 + z // 4) & (z % 2 == 0)
    bricks = mm(one(order), coarse).astype(BF)
    place = jnp.concatenate([place_ref[...].astype(F32)] * 8, axis=0)
    place = jnp.concatenate([place] * 2, axis=1)
    target = (8 * (col // 16) + col % 2).astype(F32)
    out_ref[...] = mm(one((place == target) & (row // 16 == col // 2 % 8)), bricks, TN).astype(BF)

    gec = jnp.concatenate([ge[(u * 10 + 1) * Z : (u * 10 + 9) * Z, :] for u in (1, 2)], axis=0)

    def put_a(at, v):
        grads_ref[core, at : at + v.shape[0], :] = v

    def put_b(at, v):
        grads_ref[1 - core, at : at + v.shape[0], :] = v

    for q in range(4):
        r = mm(corners[q], gec, TN).astype(BF)
        for c in range(2):
            t = 2 * q + c
            if t == 0:
                put_a(27 * C, lanes(r, c))
            else:
                put_b(27 * CIN + (t - 1) * C, lanes(r, c))
    put_b(27 * CIN + 7 * C, jnp.zeros((HALF - 27 * CIN - 7 * C, C), BF))
    weight_grad(firsts, 1, 1, C, lambda t, v: put_a(t * C, v))

    for x in range(X):
        p = taps(cots, x, Y, back_ref, NT, flip=True)
        g = lanes(p, 1) + from_above(lanes(p, 0)) + from_below(lanes(p, 2))
        g = g + cots(x + 1, 1, Y).astype(F32)
        g = (g * sg1[x * Y * Z : (x + 1) * Y * Z, :]).astype(BF)
        put_z_taps(x, g.astype(F32))
    weight_grad(cells, 2, 2, CIN, lambda t, v: put_b(t * CIN, v))


VM = pl.BlockSpec(memory_space=pltpu.VMEM)


def call(kernel, outs, args, in_specs=None, scratch=(), flops=10_000_000, vmem=40 << 20, out_specs=None, aliases={}):
    return pl.pallas_call(
        kernel,
        out_shape=tuple(jax.ShapeDtypeStruct(shape, dtype) for shape, dtype in outs),
        in_specs=in_specs or [VM] * len(args),
        out_specs=tuple(out_specs or [VM] * len(outs)),
        input_output_aliases=aliases,
        scratch_shapes=[pltpu.VMEM(*s) if isinstance(s, tuple) else s for s in scratch],
        compiler_params=pltpu.CompilerParams(vmem_limit_bytes=vmem),
        cost_estimate=pl.CostEstimate(
            flops=flops, bytes_accessed=1_000_000, transcendentals=0
        ),
    )(*args)


def arrange(w1_ref, w2_ref, after_ref, first_ref, second_ref, back_ref):
    for m in range(9):
        for k in range(3):
            first_ref[m * C : m * C + CIN, k * C : (k + 1) * C] = w1_ref[3 * m + k]
            second_ref[m * C : (m + 1) * C, k * C : (k + 1) * C] = w2_ref[3 * m + k]
            back_ref[k * C : (k + 1) * C, m * C : (m + 1) * C] = w2_ref[3 * m + k]
        first_ref[m * C + CIN : (m + 1) * C, :] = jnp.zeros((C - CIN, 3 * C), BF)


def half_forward(
    high, cells, firsts, act, w1_ref, w2_ref, part1_ref, part2_ref, put_first, put_sg1, put_second, put_slope
):
    for x in (5, 6, 7) if high else (0, 1, 2):
        p = taps(cells, x, 20, w1_ref, lines=[i for i in range(3) if not 3 <= x + i < 7])
        pre = lanes(p, 1) + from_below(lanes(p, 0)) + from_above(lanes(p, 2))
        if x in EARLY:
            pre = pre + part1_ref[EARLY[x]]
        on = act(x - 2, -2, 20)
        value, slope = silu(on * pre)
        put_first(x, value.astype(BF))
        if x in (2, 5):
            put_sg1(x - 2, (on * slope)[2 * Z : 18 * Z])
    for x in (3, 4, 5) if high else (0, 1, 2):
        p = taps(firsts, x, 18, w2_ref, lines=[i for i in range(3) if not 3 <= x + i < 5])
        on = act(x - 1, -1, 18)
        pre = lanes(p, 1) + from_below(lanes(p, 0)) + from_above(lanes(p, 2))
        if 1 <= x < 5:
            pre = pre + part2_ref[x - 1]
        value, slope = silu(on * pre + firsts(x + 1, 1, 18).astype(F32))
        if 1 <= x < 5:
            put_second(x - 1, value[Z : 17 * Z].astype(BF))
        put_slope(x, on * slope)


def near_side(
    near_ref, mask_ref, part1_ref, inner_ref, part2_ref, w1_ref, w2_ref, up_ref,
    first_ref, sg1_ref, second_ref, slope_ref, ge_ref,
):
    def run(high):
        base = 5 if high else 0
        tiles = near_ref[MASK:, :], mask_ref[...]
        masks = [[spread(t, by) for by in range(6)] for t in tiles]

        def cells(x, y, n):
            x = x - 7 if high else x
            return near_ref[(x * 22 + y) * Z : (x * 22 + y + n) * Z, :]

        def firsts(x, y, n):
            ref, x = (inner_ref, x - 3) if x in (3, 4) else (first_ref, x - base)
            return ref[(x * 20 + y) * Z : (x * 20 + y + n) * Z, :]

        def act(x, y0, n):
            here = masks[1 if (x + 4) // 4 == 1 else 0]
            return jnp.concatenate([here[(y + 4) // 4] for y in range(y0, y0 + n)], axis=0)

        def put(ref, size, start):
            def store(x, v):
                ref[(x - start) * size : (x - start + 1) * size, :] = v

            return store

        half_forward(
            high, cells, firsts, act, w1_ref, w2_ref, part1_ref, part2_ref,
            put(first_ref, 20 * Z, base), put(sg1_ref, Y * Z, 3 if high else 0),
            put(second_ref, Y * Z, 2 if high else 0), put(slope_ref, 18 * Z, 3 if high else 0),
        )

    cots = [near_ref[COTS + q * 32 : COTS + (q + 1) * 32, :] for q in range(4)]
    repeat_along_z(cots, up_ref, ge_ref, 0)
    for core in range(2):
        pl.when(lax.axis_index("c") == core)(functools.partial(run, core == 0))


def repeat_along_z(cots, up_ref, out_ref, at):
    both = jnp.concatenate(
        [jnp.concatenate([cots[2 * b + c] for b in range(2)], axis=1) for c in range(2)], axis=0
    )
    r = mm(up_ref[...], both)
    even = z_of(Z) % 2 == 0
    for v in range(10):
        by, b = (v + 1) // 2, (v + 1) % 2
        t = r[by * Z : (by + 1) * Z, b * C : (b + 1) * C]
        rows = slice(at + v * Z, at + (v + 1) * Z)
        out_ref[rows, 0:C] = jnp.where(even, t, 0.0).astype(BF)
        out_ref[rows, C : 2 * C] = jnp.where(even, 0.0, t).astype(BF)


def begin(
    mid_ref, mask_ref, w1_ref, w2_ref, gc_ref, up_ref,
    part1_ref, first_ref, sg1_ref, part2_ref, ge_ref,
):
    def cells(x, y, n):
        return mid_ref[((x - 3) * 22 + y) * Z : ((x - 3) * 22 + y + n) * Z, :]

    def firsts(x, y, n):
        return first_ref[((x - 3) * 20 + y) * Z : ((x - 3) * 20 + y + n) * Z, :]

    for u in range(2):
        repeat_along_z([gc_ref[u, q] for q in range(4)], up_ref, ge_ref, u * 160)
    masks = [spread(mask_ref[...], by) for by in range(6)]
    act = jnp.concatenate([masks[(y + 4) // 4] for y in range(-2, 18)], axis=0)
    for x in (3, 4, 1, 2, 5, 6):
        p = taps(cells, x, 20, w1_ref, lines=[i for i in range(3) if 3 <= x + i < 7])
        pre = lanes(p, 1) + from_below(lanes(p, 0)) + from_above(lanes(p, 2))
        if x in (3, 4):
            value, slope = silu(act * pre)
            first_ref[(x - 3) * 20 * Z : (x - 2) * 20 * Z, :] = value.astype(BF)
            sg1_ref[(x - 3) * Y * Z : (x - 2) * Y * Z, :] = (act * slope)[2 * Z : 18 * Z]
        else:
            part1_ref[EARLY[x]] = pre
    for x in range(1, 5):
        p = taps(firsts, x, 18, w2_ref, lines=[i for i in range(3) if 3 <= x + i < 5])
        part2_ref[x - 1] = lanes(p, 1) + from_below(lanes(p, 0)) + from_above(lanes(p, 2))


def prepare(
    grad_hbm, feat_hbm, blocks_hbm, owners_hbm, rows_ref, own_ref, near_ref, far_ref,
    wide, grad_ref, feat_ref, blocks_ref, owners_ref, sems,
):
    copies = [
        pltpu.make_async_copy(a, b, sems.at[n])
        for n, (a, b) in enumerate(
            ((grad_hbm, grad_ref), (feat_hbm, feat_ref), (blocks_hbm, blocks_ref), (owners_hbm, owners_ref))
        )
    ]
    for c in copies:
        c.start()
    copies[0].wait()
    row, col = iota((128, 32), 0), iota((128, 32), 1)
    take = one((col == 2 * (row // 8) - 2 + row % 8) & (row % 8 < 6))
    rows_ref[...] = mm(take, grad_ref[0, 0]).astype(BF)
    for c in copies[1:]:
        c.wait()
    lane = iota((Y, C), 1)
    for x in range(X):
        f = feat_ref[x].astype(F32)
        f = jnp.concatenate([f, jnp.zeros((Y, C), F32)], axis=1)
        for z in range(Z):
            t = jnp.where(lane < CIN, f[:, z * CIN : z * CIN + C], 0.0)
            wide[pl.ds(x * Y * Z + z, Y, stride=Z), :] = t
    blocks = blocks_ref[0].astype(F32)
    mine = iota((Z, 4), 0) // 4 == iota((Z, 4), 1)
    for by in range(4):
        m = jnp.sum(jnp.where(mine, blocks[by : by + 1, :], 0.0), axis=1, keepdims=True)
        m = jnp.broadcast_to(m, (Z, C))
        own_ref[OWN + by * Z : OWN + (by + 1) * Z, :] = m.astype(BF)
        for x in range(X):
            for y in range(4 * by, 4 * by + 4):
                at = (x * Y + y) * Z
                own_ref[at : at + Z, :] = (wide[at : at + Z, :] * m).astype(BF)
    row, col = iota((16, 16), 0), iota((16, 16), 1)
    across = jnp.broadcast_to(owners_ref[...].astype(F32), (16, 16))
    dest = jnp.sum(jnp.where(row == col, across, 0.0), axis=1, keepdims=True)
    rank = jnp.sum(jnp.where((col < row) & (dest == across), 1.0, 0.0), axis=1, keepdims=True)
    place = jnp.broadcast_to(dest * 8.0 + rank, (16, C)).astype(BF)
    own_ref[OWN + 4 * Z : OWN + 5 * Z, :] = place

    def fill(up, down):
        for x in range(X):
            up[x * 3 * Z : (x + 1) * 3 * Z, :] = own_ref[(x * Y + 13) * Z : (x + 1) * Y * Z, :]
            down[x * 3 * Z : (x + 1) * 3 * Z, :] = own_ref[x * Y * Z : (x * Y + 3) * Z, :]
        for ref, by in ((up, 3), (down, 0)):
            ref[192:208, :] = place
            ref[208:224, :] = own_ref[OWN + by * Z : OWN + (by + 1) * Z, :]

    @pl.when(lax.rem(lax.axis_index("x"), 2) == 0)
    def _():
        fill(near_ref, far_ref)

    @pl.when(lax.rem(lax.axis_index("x"), 2) == 1)
    def _():
        fill(far_ref, near_ref)


def widen(
    own_ref, beside_ref, beyond_ref, rows_ref, after_ref,
    mid_ref, mask_ref, gc_ref, place_ref, near_ref, far_ref,
    sides,
):
    odd = lax.rem(lax.axis_index("x"), 2)
    sides[1 - odd] = beside_ref[...]
    sides[odd] = beyond_ref[...]
    low_ref, high_ref = sides.at[0], sides.at[1]
    for x in range(X):
        at = x * 22 * Z
        mid_ref[at : at + 3 * Z, :] = low_ref[x * 3 * Z : (x + 1) * 3 * Z, :]
        mid_ref[at + 3 * Z : at + 19 * Z, :] = own_ref[x * Y * Z : (x + 1) * Y * Z, :]
        mid_ref[at + 19 * Z : at + 22 * Z, :] = high_ref[x * 3 * Z : (x + 1) * 3 * Z, :]
    tiles = [low_ref[208:224, :]]
    tiles += [own_ref[OWN + by * Z : OWN + (by + 1) * Z, :] for by in range(4)]
    tiles += [high_ref[208:224, :]]
    which = iota((Z, C), 1) // 16
    packed = jnp.zeros((Z, C), F32)
    for by in range(6):
        packed = jnp.where(which == by, tiles[by].astype(F32), packed)
    mask_ref[...] = packed.astype(BF)
    place_ref[...] = own_ref[OWN + 4 * Z : OWN + 5 * Z, :]
    place = jnp.concatenate(
        [
            low_ref[192:208, :].astype(F32),
            own_ref[OWN + 4 * Z : OWN + 5 * Z, :].astype(F32) + 2.0,
            high_ref[192:208, :].astype(F32) + 4.0,
        ],
        axis=0,
    )
    bricks = mm(one(place == iota((48, C), 1).astype(F32)), rows_ref[...])[12:44].astype(BF)
    for q in range(8):
        gc_ref[q // 4, q % 4] = lanes(bricks, q)

    def fill(up, down):
        for q in range(4):
            up[COTS + q * 32 : COTS + (q + 1) * 32, :] = lanes(bricks, 4 + q)
            down[COTS + q * 32 : COTS + (q + 1) * 32, :] = lanes(bricks, q)
        up[0:COTS, :] = mid_ref[22 * Z :, :]
        down[0:COTS, :] = mid_ref[0:COTS, :]
        for ref in (up, down):
            ref[MASK:, :] = mask_ref[...]

    @pl.when(lax.axis_index("c") == 0)
    def _():
        fill(near_ref, far_ref)

    @pl.when(lax.axis_index("c") == 1)
    def _():
        fill(far_ref, near_ref)


def places():
    core, z, x = lax.axis_index("c"), lax.axis_index("z"), lax.axis_index("x")
    pick = lambda a, b: jnp.where(core == 0, a, b)
    return pick(z, x), pick(x, z), pick(4, 1), pick(1, 4)


def fold_cores(grads_ref, theirs_ref, bricks_ref, *out_refs):
    first, _, a, b = places()
    for n, out in enumerate(out_refs):
        for t in range(4):
            to = (first ^ n) * a + t * b
            rows = pl.ds(pl.multiple_of(to * PART, 16), PART)
            out[t * PART : (t + 1) * PART, :] = (
                grads_ref[0, rows, :].astype(F32) + theirs_ref[rows, :].astype(F32)
            ).astype(BF)
            rows = pl.ds(pl.multiple_of(to * 16, 16), 16)
            out[4 * PART + t * 16 : 4 * PART + (t + 1) * 16, :] = bricks_ref[rows, :]


def fold_first(*refs):
    got, outs = [refs[i] for i in (0, 1, 3, 2)], refs[4:]
    _, second, _, _ = places()
    for m, out in enumerate(outs):
        to = second ^ m
        rows = pl.ds(pl.multiple_of(to * PART, 16), PART)
        v = [g[rows, :].astype(F32) for g in got]
        out[:PART, :] = ((v[0] + v[1]) + (v[2] + v[3])).astype(BF)
        rows = pl.ds(pl.multiple_of(4 * PART + to * 16, 16), 16)
        for n, g in enumerate(got):
            out[PART + n * 16 : PART + (n + 1) * 16, :] = g[rows, :]


def fold_second(*refs):
    got, (part_ref, bricks_ref) = [refs[i] for i in (0, 1, 3, 2)], refs[4:]
    first, second, a, b = places()
    v = [g[:PART, :].astype(F32) for g in got]
    part_ref[...] = ((v[0] + v[1]) + (v[2] + v[3])).astype(BF)
    for m, g in enumerate(got):
        for n in range(4):
            at = pl.multiple_of(((first ^ n) * a + (second ^ m) * b) * 16, 16)
            bricks_ref[pl.ds(at, 16), :] = g[PART + n * 16 : PART + (n + 1) * 16, :]


def unfold(half_ref, core, first_hbm, second_hbm, down_hbm, wide, sems):
    spans = {
        0: ((0, 27 * C, second_hbm, 0), (27 * C, 28 * C, down_hbm, 0)),
        1: ((0, 27 * CIN, first_hbm, 0), (27 * CIN, 27 * CIN + 7 * C, down_hbm, C)),
    }

    def emit(which):
        copies = []
        for lo, hi, out, to in spans[which]:
            step = 864 if hi - lo > 1024 else hi - lo
            for at in range(lo, hi, step):
                wide[at : at + step, :] = half_ref[at : at + step, :].astype(F32)
                copies.append(
                    pltpu.make_async_copy(
                        wide.at[pl.ds(at, step)],
                        out.at[pl.ds(to + at - lo, step)],
                        sems.at[len(copies)],
                    )
                )
                copies[-1].start()
        for c in copies:
            c.wait()

    for which in range(2):
        pl.when(core == which)(functools.partial(emit, which))


def unfold_own(half_ref, first_hbm, second_hbm, down_hbm, wide, sems):
    unfold(half_ref, lax.axis_index("c"), first_hbm, second_hbm, down_hbm, wide, sems)


def unfold_other(half_ref, a, b, c, first_hbm, second_hbm, down_hbm, wide, sems):
    unfold(half_ref, 1 - lax.axis_index("c"), first_hbm, second_hbm, down_hbm, wide, sems)


def swap(v, axes, first):
    n = lax.axis_size(axes)
    pairs = [(i, i + 1) for i in range(first, n - 1, 2)]
    return lax.ppermute(v, axes, pairs + [(j, i) for i, j in pairs])


def swap_cores(v):
    return lax.ppermute(v, "c", [(0, 1), (1, 0)])


def up_matrix():
    m = np.zeros((6 * Z, 64), np.float32)
    for by in range(6):
        for z in range(Z):
            m[by * Z + z, z // 2 % 2 * 32 + by * 4 + z // 4] = 1
    return jnp.asarray(m, BF)


def flip(v, axis, bits):
    return lax.ppermute(v, axis, [(i, i ^ bits) for i in range(lax.axis_size(axis))])


def flip_by_core(v, axes, bits):
    every = ("c", "z", "x")
    size = [lax.axis_size(n) for n in every]
    pairs = []
    for d in range(size[0] * size[1] * size[2]):
        at = [int(i) for i in np.unravel_index(d, size)]
        at[every.index(axes[at[0]])] ^= bits
        pairs.append((d, int(np.ravel_multi_index(at, size))))
    return lax.ppermute(v, every, pairs)


def per_device(features, block_mask, weight_first, weight_second, weight_down, owners, moved_grad):
    rows, own, beside, beyond = call(
        prepare,
        [((128, 8 * C), BF), ((X * Y * Z + 80, C), BF), ((224, C), BF), ((224, C), BF)],
        (moved_grad, features, block_mask, owners.reshape(1, 16)),
        [pl.BlockSpec(memory_space=pltpu.HBM)] * 4,
        [
            ((X * Y * Z, C), F32),
            (moved_grad.shape, BF),
            (features.shape, BF),
            (block_mask.shape, jnp.int32),
            ((1, 16), jnp.int32),
            pltpu.SemaphoreType.DMA((4,)),
        ],
        vmem=60 << 20,
    )
    beyond, beside = swap(beyond, GY, 1), swap(beside, GY, 0)
    w1, w2, back = call(
        arrange,
        [((9 * C, 3 * C), BF), ((9 * C, 3 * C), BF), ((3 * C, 9 * C), BF)],
        (weight_first, weight_second, own),
        flops=2_000_000_000,
    )
    rows = lax.all_to_all(rows, GY, 0, 0, tiled=True)

    mid, mask, gc, place, near, far = call(
        widen,
        [((4 * 22 * Z, C), BF), ((16, C), BF), ((2, 4, 32, C), BF), ((16, C), BF), ((STRIP, C), BF), ((STRIP, C), BF)],
        (own, beside, beyond, rows, w1),
        [VM] * 4 + [pl.BlockSpec(memory_space=pl.ANY)],
        scratch=[((2, 224, C), BF)],
    )
    far, near = swap(far, GX, 1), swap(near, GX, 0)
    ahead = call(
        begin,
        [((4, 20 * Z, C), F32), ((40 * Z, C), BF), ((2 * Y * Z, C), F32), ((4, 18 * Z, C), F32), ((320, 2 * C), BF)],
        (mid, mask, w1, w2, gc, up_matrix()),
        flops=3_000_000_000,
    )

    *ahead, own_ge = ahead
    part1, inner, _, part2 = ahead
    beside = call(
        near_side,
        [((60 * Z, C), BF), ((Y * Z, C), F32), ((2 * Y * Z, C), BF), ((3 * 18 * Z, C), F32), ((160, 2 * C), BF)],
        (near, mask, part1, inner, part2, w1, w2, up_matrix()),
        flops=3_000_000_000,
    )
    grads, outgoing = call(
        section,
        [((2, HALF, C), BF), ((256, C), BF)],
        (near, mid, far, mask, own_ge, place, *ahead, *beside, w1, w2, back, weight_down, up_matrix()),
        scratch=[
            ((2, STRIP, C), BF),
            ((8 * 20 * Z, C), BF),
            ((X * Y * Z, C), F32),
            ((X * Y * Z, C), BF),
            ((6 * 18 * Z, C), F32),
            ((40 * Z, 2 * C), BF),
            ((6 * 18 * Z, C), BF),
            ((X * Y * Z, 3 * C), BF),
            ((3 * C, 6 * Y * Z), BF),
        ],
        flops=8_000_000_000,
    )

    blocks = call(
        fold_cores, [((4 * PART + 64, C), BF)] * 4, (grads, swap_cores(grads[1]), outgoing)
    )
    far = flip_by_core(blocks[2], ("z", "x"), 2)
    blocks = [blocks[0]] + [flip_by_core(blocks[n], ("z", "x"), n) for n in (1, 3)] + [far]
    blocks = call(fold_first, [((PART + 64, C), BF)] * 4, blocks)
    far = flip_by_core(blocks[2], ("x", "z"), 2)
    blocks = [blocks[0]] + [flip_by_core(blocks[n], ("x", "z"), n) for n in (1, 3)] + [far]
    part, arrived = call(fold_second, [((PART, C), BF), ((256, C), BF)], blocks)
    moved = arrived.reshape(16, 8, 2, C).transpose(0, 2, 1, 3).reshape(1, 1, 32, 8 * C)
    others = [flip(part, "y", n).astype(F32) for n in (1, 2, 3)]
    part = ((part.astype(F32) + others[0]) + (others[1] + others[2])).astype(BF)
    part = lax.all_to_all(jnp.broadcast_to(part[None], (16, PART, C)), GY, 0, 0, tiled=True)
    part = part.reshape(HALF, C)
    grads = [((27 * CIN, C), F32), ((27 * C, C), F32), ((8 * C, C), F32)]
    scratch = [((HALF, C), F32), pltpu.SemaphoreType.DMA((5,))]
    hbm = pl.BlockSpec(memory_space=pl.ANY)
    other = swap_cores(part)
    grads_own = call(unfold_own, grads, (part,), [VM], scratch, out_specs=[hbm] * 3)
    grad_first, grad_second, grad_down = call(
        unfold_other, grads, (other, *grads_own), [VM] + [hbm] * 3, scratch, out_specs=[hbm] * 3,
        aliases={1: 0, 2: 1, 3: 2},
    )
    return (
        moved,
        grad_first.reshape(27, CIN, C),
        grad_second.reshape(27, C, C),
        grad_down.reshape(8, C, C),
    )


def solution(mesh):
    shape = dict(mesh.shape)
    fine = Mesh(
        mesh.devices.reshape(shape["gx"] // 2, 2, 4, shape["gy"] // 4), ("y", "c", "z", "x")
    )
    whole, tiles = P(GX, GY, None), P(GX, GY, None, None)
    return jax.shard_map(
        per_device,
        mesh=fine,
        in_specs=(whole, whole, P(), P(), P(), tiles, tiles),
        out_specs=(tiles, P(), P(), P()),
        check_vma=False,
    )
```
